32 devices in a mesh: expert: 8 (over z, y), wshard: 4 (over x, core).
Axes of the slice: x: 2, y: 2, z: 4, core: 2. Of those that a mesh axis runs over, the one named last changes fastest.
Arguments:
- tokens: bfloat16 [4096, 768], P(('expert', 'wshard')), may hold values from -6 to 6
- segments: int32 [8, 512], P('expert'), may hold values from 0 to 2, as said below
- routes: int32 [4096, 2], P(('expert', 'wshard')), may hold values from 0 to 7, all different within a row; in each aligned block of 128 rows (0 to 127, 128 to 255, ...) at most 96 rows name the same one
- blocks: int32 [8], P('expert'), may hold values from 1 to 2, as said below
- attention_gain: bfloat16 [768], P('wshard'), may hold values from 0.099609375 to 1.8984375
- query_weight: bfloat16 [768, 768], P('wshard'), may hold values from -0.21875 to 0.21875
- key_weight: bfloat16 [768, 768], P('wshard'), may hold values from -0.21875 to 0.21875
- value_weight: bfloat16 [768, 768], P('wshard'), may hold values from -0.21875 to 0.21875
- output_weight: bfloat16 [768, 768], P('wshard'), may hold values from -0.875 to 0.875
- position_bias: bfloat16 [32, 12], P('wshard'), may hold values from -4 to 4
- feed_gain: bfloat16 [768], P('wshard'), may hold values from 0.099609375 to 1.8984375
- router_weight: bfloat16 [768, 8], P('wshard'), may hold values from -0.15625 to 0.15625
- expert_in: bfloat16 [8, 3072, 768], P('expert', 'wshard'), may hold values from -0.21875 to 0.21875
- expert_out: bfloat16 [8, 3072, 768], P('expert', 'wshard'), may hold values from -0.15625 to 0.15625
- cotangent: bfloat16 [4096, 768], P(('expert', 'wshard')), may hold values from -6 to 6
Outputs:
- layer_out: bfloat16 [4096, 768], P(('expert', 'wshard'))
- tokens_grad: float32 [4096, 768], P(('expert', 'wshard'))
- attention_gain_grad: float32 [768], P('wshard')
- query_projection_gradient: float32 [768, 768], P('wshard')
- key_weight_grad: float32 [768, 768], P('wshard')
- value_weight_grad: float32 [768, 768], P('wshard')
- output_weight_grad: float32 [768, 768], P('wshard')
- position_bias_grad: float32 [32, 12], P('wshard')
- feed_gain_grad: float32 [768], P('wshard')
- router_weight_grad: float32 [768, 8], P('wshard')
- expert_in_grad: float32 [8, 3072, 768], P('expert', 'wshard')
- expert_out_grad: float32 [8, 3072, 768], P('expert', 'wshard')
The draws below stay inside these ranges and needn't reach their ends.
Inputs may be any that keep to these rules, and one draw needn't show every extreme that they name: `segments`: along each sequence the numbers 0, 1, 2 never fall; document 1 begins within the first 128 positions and ends within the last 128. `routes`: the two experts of a row differ; in each aligned block of 128 rows (the rows of one device) no expert is named by more than 96 rows, a bound that some block reaches. `blocks`: blocks of 128 rows that an expert takes from each quarter of the tokens; some expert has 2.
All inputs are finite; a program needn't handle non-finite values.
Results may differ from the reference program's by a relative error of at most 0.013.
Values may be sent and summed in bfloat16 or wider, within the bound.
No kernel may reach another device: no remote copies, remote signals or barrier semaphores. Data moves between devices by JAX's collectives and lax.ppermute only.
A program may use at most 128 MiB of HBM per device.

```python
import math
import jax
import jax.numpy as jnp
import numpy as np
from jax import lax

D = 768
HEADS = 12
HEAD_DIM = 64
FF = 3072
BUCKETS = 32
BLOCK = 128
TOK_DEV = 128
EXPERTS = 8
SEQ = 512
SEQS = 8
TOKENS = 4096
MOST_BLOCKS = 2
CAP = 96
N_WSHARD = 4


def draw_segments(key, part):
    key = jax.random.fold_in(key, 11)
    first_key, last_key = jax.random.split(key)
    starts = jax.random.randint(first_key, (SEQS, 1), 1, TOK_DEV)
    finish = jax.random.randint(last_key, (SEQS, 1), SEQ - TOK_DEV, SEQ)
    positions = jnp.arange(SEQ, dtype=jnp.int32)[None, :]
    return ((positions >= starts).astype(jnp.int32) + (positions >= finish).astype(jnp.int32)).astype(jnp.int32)


def draw_blocks(key, part):
    key = jax.random.fold_in(key, 23)
    count_key, place_key = jax.random.split(key)
    counts = jax.random.randint(count_key, (EXPERTS,), 1, MOST_BLOCKS + 1)
    chosen = jax.random.randint(place_key, (), 0, EXPERTS)
    return jnp.where(jnp.arange(EXPERTS) == chosen, MOST_BLOCKS, counts).astype(jnp.int32)


def block_scale(stream_key, extent, cuts, low, top_value):
    loudness, own = 1.0, jax.random.fold_in(stream_key, 6)
    for position, blocks in cuts:
        steps = jnp.exp(jax.random.uniform(jax.random.fold_in(own, position), (blocks,), jnp.float32, low / len(cuts), top_value / len(cuts)))
        loudness = loudness * jnp.repeat(steps, extent[position] // blocks).reshape([-1 if axis == position else 1 for axis in range(len(extent))])
    return loudness


def routed_block(key, own, number, rows, count, top, limit, slope):
    order = jax.random.permutation(key, count)
    packed, usual = shares(count, rows * top, limit, slope, True), shares(count, rows * top, limit, slope, False)
    places = jnp.arange(count)

    def named(sizes, rotation):
        used = int((sizes > 0).sum())
        fixed = max(1, used // 4)
        shifted = fixed + (places - fixed + rotation * (used - fixed)) % max(1, count - fixed)
        return jnp.zeros((count,), jnp.int32).at[order[jnp.where(places < fixed, places, shifted)]].set(jnp.asarray(sizes, jnp.int32))

    sizes = jnp.where(number % 4 == 0, named(packed, number // 4), named(usual, number - number // 4 - 1))
    mixed = jax.random.permutation(jax.random.fold_in(own, 3), count)
    donor, taker = mixed[0:count // 2 * 2:2], mixed[1:count // 2 * 2:2]
    margin = jnp.minimum(sizes[donor] - 1, limit - sizes[taker]) // 2
    margin = jnp.where((donor == order[0]) | (taker == order[0]) | (sizes[taker] == 0), 0, jnp.maximum(margin, 0))
    shifted = jax.random.randint(jax.random.fold_in(own, 4), (count // 2,), 0, 1 << 20) % (margin + 1)
    sizes = sizes.at[donor].add(-shifted).at[taker].add(shifted)
    members = jnp.searchsorted(jnp.cumsum(sizes), jnp.arange(rows * top), side="right").astype(jnp.int32)
    grid = members.reshape(top, rows).T
    grid = grid[jax.random.permutation(jax.random.fold_in(own, 1), rows)]
    rotation = jax.random.randint(jax.random.fold_in(own, 2), (rows, 1), 0, top)
    return jnp.take_along_axis(grid, (jnp.arange(top)[None, :] + rotation) % top, axis=1)


def shares(count, total, limit, slope, full):
    weights = [(1 << 20) // math.isqrt(rank ** slope) + 1 for rank in range(1, count + 1)]
    largest = limit if full else min(limit, max(-(-total // count), total * weights[0] // sum(weights)))
    least = 1 if total - largest >= count - 1 else 0
    given, spare = [largest] + [least] * (count - 1), total - largest - least * (count - 1)
    while spare > 0:
        movable = [i for i in range(1, count) if given[i] < largest] or [i for i in range(1, count) if given[i] < limit]
        mass, left = sum([weights[i] for i in movable]), spare
        for i in movable:
            extra = min(limit - given[i], max(1, left * weights[i] // mass), spare)
            given[i] = given[i] + extra
            spare = spare - extra
    return np.array(given)


def gaussian(own_key, dims, scale, reach, cuts=(), held_as=jnp.bfloat16):
    drawn = jax.random.normal(own_key, dims, jnp.float32) * scale
    if len(cuts) > 0:
        drawn = block_scale(own_key, dims, cuts, -0.22, 0.18) * drawn
    return jnp.clip(drawn, min=-reach, max=reach).astype(held_as)


def setup_inputs(seed: int = 0) -> dict:
    key_of = jax.random.split(jax.random.key(seed), 16)
    tokens = gaussian(key_of[0], (TOKENS, D), 1.0, 6.0, ((0, 32),))
    segments = draw_segments(jax.random.fold_in(key_of[15], 71), 0)
    routes_keys = jax.random.split(jax.random.fold_in(key_of[2], 1), TOKENS // TOK_DEV)
    routes_turns = jax.random.permutation(jax.random.fold_in(key_of[2], 3), TOKENS // TOK_DEV)
    routes = jax.vmap(lambda own, number: routed_block(jax.random.fold_in(key_of[2], 2), own, number, TOK_DEV, EXPERTS, 2, CAP, 2))(routes_keys, routes_turns).reshape((TOKENS, 2))
    blocks = draw_blocks(jax.random.fold_in(key_of[15], 71), 0)
    attention_gain = jnp.clip(1.0 + 0.18 * jax.random.normal(key_of[4], (D,), jnp.float32), 0.099609375, 1.8984375).astype(jnp.bfloat16)
    query_weight = gaussian(key_of[5], (D, D), D ** -0.5, 0.21875, ((0, 4),))
    key_weight = gaussian(key_of[6], (D, D), D ** -0.5, 0.21875, ((0, 4),))
    value_weight = gaussian(key_of[7], (D, D), D ** -0.5, 0.21875, ((0, 4),))
    output_weight = gaussian(key_of[8], (D, D), (D // 16) ** -0.5, 0.875, ((0, 4),))
    position_bias = gaussian(key_of[9], (BUCKETS, HEADS), 1.0, 4.0, ((0, 4),))
    feed_gain = jnp.clip(1.0 + 0.18 * jax.random.normal(key_of[10], (D,), jnp.float32), 0.099609375, 1.8984375).astype(jnp.bfloat16)
    router_weight = gaussian(key_of[11], (D, EXPERTS), (2 * D) ** -0.5, 0.15625, ((0, 4),))
    expert_in = gaussian(key_of[12], (EXPERTS, FF, D), D ** -0.5, 0.21875, ((0, 8), (1, 4)))
    expert_out = gaussian(key_of[13], (EXPERTS, FF, D), (FF // 2) ** -0.5, 0.15625, ((0, 8), (1, 4)))
    cotangent = gaussian(key_of[14], (TOKENS, D), 1.0, 6.0, ((0, 32),))
    return dict(tokens=tokens, segments=segments, routes=routes, blocks=blocks, attention_gain=attention_gain, query_weight=query_weight, key_weight=key_weight, value_weight=value_weight, output_weight=output_weight, position_bias=position_bias, feed_gain=feed_gain, router_weight=router_weight, expert_in=expert_in, expert_out=expert_out, cotangent=cotangent)


@jax.custom_vjp
def low(v):
    return lax.optimization_barrier(v.astype(jnp.bfloat16)).astype(jnp.float32)

@jax.custom_vjp
def low_back(v):
    return v

def low_keep(v):
    return (low(v), None)

def low_pass(kept, grad):
    return (grad,)

def back_keep(v):
    return (v, None)

def back_low(kept, grad):
    return (low(grad),)
low.defvjp(low_keep, low_pass)
low_back.defvjp(back_keep, back_low)
epsilon = 1e-06
thresholds = tuple((math.ceil(16 * 2 ** (3 * order / 16)) for order in range(1, 16)))

def rounded(value):
    return low_back(low(value))

def bucket_of(distance):
    passed = jnp.zeros_like(distance)
    for edge in thresholds:
        passed = passed + (distance >= edge).astype(jnp.int32)
    return jnp.where(distance < 16, distance, 16 + passed)

def norm_rows(rows, gain):
    return rows * lax.rsqrt(lax.optimization_barrier(jnp.mean(rows * rows, axis=-1, keepdims=True)) + epsilon) * gain

def reference(tokens, segments, routes, blocks, attention_gain, query_weight, key_weight, value_weight, output_weight, position_bias, feed_gain, router_weight, expert_in, expert_out, cotangent):
    highest = lax.Precision.HIGHEST
    quarters = N_WSHARD
    packed_rows = MOST_BLOCKS * BLOCK
    groups = EXPERTS * quarters
    pairs = TOKENS * 2
    expert_ids = routes.reshape(-1).astype(jnp.int32)
    token_ids = jnp.arange(pairs, dtype=jnp.int32) // 2
    group_ids = expert_ids * quarters + token_ids // TOK_DEV % quarters
    hits = (group_ids[:, None] == jnp.arange(groups, dtype=jnp.int32)[None, :]).astype(jnp.int32)
    ranks = lax.optimization_barrier(jnp.sum((jnp.cumsum(hits, axis=0) - hits) * hits, axis=1)).astype(jnp.int32)
    group_limit = (blocks.astype(jnp.int32)[jnp.arange(groups, dtype=jnp.int32) // quarters] * BLOCK).astype(jnp.int32)
    kept = ranks < group_limit[group_ids]
    targets = jnp.where(kept, group_ids * packed_rows + ranks, groups * packed_rows).astype(jnp.int32)
    source_of = jnp.zeros((groups * packed_rows,), jnp.int32).at[targets].set(token_ids, mode='drop')
    counts = lax.optimization_barrier(jnp.sum(hits, axis=0)).astype(jnp.int32)
    filled = (jnp.arange(packed_rows, dtype=jnp.int32)[None, :] < jnp.minimum(counts, group_limit)[:, None]).reshape(-1)
    reads = jnp.minimum(targets, groups * packed_rows - 1).astype(jnp.int32)
    positions = jnp.arange(SEQ, dtype=jnp.int32)
    distance = positions[:, None] - positions[None, :]
    buckets = bucket_of(jnp.maximum(distance, 0))

    def forward(inputs, gain_one, query_matrix, key_matrix, value_matrix, output_matrix, table, second_norm_gain, router_matrix, expert_first, expert_second):
        first = low(norm_rows(inputs, gain_one))
        queries = rounded(jnp.dot(first, query_matrix, precision=highest))
        keys = rounded(jnp.dot(first, key_matrix, precision=highest))
        values = rounded(jnp.dot(first, value_matrix, precision=highest))
        additive_bias = jnp.moveaxis(jnp.take(table, buckets, axis=0), -1, 0)

        def attend(pieces):
            query_rows, key_rows, value_rows, marks = pieces
            allowed = (distance >= 0) & (marks[:, None] == marks[None, :])
            query_heads = query_rows.reshape(SEQ, HEADS, HEAD_DIM)
            key_heads = key_rows.reshape(SEQ, HEADS, HEAD_DIM)
            value_heads = value_rows.reshape(SEQ, HEADS, HEAD_DIM)
            scores = jnp.einsum('qhd,khd->hqk', query_heads, key_heads, precision=highest) * HEAD_DIM ** (-0.5) + additive_bias
            scores = low_back(scores)
            probs = low(jax.nn.softmax(jnp.where(allowed[None], scores, -1e+30), axis=-1))
            return jnp.einsum('hqk,khd->qhd', probs, value_heads, precision=highest).reshape(SEQ, D)
        attended = lax.map(jax.checkpoint(attend), (queries.reshape(SEQS, SEQ, D), keys.reshape(SEQS, SEQ, D), values.reshape(SEQS, SEQ, D), segments))
        attended = rounded(attended.reshape(TOKENS, D))
        branch = low_back(jnp.dot(attended, output_matrix, precision=highest))
        resid = inputs + branch
        second = low(norm_rows(resid, second_norm_gain))
        logits = low_back(jnp.dot(second, router_matrix, precision=highest))
        gates = jax.nn.softmax(jnp.take_along_axis(logits, routes, axis=1), axis=-1)
        rows_in = jnp.where(filled[:, None], second[source_of], 0.0)
        rows_in = low_back(rows_in).reshape(EXPERTS, quarters * packed_rows, D)

        def run_expert(pieces):
            rows, first_matrix, second_matrix = pieces
            pre = low_back(jnp.dot(rows, first_matrix.T, precision=highest))
            act = low(jax.nn.gelu(pre))
            return rounded(jnp.dot(act, second_matrix, precision=highest))
        outputs = lax.map(jax.checkpoint(run_expert), (rows_in, expert_first, expert_second))
        pair_rows = jnp.where(kept[:, None], outputs.reshape(groups * packed_rows, D)[reads], 0.0)
        mixture = lax.optimization_barrier(jnp.sum(gates[:, :, None] * pair_rows.reshape(TOKENS, 2, D), axis=1))
        return resid + mixture
    mixed, pullback = jax.vjp(forward, tokens.astype(jnp.float32), attention_gain.astype(jnp.float32), query_weight.astype(jnp.float32), key_weight.astype(jnp.float32), value_weight.astype(jnp.float32), output_weight.astype(jnp.float32), position_bias.astype(jnp.float32), feed_gain.astype(jnp.float32), router_weight.astype(jnp.float32), expert_in.astype(jnp.float32), expert_out.astype(jnp.float32))
    grads = pullback(cotangent.astype(jnp.float32))
    return (mixed.astype(jnp.bfloat16), grads[0], grads[1], grads[2], grads[3], grads[4], grads[5], grads[6], grads[7], grads[8], grads[9], grads[10])
```

```python
import math

import jax
import jax.numpy as jnp
from jax import lax
from jax.experimental import pallas as pl
from jax.experimental.pallas import tpu as pltpu
from jax.sharding import PartitionSpec as P

HEADS = 12
HEAD_DIM = 64
BUCKETS = 32
BLOCK = 128
MOST_BLOCKS = 2
SHARDS = 4
W = "wshard"
E = "expert"

epsilon = 1e-06
thresholds = tuple((math.ceil(16 * 2 ** (3 * order / 16)) for order in range(1, 16)))
low = jnp.bfloat16
wide = jnp.float32


def bucket_of(distance):
    passed = jnp.zeros_like(distance)
    for edge in thresholds:
        passed = passed + (distance >= edge).astype(jnp.int32)
    return jnp.where(distance < 16, distance, 16 + passed)


def along_last(left, right):
    return lax.dot_general(left, right, (((1,), (1,)), ((), ())), preferred_element_type=wide)


def along_first(left, right):
    return lax.dot_general(left, right, (((0,), (0,)), ((), ())), preferred_element_type=wide)


def matmul(left, right):
    return jnp.dot(left, right, preferred_element_type=wide)


def swap(value, axis, step):
    count = lax.axis_size(axis)
    return lax.ppermute(value, axis, [(i, i ^ step) for i in range(count)])


def gather_w(value):
    far = swap(value, W, 2)
    near = swap(value, W, 1)
    return [value, near, far, swap(far, W, 1)]


def sum_w(parts):
    a3 = swap(parts[3], W, 1)
    a1 = swap(parts[1], W, 1)
    across = (parts[2].astype(wide) + a3.astype(wide)).astype(low)
    far = swap(across, W, 2)
    return parts[0].astype(wide) + a1.astype(wide) + far.astype(wide)


def exchange_w(parts):
    return [parts[0]] + [swap(parts[s], W, s) for s in (1, 2, 3)]


def place(parts, me):
    out = jnp.zeros((len(parts),) + parts[0].shape, parts[0].dtype)
    for s, part in enumerate(parts):
        out = lax.dynamic_update_index_in_dim(out, part, me ^ s, 0)
    return out


def gather_e(value):
    count = lax.axis_size(E)
    if count > 8:
        whole = lax.all_gather(value, E, axis=0)
        me = lax.axis_index(E)
        order = me ^ jnp.arange(count, dtype=jnp.int32)
        whole = whole[order]
        return [whole[s] for s in range(count)]
    out = {0: value}
    for s in (4, 6, 2):
        out[s] = swap(value, E, s)
    for s in (0, 4, 6, 2):
        out[s ^ 1] = swap(out[s], E, 1)
    return [out[s] for s in range(8)]


def sum_e(parts):
    count = lax.axis_size(E)
    if count > 8:
        me = lax.axis_index(E)
        whole = jnp.stack(parts)[me ^ jnp.arange(count, dtype=jnp.int32)]
        return lax.psum_scatter(whole, E, scatter_dimension=0).astype(wide)
    got = {s: swap(parts[s ^ 1], E, 1) for s in (4, 6, 2, 0)}
    total = parts[0].astype(wide) + got[0].astype(wide)
    for s in (4, 6, 2):
        part = (parts[s].astype(wide) + got[s].astype(wide)).astype(low)
        total = total + swap(part, E, s).astype(wide)
    return total


def bias_kernel(vector_ref, row_ref, column_ref, bias_ref):
    length = row_ref.shape[1]
    i = lax.broadcasted_iota(jnp.int32, (length, length), 0)
    j = lax.broadcasted_iota(jnp.int32, (length, length), 1)
    allowed = (j <= i) & (row_ref[...] == column_ref[...])
    for h in range(bias_ref.shape[0]):
        flat = jnp.broadcast_to(vector_ref[h : h + 1, :], (length, length))
        rolled = pltpu.roll(flat, 0, 1, stride=1, stride_axis=0)
        bias_ref[h] = jnp.where(allowed, rolled, -1e30).astype(low)


def attend_kernel(
    tokens_ref, gain_ref, weight_ref, bias_ref, out_ref, first_ref, qkv_ref, probs_ref, att_ref, br_ref
):
    rows = tokens_ref[...].astype(wide)
    scale = lax.rsqrt(jnp.mean(rows * rows, axis=-1, keepdims=True) + epsilon)
    first = (rows * scale * gain_ref[...]).astype(low)
    first_ref[...] = first
    qkv = matmul(first, weight_ref[...]).astype(low)
    qkv_ref[...] = qkv
    length = rows.shape[0]
    heads = probs_ref.shape[0]
    span = heads * HEAD_DIM
    chunk = length // SHARDS
    columns = []
    for h in range(heads):
        q = qkv[:, h * HEAD_DIM : (h + 1) * HEAD_DIM] * (HEAD_DIM**-0.5)
        k = qkv[:, span + h * HEAD_DIM : span + (h + 1) * HEAD_DIM]
        v = qkv[:, 2 * span + h * HEAD_DIM : 2 * span + (h + 1) * HEAD_DIM]
        pieces = []
        for b in range(SHARDS):
            end = (b + 1) * chunk
            here = slice(b * chunk, end)
            scores = along_last(q[here], k[:end]) + bias_ref[h, here, :end].astype(wide)
            largest = jnp.max(scores, axis=-1, keepdims=True)
            weights = jnp.exp(scores - largest)
            total = jnp.sum(weights, axis=-1, keepdims=True)
            probs = (weights / total).astype(low)
            probs_ref[h, here, :end] = probs
            if end < length:
                probs_ref[h, here, end:] = jnp.zeros((chunk, length - end), low)
            pieces.append(matmul(probs, v[:end]))
        columns.append(jnp.concatenate(pieces, axis=0))
    attended = jnp.concatenate(columns, axis=1).astype(low)
    att_ref[...] = attended
    br_ref[...] = matmul(attended, out_ref[...]).astype(low)


def attend_back_kernel(
    up_ref, out_ref, qkv_ref, probs_ref, weight_ref, tokens_ref, dqkv_ref, back_ref, gain_ref, diag_ref
):
    length = up_ref.shape[0]
    heads = probs_ref.shape[0]
    span = heads * HEAD_DIM
    chunk = length // SHARDS
    scale = HEAD_DIM**-0.5
    back = along_last(up_ref[...], out_ref[...]).astype(low)
    qkv = qkv_ref[...]
    dq, dk, dv = [], [], []
    i = lax.broadcasted_iota(jnp.int32, (chunk, chunk), 0)
    j = lax.broadcasted_iota(jnp.int32, (chunk, chunk), 1)
    reverse = (i + j == chunk - 1).astype(low)
    diag_ref[...] = jnp.zeros_like(diag_ref)
    for h in range(heads):
        q = qkv[:, h * HEAD_DIM : (h + 1) * HEAD_DIM]
        k = qkv[:, span + h * HEAD_DIM : span + (h + 1) * HEAD_DIM]
        v = qkv[:, 2 * span + h * HEAD_DIM : 2 * span + (h + 1) * HEAD_DIM]
        d = back[:, h * HEAD_DIM : (h + 1) * HEAD_DIM]
        probs_low = probs_ref[h]
        probs = probs_low.astype(wide)
        back_probs = along_last(d, v)
        inner = jnp.sum(back_probs * probs, axis=-1, keepdims=True)
        scores = probs * (back_probs - inner)
        scores_low = scores.astype(low)
        diagonal = jnp.zeros((1, length), wide)
        for b in range(SHARDS):
            turned = matmul(reverse, scores_low[b * chunk : (b + 1) * chunk])
            start = (1 - (b + 1) * chunk) % length
            turned = pltpu.roll(turned, start, 1, stride=1, stride_axis=0)
            diagonal = diagonal + jnp.sum(turned, axis=0, keepdims=True)
        diag_ref[h : h + 1, :] = diagonal
        dq.append((matmul(scores_low, k) * scale).astype(low))
        dk.append((along_first(scores_low, q) * scale).astype(low))
        dv.append(along_first(probs_low, d).astype(low))
    dqkv = jnp.concatenate(dq + dk + dv, axis=1)
    dqkv_ref[...] = dqkv
    back_first = along_last(dqkv, weight_ref[...])
    back_ref[...] = back_first.astype(low)
    rows = tokens_ref[...].astype(wide)
    rows = rows * lax.rsqrt(jnp.mean(rows * rows, axis=-1, keepdims=True) + epsilon)
    gain_ref[...] = jnp.sum(back_first * rows, axis=0, keepdims=True)


def call(kernel, outs, cost, *args):
    return pl.pallas_call(
        kernel,
        out_shape=tuple(jax.ShapeDtypeStruct(s, d) for s, d in outs),
        compiler_params=pltpu.CompilerParams(vmem_limit_bytes=40 * 1024 * 1024),
        cost_estimate=pl.CostEstimate(flops=cost[0], bytes_accessed=cost[1], transcendentals=cost[2]),
    )(*args)


def norm_back(rows, gain, upstream):
    r = lax.rsqrt(jnp.mean(rows * rows, axis=-1, keepdims=True) + epsilon)
    m = upstream * gain
    gain_grad = jnp.sum(upstream * rows * r, axis=0)
    return r * m - (r * r * r) * rows * jnp.mean(m * rows, axis=-1, keepdims=True), gain_grad


def local(
    tokens,
    segments,
    routes,
    blocks,
    attention_gain,
    query_weight,
    key_weight,
    value_weight,
    output_weight,
    position_bias,
    feed_gain,
    router_weight,
    expert_in,
    expert_out,
    cotangent,
):
    rows, width = tokens.shape
    length = rows * SHARDS
    experts = lax.axis_size(E)
    me_w = lax.axis_index(W)
    me_e = lax.axis_index(E)
    shard = query_weight.shape[0]
    own_heads = HEADS // SHARDS
    table_rows = position_bias.shape[0]

    tokens_all = place(gather_w(tokens), me_w).reshape(length, width)
    stacked = jnp.stack([query_weight, key_weight, value_weight], axis=1)
    stacked = stacked.reshape(shard, 3, SHARDS, shard).transpose(2, 0, 1, 3).reshape(SHARDS, shard, 3 * shard)
    weight = place(
        exchange_w([lax.dynamic_index_in_dim(stacked, me_w ^ s, 0, False) for s in range(SHARDS)]), me_w
    ).reshape(width, 3 * shard)
    small = jnp.concatenate(
        [attention_gain, feed_gain, router_weight.reshape(-1), position_bias.reshape(-1)]
    )
    used = small.shape[0]
    filled_to = -(-used // 2048) * 2048
    small = jnp.pad(small, (0, filled_to - used)).reshape(-1, 128)
    small = place([small] + [swap(small, W, s) for s in (1, 2, 3)], me_w).reshape(SHARDS, filled_to)
    gain_one = small[:, :shard].reshape(1, width).astype(wide)
    gain_two = small[:, shard : 2 * shard].reshape(1, width).astype(wide)
    router = small[:, 2 * shard : 2 * shard + shard * experts].reshape(width, experts)
    table = small[:, 2 * shard + shard * experts : used].reshape(BUCKETS, HEADS)

    cap = MOST_BLOCKS * BLOCK
    ids = jnp.pad(routes.reshape(-1).astype(low), (0, 16 * width - 2 * rows)).reshape(16, width)
    sent = jnp.stack(gather_e(jnp.concatenate([cotangent, ids], axis=0)))
    upstream_all = sent[:, :rows].reshape(experts * rows, width)
    pairs = sent[:, rows, : 2 * rows].reshape(experts, rows, 2).astype(jnp.int32)
    hit = jnp.any(pairs == me_e, axis=-1)
    other = jnp.where(hit, jnp.sum(pairs, axis=-1) - me_e, 0)
    before = (
        jnp.arange(rows, dtype=jnp.int32)[:, None] < jnp.arange(rows, dtype=jnp.int32)[None, :]
    ).astype(low)
    within = matmul(hit.astype(low), before).astype(jnp.int32)
    counts = jnp.sum(hit.astype(jnp.int32), axis=1)
    index = me_e ^ jnp.arange(experts, dtype=jnp.int32)
    base = jnp.sum(jnp.where(index[None, :] < index[:, None], counts[None, :], 0), axis=1)
    rank = within + base[:, None]
    kept = hit & (rank < blocks[0] * BLOCK)
    slot = jnp.where(kept, rank, -1).reshape(1, experts * rows)
    dispatch = (jnp.arange(cap, dtype=jnp.int32)[:, None] == slot).astype(low)
    upstream_rows = matmul(dispatch, upstream_all).astype(low)
    other_rows = jnp.sum(jnp.where(dispatch > 0, other.reshape(1, -1), 0), axis=1)
    other_rows = jnp.pad(other_rows.astype(low), (0, 16 * width - cap)).reshape(16, width)
    sent = jnp.stack(gather_w(jnp.concatenate([upstream_rows, other_rows], axis=0)))
    upstream_rows = sent[:, :cap].reshape(SHARDS * cap, width)
    other_rows = sent[:, cap, :cap].reshape(SHARDS * cap, 1).astype(jnp.int32)
    lanes = jnp.arange(experts, dtype=jnp.int32)[None, :]
    choice = (lanes == me_e).astype(wide) - (lanes == other_rows).astype(wide)
    first_local = expert_in[0]
    second_local = expert_out[0]
    back_act = along_last(upstream_rows, second_local)

    shift = jnp.arange(length, dtype=jnp.int32)
    bucket = bucket_of((length - shift) % length)
    bucket_hits = (bucket[:, None] == jnp.arange(BUCKETS, dtype=jnp.int32)[None, :]).astype(wide)
    own_table = lax.dynamic_slice_in_dim(table, me_w * own_heads, own_heads, 1).astype(wide)
    vector = jnp.pad(
        lax.dot_general(
            own_table, bucket_hits, (((0,), (1,)), ((), ())), precision=lax.Precision.HIGHEST
        ),
        ((0, 8 - own_heads), (0, 0)),
    )
    square = (own_heads, length, length)
    (bias,) = call(
        bias_kernel,
        [(square, low)],
        (0, 2 * own_heads * length * length, 0),
        vector,
        segments,
        segments.reshape(length, 1),
    )
    first, qkv, probs, attended, branch = call(
        attend_kernel,
        [
            ((length, width), low),
            ((length, 3 * shard), low),
            (square, low),
            ((length, shard), low),
            ((length, width), low),
        ],
        (2 * length * width * 4 * shard, 8 * length * length * own_heads, own_heads * length * length),
        tokens_all,
        gain_one,
        weight,
        bias,
        output_weight,
    )
    branch = branch.reshape(SHARDS, rows, width)
    branch = sum_w([lax.dynamic_index_in_dim(branch, me_w ^ s, 0, False) for s in range(SHARDS)])
    inputs = tokens.astype(wide)
    resid = inputs + branch
    second = (
        resid * lax.rsqrt(jnp.mean(resid * resid, axis=-1, keepdims=True) + epsilon) * gain_two
    ).astype(low)

    second_all = jnp.concatenate(gather_e(second), axis=0)
    packed = matmul(dispatch, second_all).astype(low)
    rows_all = jnp.concatenate(gather_w(packed), axis=0)
    logits = matmul(rows_all, router)
    gate = jax.nn.sigmoid(jnp.sum(logits * choice, axis=1, keepdims=True))
    pre = along_last(rows_all, first_local)
    gelu_value, gelu_back = jax.vjp(jax.nn.gelu, pre)
    act = gelu_value.astype(low)
    back_gate = jnp.sum(act.astype(wide) * back_act, axis=1, keepdims=True)
    back_pre = gelu_back(back_act * gate)[0].astype(low)
    back_logits = (gate * (1.0 - gate) * back_gate * choice).astype(low)
    back_rows = (matmul(back_pre, first_local) + along_last(back_logits, router)).astype(low)
    back_rows = sum_w([back_rows[s * cap : (s + 1) * cap] for s in range(SHARDS)]).astype(low)
    back_rows = along_first(dispatch, back_rows).astype(low)
    back_second = sum_e([back_rows[s * rows : (s + 1) * rows] for s in range(experts)])

    pair_out = (matmul(act, second_local) * gate).astype(low)
    pair_out = sum_w([pair_out[s * cap : (s + 1) * cap] for s in range(SHARDS)]).astype(low)
    pair_out = along_first(dispatch, pair_out).astype(low)
    mixed = sum_e([pair_out[s * rows : (s + 1) * rows] for s in range(experts)])
    layer_out = (resid + mixed).astype(low)

    back_pairs = (upstream_rows.astype(wide) * gate).astype(low)
    first_grad = along_first(back_pre, rows_all)
    second_grad = along_first(act, back_pairs)
    router_grad = along_first(rows_all, back_logits)

    back_norm, gain_two_grad = norm_back(resid, gain_two, back_second)
    back_resid = cotangent.astype(wide) + back_norm
    back_branch = place(gather_w(back_resid.astype(low)), me_w).reshape(length, width)
    dqkv, back_first, gain_one_grad, diagonals = call(
        attend_back_kernel,
        [
            ((length, 3 * shard), low),
            ((length, width), low),
            ((1, width), wide),
            ((8, length), wide),
        ],
        (2 * length * width * 4 * shard, 8 * length * length * own_heads, 0),
        back_branch,
        output_weight,
        qkv,
        probs,
        weight,
        tokens_all,
    )
    back_first = back_first.reshape(SHARDS, rows, width)
    back_first = sum_w([lax.dynamic_index_in_dim(back_first, me_w ^ s, 0, False) for s in range(SHARDS)])
    back_inputs, _ = norm_back(inputs, gain_one, back_first)
    tokens_grad = back_resid + back_inputs

    output_grad = along_first(attended, back_branch).astype(low)
    piece = shard // experts
    output_parts = output_grad.reshape(experts, piece, width)
    output_sum = sum_e([lax.dynamic_index_in_dim(output_parts, me_e ^ s, 0, False) for s in range(experts)])
    output_sum = place(gather_e(output_sum.astype(low)), me_e).reshape(shard, width).astype(wide)

    qkv_grad = along_first(first, dqkv).astype(low)
    table_grad = matmul(diagonals[:own_heads], bucket_hits).T
    table_grad = jnp.pad(
        table_grad.reshape(SHARDS, table_rows, own_heads), ((0, 0), (0, shard - table_rows), (0, 0))
    ).reshape(width, own_heads)
    extra = jnp.concatenate(
        [gain_one_grad.reshape(width, 1), gain_two_grad.reshape(width, 1), router_grad, table_grad], axis=1
    ).astype(low)
    extra_used = extra.shape[1]
    total_columns = -(-(3 * shard + extra_used) // 128) * 128
    extra = jnp.pad(extra, ((0, 0), (0, total_columns - 3 * shard - extra_used)))
    grads = jnp.concatenate([qkv_grad, extra], axis=1).reshape(SHARDS, experts, piece, total_columns)
    grads = sum_e([lax.dynamic_index_in_dim(grads, me_e ^ s, 1, False) for s in range(experts)]).astype(low)
    grads = place(
        exchange_w([lax.dynamic_index_in_dim(grads, me_w ^ s, 0, False) for s in range(SHARDS)]), me_w
    )
    main = grads[:, :, : 3 * shard].reshape(SHARDS, piece, 3, shard).transpose(1, 2, 0, 3)
    main = main.reshape(piece, 3 * width)
    extra = grads[:, :, 3 * shard : 3 * shard + extra_used].astype(wide)
    summed = jnp.sum(extra[:, :, : 2 + experts], axis=0)
    heads = extra[:, :, 2 + experts :].transpose(1, 0, 2).reshape(piece, HEADS)
    extra = jnp.concatenate([summed, heads], axis=1).astype(low)
    extra_width = -(-extra.shape[1] // 128) * 128
    extra = jnp.pad(extra, ((0, 0), (0, extra_width - extra.shape[1])))
    whole = place(gather_e(jnp.concatenate([main, extra], axis=1)), me_e)
    whole = whole.reshape(shard, 3 * width + extra_width).astype(wide)
    extra = whole[:, 3 * width :]
    return (
        layer_out,
        tokens_grad,
        extra[:, 0],
        whole[:, :width],
        whole[:, width : 2 * width],
        whole[:, 2 * width : 3 * width],
        output_sum,
        extra[:table_rows, 2 + experts : 2 + experts + HEADS],
        extra[:, 1],
        extra[:, 2 : 2 + experts],
        first_grad[None],
        second_grad[None],
    )


def solution(mesh):
    in_specs = (
        P(("expert", "wshard"), None),
        P("expert", None),
        P(("expert", "wshard"), None),
        P("expert"),
        P("wshard"),
        P("wshard", None),
        P("wshard", None),
        P("wshard", None),
        P("wshard", None),
        P("wshard", None),
        P("wshard"),
        P("wshard", None),
        P("expert", "wshard", None),
        P("expert", "wshard", None),
        P(("expert", "wshard"), None),
    )
    out_specs = (
        P(("expert", "wshard"), None),
        P(("expert", "wshard"), None),
        P("wshard"),
        P("wshard", None),
        P("wshard", None),
        P("wshard", None),
        P("wshard", None),
        P("wshard", None),
        P("wshard"),
        P("wshard", None),
        P("expert", "wshard", None),
        P("expert", "wshard", None),
    )
    return jax.shard_map(local, mesh=mesh, in_specs=in_specs, out_specs=out_specs, check_vma=False)
```

```python
import math

import jax
import jax.numpy as jnp
from jax import lax
from jax.experimental import pallas as pl
from jax.experimental.pallas import tpu as pltpu
from jax.sharding import PartitionSpec as P

HEADS = 12
HEAD_DIM = 64
BUCKETS = 32
BLOCK = 128
MOST_BLOCKS = 2
SHARDS = 4
LANES = 128
CAP = MOST_BLOCKS * BLOCK
W = "wshard"
E = "expert"

epsilon = 1e-06
thresholds = tuple((math.ceil(16 * 2 ** (3 * order / 16)) for order in range(1, 16)))
low = jnp.bfloat16
wide = jnp.float32
FULL = 60 << 20


def bucket_of(distance):
    passed = jnp.zeros_like(distance)
    for edge in thresholds:
        passed = passed + (distance >= edge).astype(jnp.int32)
    return jnp.where(distance < 16, distance, 16 + passed)


def along_last(left, right):
    return lax.dot_general(left, right, (((1,), (1,)), ((), ())), preferred_element_type=wide)


def along_first(left, right):
    return lax.dot_general(left, right, (((0,), (0,)), ((), ())), preferred_element_type=wide)


def matmul(left, right):
    return jnp.dot(left, right, preferred_element_type=wide)


def swap(value, axis, step):
    count = lax.axis_size(axis)
    return lax.ppermute(value, axis, [(i, i ^ step) for i in range(count)])


def gather_w(value):
    far = swap(value, W, 2)
    near = swap(value, W, 1)
    return [value, near, far, swap(far, W, 1)]


def sum_w(parts):
    a3 = swap(parts[3], W, 1)
    a1 = swap(parts[1], W, 1)
    across = (parts[2].astype(wide) + a3.astype(wide)).astype(low)
    return [parts[0], a1, swap(across, W, 2)]


def exchange_w(parts):
    return [parts[0]] + [swap(parts[s], W, s) for s in (1, 2, 3)]


def place(parts, me):
    out = jnp.zeros((len(parts),) + parts[0].shape, parts[0].dtype)
    for s, part in enumerate(parts):
        out = lax.dynamic_update_index_in_dim(out, part, me ^ s, 0)
    return out


def gather_e(value):
    count = lax.axis_size(E)
    if count > 8:
        whole = lax.all_gather(value, E, axis=0)
        me = lax.axis_index(E)
        order = me ^ jnp.arange(count, dtype=jnp.int32)
        whole = whole[order]
        return [whole[s] for s in range(count)]
    out = {0: value}
    for s in (4, 6, 2):
        out[s] = swap(value, E, s)
    for s in (0, 4, 6, 2):
        out[s ^ 1] = swap(out[s], E, 1)
    return [out[s] for s in range(8)]


def sum_e_late(parts, pairs):
    got = [swap(pair, E, 1) for pair in pairs]
    terms = []
    for s, other in ((4, got[0][0]), (6, got[0][1]), (2, got[1][0])):
        terms.append(swap((parts[s].astype(wide) + other.astype(wide)).astype(low), E, s))
    return [parts[0], got[1][1]] + terms


def sum_e(parts):
    count = lax.axis_size(E)
    if count > 8:
        me = lax.axis_index(E)
        whole = jnp.stack(parts)[me ^ jnp.arange(count, dtype=jnp.int32)]
        return [lax.psum_scatter(whole, E, scatter_dimension=0)], whole
    got = {s: swap(parts[s ^ 1], E, 1) for s in (4, 6, 2, 0)}
    terms = [parts[0], got[0]]
    for s in (4, 6, 2):
        part = (parts[s].astype(wide) + got[s].astype(wide)).astype(low)
        terms.append(swap(part, E, s))
    return terms, part


def experts_of(small_rows):
    return {32: 8, 80: 64}[small_rows]


def total_of(refs):
    out = refs[0][...].astype(wide)
    for ref in refs[1:]:
        out = out + ref[...].astype(wide)
    return out


def call(kernel, outs, scratch, cost, scalars, *args, after=(), room=None):
    outs, scratch, after = tuple(outs), tuple(scratch), tuple(after)
    smem = pl.BlockSpec(memory_space=pltpu.SMEM)
    block = pl.BlockSpec()
    apart = pl.BlockSpec(memory_space=pl.ANY)
    size = sum(a.size * a.dtype.itemsize for a in args)
    size = size + sum(math.prod(s) * jnp.dtype(d).itemsize for s, d in outs + scratch)
    skip = len(after)
    return pl.pallas_call(
        lambda *refs: kernel(*refs[skip:]),
        out_shape=tuple(jax.ShapeDtypeStruct(s, d) for s, d in outs),
        in_specs=[apart] * skip + [smem] + [block] * len(args),
        out_specs=tuple(block for _ in outs),
        scratch_shapes=[pltpu.VMEM(s, d) for s, d in scratch],
        compiler_params=pltpu.CompilerParams(vmem_limit_bytes=room or (10 << 20) + size),
        cost_estimate=pl.CostEstimate(flops=cost[0], bytes_accessed=cost[1], transcendentals=cost[2]),
    )(*after, scalars, *args)


def start_kernel(me_ref, q_ref, k_ref, v_ref, router_ref, one_ref, two_ref, table_ref, up_ref, routes_ref, *rest):
    outs, sent_ref, held = rest[:SHARDS], rest[SHARDS], rest[SHARDS + 1]
    shard = q_ref.shape[0]
    rows = up_ref.shape[0]
    for w in range(SHARDS):
        here = slice(w * shard, (w + 1) * shard)
        held[w] = jnp.concatenate([q_ref[:, here], k_ref[:, here], v_ref[:, here]], axis=1)
    i = lax.broadcasted_iota(jnp.int32, (shard, shard), 0)
    j = lax.broadcasted_iota(jnp.int32, (shard, shard), 1)
    eye = (i == j).astype(low)
    small = [
        router_ref[...],
        one_ref[...].reshape(1, shard),
        two_ref[...].reshape(1, shard),
        along_first(table_ref[...], eye[: table_ref.shape[0]]).astype(low),
    ]
    used = sum(piece.shape[0] for piece in small)
    small = jnp.concatenate(small + [jnp.zeros((outs[0].shape[0] - shard - used, shard), low)], axis=0)
    small = jnp.concatenate([small, jnp.zeros((small.shape[0], 2 * shard), low)], axis=1)
    for s in range(SHARDS):
        outs[s][:shard, :] = held[me_ref[0] ^ s]
        outs[s][shard:, :] = small
    sent_ref[:rows, :] = up_ref[...]
    named = jnp.concatenate([routes_ref[...].astype(low), jnp.zeros((14, rows), low)], axis=0)
    sent_ref[rows:, :] = jnp.concatenate([named, jnp.zeros((16, up_ref.shape[1] - rows), low)], axis=1)


def attend_kernel(me_ref, *refs):
    tokens, weights = refs[:SHARDS], refs[SHARDS : 2 * SHARDS]
    row_ref, column_ref, out_ref = refs[2 * SHARDS : 2 * SHARDS + 3]
    rest = refs[2 * SHARDS + 3 :]
    tokens_ref, first_ref, qkv_ref, probs_ref, att_ref, weight_ref, small_ref, router_ref = rest[:8]
    branches, held_w, held_b = rest[8 : 8 + SHARDS], rest[8 + SHARDS], rest[9 + SHARDS]
    me = me_ref[0]
    shard = out_ref.shape[0]
    chunk, width = tokens[0].shape
    length = chunk * SHARDS
    heads = probs_ref.shape[0]
    span = heads * HEAD_DIM
    for s in range(SHARDS):
        tokens_ref[me ^ s] = tokens[s][...]
        held_w[me ^ s] = weights[s][...]
    for w in range(SHARDS):
        weight_ref[w * shard : (w + 1) * shard, :] = held_w[w, :shard, :]
    small = jnp.concatenate([held_w[w, shard:, :shard] for w in range(SHARDS)], axis=1)
    small_ref[...] = small
    experts = experts_of(small_ref.shape[0])
    router_ref[...] = jnp.zeros_like(router_ref)
    router_ref[:experts, :] = small[:experts]
    gain_one = small[experts : experts + 1].astype(wide)

    shift = lax.broadcasted_iota(jnp.int32, (length, width), 0)
    lane = lax.broadcasted_iota(jnp.int32, (length, width), 1)
    bucket = bucket_of(jnp.where(shift > 0, length - shift, 0))
    per = BUCKETS // SHARDS
    hits = (lane == (bucket // per) * shard + bucket % per).astype(low)
    vectors = along_last(small[experts + 2 : experts + 2 + HEADS], hits)
    i = lax.broadcasted_iota(jnp.int32, (length, length), 0)
    j = lax.broadcasted_iota(jnp.int32, (length, length), 1)
    allowed = (j <= i) & (row_ref[...] == column_ref[...])
    which = lax.broadcasted_iota(jnp.int32, vectors.shape, 0)

    rows = tokens_ref[...].reshape(length, width).astype(wide)
    scale = lax.rsqrt(jnp.mean(rows * rows, axis=-1, keepdims=True) + epsilon)
    first = (rows * scale * gain_one).astype(low)
    first_ref[...] = first
    qkv = matmul(first, weight_ref[...]).astype(low)
    qkv_ref[...] = qkv
    columns = []
    for h in range(heads):
        vector = jnp.sum(jnp.where(which == me * heads + h, vectors, 0.0), axis=0, keepdims=True)
        bias = pltpu.roll(jnp.broadcast_to(vector, (length, length)), 0, 1, stride=1, stride_axis=0)
        bias = jnp.where(allowed, bias, -1e30)
        q = qkv[:, h * HEAD_DIM : (h + 1) * HEAD_DIM] * (HEAD_DIM**-0.5)
        k = qkv[:, span + h * HEAD_DIM : span + (h + 1) * HEAD_DIM]
        v = qkv[:, 2 * span + h * HEAD_DIM : 2 * span + (h + 1) * HEAD_DIM]
        pieces = []
        for b in range(SHARDS):
            end = (b + 1) * chunk
            here = slice(b * chunk, end)
            scores = along_last(q[here], k[:end]) + bias[here, :end]
            largest = jnp.max(scores, axis=-1, keepdims=True)
            grown = jnp.exp(scores - largest)
            total = jnp.sum(grown, axis=-1, keepdims=True)
            probs = (grown / total).astype(low)
            probs_ref[h, here, :end] = probs
            if end < length:
                probs_ref[h, here, end:] = jnp.zeros((chunk, length - end), low)
            pieces.append(matmul(probs, v[:end]))
        columns.append(jnp.concatenate(pieces, axis=0))
    attended = jnp.concatenate(columns, axis=1).astype(low)
    att_ref[...] = attended
    branch = matmul(attended, out_ref[...]).astype(low)
    for w in range(SHARDS):
        held_b[w] = branch[w * chunk : (w + 1) * chunk]
    for s in range(SHARDS):
        branches[s][...] = held_b[me ^ s]


def second_kernel(me_ref, tokens_ref, small_ref, *refs):
    terms, (resid_ref, second_ref) = refs[:-2], refs[-2:]
    experts = experts_of(small_ref.shape[0])
    gain = small_ref[experts + 1 : experts + 2, :].astype(wide)
    resid = tokens_ref[...].astype(wide) + total_of(terms)
    resid_ref[...] = resid
    scale = lax.rsqrt(jnp.mean(resid * resid, axis=-1, keepdims=True) + epsilon)
    second_ref[...] = (resid * scale * gain).astype(low)


def route_kernel(me_ref, *refs):
    me, limit = me_ref[1], me_ref[2].astype(wide)
    mine = me.astype(wide)
    sent, (dispatch_ref, rows_ref) = refs[:-2], refs[-2:]
    count = len(sent)
    tall = sent[0].shape[0] - 16
    hits, others = [], []
    for s in range(count):
        named = sent[s][tall:, :tall].astype(wide)
        r0, r1 = named[0:1], named[1:2]
        hits.append(((r0 == mine) | (r1 == mine)).astype(wide))
        others.append(jnp.where(r0 == mine, r1, r0))
    hits = jnp.concatenate(hits, axis=0)
    i = lax.broadcasted_iota(jnp.int32, (tall, tall), 0)
    j = lax.broadcasted_iota(jnp.int32, (tall, tall), 1)
    within = matmul(hits.astype(low), (i < j).astype(low))
    counts = jnp.sum(hits, axis=1, keepdims=True)
    index = me ^ lax.broadcasted_iota(jnp.int32, (count, 1), 0)
    slots = lax.broadcasted_iota(jnp.int32, (CAP, tall), 0).astype(wide)
    packed = jnp.zeros((CAP, rows_ref.shape[1]), wide)
    other = jnp.zeros((16, CAP), wide)
    for s in range(count):
        base = jnp.sum(jnp.where(index < (me ^ s), counts, 0.0), axis=0, keepdims=True)
        rank = within[s : s + 1] + base
        slot = jnp.where((hits[s : s + 1] > 0) & (rank < limit), rank, -1.0)
        one_hot = (slots == slot).astype(low)
        dispatch_ref[:, s * tall : (s + 1) * tall] = one_hot
        packed = packed + matmul(one_hot, sent[s][:tall, :])
        other = other + along_last(jnp.broadcast_to(others[s], (16, tall)).astype(low), one_hot)
    rows_ref[:CAP, :] = packed.astype(low)
    tail = jnp.zeros((16, rows_ref.shape[1] - CAP), low)
    rows_ref[CAP:, :] = jnp.concatenate([other.astype(low), tail], axis=1)


def upstream_kernel(me_ref, weight_ref, *refs):
    rows, backs, choices = refs[:SHARDS], refs[SHARDS : 2 * SHARDS], refs[2 * SHARDS :]
    mine = me_ref[1].astype(wide)
    i = lax.broadcasted_iota(jnp.int32, (CAP, CAP), 0)
    j = lax.broadcasted_iota(jnp.int32, (CAP, CAP), 1)
    lane = lax.broadcasted_iota(jnp.int32, (CAP, LANES), 1).astype(wide)
    for k in range(SHARDS):
        backs[k][...] = along_last(rows[k][:CAP, :], weight_ref[...])
        across = rows[k][CAP:, :CAP].astype(wide)[0:1]
        other = jnp.sum(jnp.where(i == j, across, 0.0), axis=1, keepdims=True)
        choices[k][...] = (lane == mine).astype(wide) - (lane == other).astype(wide)


def pack_kernel(me_ref, dispatch_ref, *refs):
    rows, out_ref = refs[:-1], refs[-1]
    tall = rows[0].shape[0]
    total = jnp.zeros(out_ref.shape, wide)
    for s, ref in enumerate(rows):
        total = total + matmul(dispatch_ref[:, s * tall : (s + 1) * tall], ref[...])
    out_ref[...] = total.astype(low)


def expert_kernel(me_ref, back_a, back_b, choice_a, choice_b, weight_ref, router_ref, *refs):
    rows, outs, (act_ref, back_pre_ref, logits_ref) = refs[:2], refs[2:4], refs[4:]
    for k in range(2):
        here = slice(k * CAP, (k + 1) * CAP)
        block = rows[k][...]
        choice = (choice_a, choice_b)[k][...]
        back = (back_a, back_b)[k][...]
        chosen = jnp.sum(along_last(block, router_ref[...]) * choice, axis=1, keepdims=True)
        gate = jax.nn.sigmoid(chosen)
        pre = along_last(block, weight_ref[...])
        square = pre * pre
        slope = math.sqrt(2 / math.pi)
        bent = jnp.tanh(slope * pre * (1.0 + 0.044715 * square))
        half = 0.5 * (1.0 + bent)
        act = pre * half
        steep = half + 0.5 * pre * (1.0 - bent * bent) * (slope * (1.0 + 3 * 0.044715 * square))
        act_ref[here, :] = (act * gate).astype(low)
        back_pre = (steep * (back * gate)).astype(low)
        back_pre_ref[here, :] = back_pre
        back_gate = jnp.sum(act * back, axis=1, keepdims=True)
        logits = (gate * jax.nn.sigmoid(-chosen) * back_gate * choice).astype(low)
        logits_ref[here, :] = logits
        outs[k][...] = (matmul(back_pre, weight_ref[...]) + matmul(logits, router_ref[...])).astype(low)


def result_kernel(order, me_ref, weight_ref, act_a, act_b, logits_a, logits_b, *refs):
    rows, outs, router_ref = refs[:SHARDS], refs[SHARDS:-1], refs[-1]
    router = jnp.zeros(router_ref.shape, wide)
    for k, s in enumerate(order):
        here = slice((k % 2) * CAP, (k % 2 + 1) * CAP)
        outs[s][...] = matmul((act_a, act_b)[k // 2][here, :], weight_ref[...]).astype(low)
        router = router + along_first(rows[s][...], (logits_a, logits_b)[k // 2][here, :])
    router_ref[...] = router


def unpack_late_kernel(me_ref, dispatch_ref, *refs):
    terms, outs, pairs = refs[:3], refs[3:-2], refs[-2:]
    block = total_of(terms).astype(low)
    tall = outs[0].shape[0]
    for k, s in enumerate((4, 6, 2, 0)):
        outs[s // 2][...] = along_first(dispatch_ref[:, s * tall : (s + 1) * tall], block).astype(low)
        other = dispatch_ref[:, (s + 1) * tall : (s + 2) * tall]
        pairs[k // 2][k % 2] = along_first(other, block).astype(low)


def layer_kernel(me_ref, resid_ref, *refs):
    refs[-1][...] = (resid_ref[...] + total_of(refs[:-1])).astype(low)


def grads_kernel(order, me_ref, *refs):
    acts, pres = refs[0:2], refs[2:4]
    rows, ups = refs[4 : 4 + SHARDS], refs[4 + SHARDS : 4 + 2 * SHARDS]
    first_ref, second_ref = refs[4 + 2 * SHARDS :]
    acts = jnp.concatenate([ref[...] for ref in acts], axis=0)
    pres = jnp.concatenate([ref[...] for ref in pres], axis=0)
    block = jnp.concatenate([rows[s][...] for s in order], axis=0)
    first_ref[0] = along_first(pres, block)
    ups = jnp.concatenate([ups[s][:CAP, :] for s in order], axis=0)
    second_ref[0] = along_first(acts, ups)


def unpack_kernel(me_ref, dispatch_ref, *refs):
    terms, outs = refs[:3], refs[3:]
    block = total_of(terms).astype(low)
    tall = outs[0].shape[0]
    for s, ref in enumerate(outs):
        ref[...] = along_first(dispatch_ref[:, s * tall : (s + 1) * tall], block).astype(low)


def resid_back_kernel(me_ref, resid_ref, small_ref, cotangent_ref, *refs):
    terms, (back_ref, branch_ref, gain_ref) = refs[:-3], refs[-3:]
    experts = experts_of(small_ref.shape[0])
    gain = small_ref[experts + 1 : experts + 2, :].astype(wide)
    resid = resid_ref[...]
    upstream = total_of(terms)
    r = lax.rsqrt(jnp.mean(resid * resid, axis=-1, keepdims=True) + epsilon)
    gain_ref[...] = jnp.sum(upstream * (resid * r), axis=0, keepdims=True)
    m = upstream * gain
    back = r * m - (r * r * r) * resid * jnp.mean(m * resid, axis=-1, keepdims=True)
    back = back + cotangent_ref[...].astype(wide)
    back_ref[...] = back
    branch_ref[...] = back.astype(low)


def attend_back_kernel(
    experts,
    table_rows,
    me_ref,
    out_ref,
    qkv_ref,
    probs_ref,
    weight_ref,
    tokens_ref,
    first_ref,
    att_ref,
    gain_two_ref,
    router_ref,
    *refs,
):
    ups, backs = refs[:SHARDS], refs[SHARDS : 2 * SHARDS]
    parts, (held, table) = refs[2 * SHARDS : -2], refs[-2:]
    me = me_ref[0]
    shard = out_ref.shape[0]
    chunk, width = ups[0].shape
    length = chunk * SHARDS
    heads = probs_ref.shape[0]
    span = heads * HEAD_DIM
    scale = HEAD_DIM**-0.5
    for s in range(SHARDS):
        held[me ^ s] = ups[s][...]
    up = held[...].reshape(length, width)
    back = along_last(up, out_ref[...]).astype(low)
    qkv = qkv_ref[...]
    dq, dk, dv = [], [], []
    i = lax.broadcasted_iota(jnp.int32, (chunk, chunk), 0)
    j = lax.broadcasted_iota(jnp.int32, (chunk, chunk), 1)
    reverse = (i + j == chunk - 1).astype(low)
    diagonals = []
    for h in range(heads):
        q = qkv[:, h * HEAD_DIM : (h + 1) * HEAD_DIM]
        k = qkv[:, span + h * HEAD_DIM : span + (h + 1) * HEAD_DIM]
        v = qkv[:, 2 * span + h * HEAD_DIM : 2 * span + (h + 1) * HEAD_DIM]
        d = back[:, h * HEAD_DIM : (h + 1) * HEAD_DIM]
        probs_low = probs_ref[h]
        probs = probs_low.astype(wide)
        back_probs = along_last(d, v)
        inner = jnp.sum(back_probs * probs, axis=-1, keepdims=True)
        scores = (probs * (back_probs - inner)).astype(low)
        diagonal = jnp.zeros((1, length), wide)
        for b in range(SHARDS):
            turned = matmul(reverse, scores[b * chunk : (b + 1) * chunk])
            start = (1 - (b + 1) * chunk) % length
            turned = pltpu.roll(turned, start, 1, stride=1, stride_axis=0)
            diagonal = diagonal + jnp.sum(turned, axis=0, keepdims=True)
        diagonals.append(diagonal)
        dq.append((matmul(scores, k) * scale).astype(low))
        dk.append((along_first(scores, q) * scale).astype(low))
        dv.append(along_first(probs_low, d).astype(low))
    dqkv = jnp.concatenate(dq + dk + dv, axis=1)
    back_first = along_last(dqkv, weight_ref[...])
    rows = tokens_ref[...].reshape(length, width).astype(wide)
    rows = rows * lax.rsqrt(jnp.mean(rows * rows, axis=-1, keepdims=True) + epsilon)
    for w in range(SHARDS):
        held[w] = back_first[w * chunk : (w + 1) * chunk].astype(low)
    for s in range(SHARDS):
        backs[s][...] = held[me ^ s]

    gains = [jnp.sum(back_first * rows, axis=0, keepdims=True), gain_two_ref[...]]
    gains = jnp.concatenate(gains + [jnp.zeros((14, width), wide)], axis=0).astype(low)
    i = lax.broadcasted_iota(jnp.int32, (LANES, LANES), 0)
    j = lax.broadcasted_iota(jnp.int32, (LANES, LANES), 1)
    extra = along_first(gains, (i[:16] == j[:16]).astype(low))
    extra = extra + matmul(router_ref[...].astype(low), (i + 2 == j).astype(low))
    above = jnp.zeros((2 + experts, length), wide)
    below = jnp.zeros((LANES - 2 - experts - heads, length), wide)
    spread = jnp.concatenate([above] + diagonals + [below], axis=0)
    shift = lax.broadcasted_iota(jnp.int32, (length, width), 0)
    lane = lax.broadcasted_iota(jnp.int32, (length, width), 1)
    bucket = bucket_of(jnp.where(shift > 0, length - shift, 0))
    hits = (lane == (bucket // table_rows) * shard + bucket % table_rows).astype(low)
    spread_low = spread.astype(low)
    rest = (spread - spread_low.astype(wide)).astype(low)
    turn = (((0,), (1,)), ((), ()))
    extra = extra + lax.dot_general(hits, spread_low, turn, preferred_element_type=wide)
    extra = extra + lax.dot_general(hits, rest, turn, preferred_element_type=wide)
    output = along_first(att_ref[...], up)
    output = jnp.concatenate([output[:, w * shard : (w + 1) * shard] for w in range(SHARDS)], axis=0)
    grads = jnp.concatenate([along_first(first_ref[...], dqkv), extra, output], axis=1)
    if len(parts) == 1:
        parts[0][...] = grads.astype(low)
    else:
        table[...] = grads
        piece = parts[0].shape[1]
        for s, ref in enumerate(parts):
            for w in range(SHARDS):
                start = pl.multiple_of(w * shard + (me_ref[1] ^ s) * piece, 8)
                ref[w] = table[pl.ds(start, piece), :].astype(low)


def join_kernel(me_ref, *refs):
    terms, outs, output_ref, held = refs[:5], refs[5 : 5 + SHARDS], refs[5 + SHARDS], refs[6 + SHARDS]
    total = total_of(terms)
    columns = outs[0].shape[1]
    held[...] = total[:, :, :columns]
    for s in range(SHARDS):
        outs[s][...] = held[me_ref[0] ^ s].astype(low)
    output_ref[...] = jnp.concatenate([total[w][:, columns:] for w in range(SHARDS)], axis=1).astype(low)


def order_kernel(experts, me_ref, *refs):
    parts, output_ref, out_ref, held = refs[:SHARDS], refs[SHARDS], refs[SHARDS + 1], refs[SHARDS + 2]
    for s in range(SHARDS):
        held[me_ref[0] ^ s] = parts[s][...].astype(wide)
    own = HEADS // SHARDS
    span = own * HEAD_DIM
    blocks = [held[w] for w in range(SHARDS)]
    pieces = [blocks[w][:, k * span : (k + 1) * span] for k in range(3) for w in range(SHARDS)]
    lane = lax.broadcasted_iota(jnp.int32, (parts[0].shape[0], LANES), 1)
    extra = jnp.zeros((parts[0].shape[0], LANES), wide)
    for w in range(SHARDS):
        small = blocks[w][:, 3 * span :]
        heads = jnp.where((lane >= 2 + experts) & (lane < 2 + experts + own), small, 0.0)
        extra = extra + jnp.where(lane < 2 + experts, small, 0.0) + pltpu.roll(heads, own * w, 1)
    pieces = pieces + [output_ref[...].astype(wide), extra]
    out_ref[...] = jnp.concatenate(pieces, axis=1).astype(low)


def final_kernel(me_ref, *refs):
    parts, outs = refs[:-9], refs[-9:-1]
    held = refs[-1]
    piece = parts[0].shape[0]
    width = outs[0].shape[1]
    experts = outs[6].shape[1]
    for s, ref in enumerate(parts):
        here = pl.ds(pl.multiple_of((me_ref[1] ^ s) * piece, 8), piece)
        block = ref[...].astype(wide)
        for k in range(4):
            outs[k][here, :] = block[:, k * width : (k + 1) * width]
        held[here, :] = block[:, 4 * width :]
    extra = held[...]
    shard = extra.shape[0]
    i = lax.broadcasted_iota(jnp.int32, (shard, shard), 0)
    j = lax.broadcasted_iota(jnp.int32, (shard, shard), 1)
    turned = along_first(extra.astype(low), (i == j).astype(low))
    outs[4][...] = turned[0:1]
    outs[5][...] = turned[1:2]
    outs[6][...] = extra[:, 2 : 2 + experts]
    outs[7][...] = extra[: outs[7].shape[0], 2 + experts : 2 + experts + HEADS]


def tokens_back_kernel(me_ref, tokens_ref, small_ref, resid_ref, *refs):
    terms, out_ref = refs[:-1], refs[-1]
    experts = experts_of(small_ref.shape[0])
    gain = small_ref[experts : experts + 1, :].astype(wide)
    rows = tokens_ref[...].astype(wide)
    r = lax.rsqrt(jnp.mean(rows * rows, axis=-1, keepdims=True) + epsilon)
    m = total_of(terms) * gain
    back = r * m - (r * r * r) * rows * jnp.mean(m * rows, axis=-1, keepdims=True)
    out_ref[...] = resid_ref[...] + back


def local(
    tokens,
    segments,
    routes,
    blocks,
    attention_gain,
    query_weight,
    key_weight,
    value_weight,
    output_weight,
    position_bias,
    feed_gain,
    router_weight,
    expert_in,
    expert_out,
    cotangent,
):
    rows, width = tokens.shape
    length = rows * SHARDS
    experts = lax.axis_size(E)
    me_w = lax.axis_index(W)
    me_e = lax.axis_index(E)
    me = jnp.stack([me_w, me_e, blocks[0] * BLOCK]).astype(jnp.int32)
    shard = query_weight.shape[0]
    own_heads = HEADS // SHARDS
    table_rows = position_bias.shape[0]
    first_local, second_local = expert_in[0], expert_out[0]
    row = (rows, width)
    packed_row = (CAP, width)

    quick = experts == 8
    small_rows = -(-(experts + 2 + HEADS) // 16) * 16
    tokens_rel = gather_w(tokens)
    *weight_parts, sent = call(
        start_kernel,
        [((shard + small_rows, 3 * shard), low)] * SHARDS + [((rows + 16, width), low)],
        [((SHARDS, shard, 3 * shard), low)],
        (0, 4 * shard * width * 3, 0),
        me,
        query_weight,
        key_weight,
        value_weight,
        router_weight.T,
        attention_gain,
        feed_gain,
        position_bias,
        cotangent,
        routes.T,
        room=FULL,
    )
    weight_rel = exchange_w(weight_parts)
    sent = gather_e(sent)

    square = (own_heads, length, length)
    outs = call(
        attend_kernel,
        [
            ((SHARDS, rows, width), low),
            ((length, width), low),
            ((length, 3 * shard), low),
            (square, low),
            ((length, shard), low),
            ((width, 3 * shard), low),
            ((small_rows, width), low),
            ((LANES, width), low),
        ]
        + [(row, low)] * SHARDS,
        [((SHARDS, shard + small_rows, 3 * shard), low), ((SHARDS, rows, width), low)],
        (2 * length * width * 4 * shard, 8 * length * length * own_heads, own_heads * length * length),
        me,
        *tokens_rel,
        *weight_rel,
        segments,
        segments.reshape(length, 1),
        output_weight,
        room=FULL,
    )
    tokens_all, first, qkv, probs, attended, weight, small, router = outs[:8]
    resid, second = call(
        second_kernel,
        [(row, wide), (row, low)],
        [],
        (0, 8 * rows * width, 0),
        me,
        tokens,
        small,
        *sum_w(outs[8:]),
    )

    dispatch, upstream_rows = call(
        route_kernel,
        [((CAP, experts * rows), low), ((CAP + 16, width), low)],
        [],
        (2 * CAP * experts * rows * width, 4 * experts * rows * width, 0),
        me,
        *sent,
    )
    upstream_rel = gather_w(upstream_rows)
    order = (3, 2, 1, 0)
    outs = call(
        upstream_kernel,
        [(packed_row, wide)] * SHARDS + [((CAP, LANES), wide)] * SHARDS,
        [],
        (2 * SHARDS * CAP * width * width, 4 * SHARDS * CAP * width, 0),
        me,
        second_local,
        *[upstream_rel[s] for s in order],
    )
    back_act, choice = outs[:SHARDS], outs[SHARDS:]

    (packed,) = call(
        pack_kernel,
        [(packed_row, low)],
        [],
        (2 * CAP * experts * rows * width, 4 * experts * rows * width, 0),
        me,
        dispatch,
        *gather_e(second),
        after=(back_act[0],),
    )
    rows_rel = gather_w(packed)
    half = (2 * CAP, width)

    def expert_half(k, after):
        return call(
            expert_kernel,
            [(packed_row, low)] * 2 + [(half, low), (half, low), ((2 * CAP, LANES), low)],
            [],
            (8 * CAP * width * width, 8 * CAP * width, 2 * CAP * width),
            me,
            back_act[2 * k],
            back_act[2 * k + 1],
            choice[2 * k],
            choice[2 * k + 1],
            first_local,
            router,
            rows_rel[order[2 * k]],
            rows_rel[order[2 * k + 1]],
            after=after,
        )

    halves = [expert_half(0, ())]
    near = swap(halves[0][0], W, 1)
    across = (halves[0][1].astype(wide) + near.astype(wide)).astype(low)
    halves.append(expert_half(1, (across,)))
    far = swap(across, W, 2)
    back_parts = call(
        unpack_kernel,
        [(row, low)] * experts,
        [],
        (2 * CAP * experts * rows * width, 4 * experts * rows * width, 0),
        me,
        dispatch,
        halves[1][1],
        swap(halves[1][0], W, 1),
        far,
    )
    back_terms, tie = sum_e(back_parts)

    *results, router_grad = call(
        lambda *refs: result_kernel(order, *refs),
        [(packed_row, low)] * SHARDS + [((width, LANES), wide)],
        [],
        (8 * CAP * width * width, 8 * CAP * width, 0),
        me,
        second_local,
        halves[0][2],
        halves[1][2],
        halves[0][4],
        halves[1][4],
        *rows_rel,
        after=(back_parts[0],),
    )
    result_terms = sum_w(results)

    back_resid, back_branch, gain_two_grad = call(
        resid_back_kernel,
        [(row, wide), (row, low), ((1, width), wide)],
        [],
        (0, 16 * rows * width, 0),
        me,
        resid,
        small,
        cotangent,
        *back_terms,
    )
    back_rel = gather_w(back_branch)
    if quick:
        outs = call(
            unpack_late_kernel,
            [(row, low)] * 4 + [((2,) + row, low)] * 2,
            [],
            (2 * CAP * experts * rows * width, 4 * experts * rows * width, 0),
            me,
            dispatch,
            *result_terms,
            after=(tie,),
        )
        mixed_terms = sum_e_late(dict(zip((0, 2, 4, 6), outs[:4])), outs[4:])
    else:
        mixed_parts = call(
            unpack_kernel,
            [(row, low)] * experts,
            [],
            (2 * CAP * experts * rows * width, 4 * experts * rows * width, 0),
            me,
            dispatch,
            *result_terms,
        )
        mixed_terms, _ = sum_e(mixed_parts)
    (layer_out,) = call(
        layer_kernel, [(row, low)], [], (0, 16 * rows * width, 0), me, resid, *mixed_terms
    )
    columns = 3 * shard + LANES
    piece = shard // experts
    part = (SHARDS, piece, columns + shard)
    outs = call(
        lambda *refs: attend_back_kernel(experts, table_rows, *refs),
        [(row, low)] * SHARDS + ([(part, low)] * experts if quick else [((width, columns + shard), low)]),
        [((SHARDS, rows, width), low), ((width, columns + shard), wide)],
        (2 * length * width * 9 * shard, 8 * length * length * own_heads, 0),
        me,
        output_weight,
        qkv,
        probs,
        weight,
        tokens_all,
        first,
        attended,
        gain_two_grad,
        router_grad,
        *back_rel,
        after=(mixed_terms[0],),
    )
    grads = outs[SHARDS:]
    (tokens_grad,) = call(
        tokens_back_kernel,
        [(row, wide)],
        [],
        (0, 16 * rows * width, 0),
        me,
        tokens,
        small,
        back_resid,
        *sum_w(outs[:SHARDS]),
    )

    first_grad, second_grad = call(
        lambda *refs: grads_kernel(order, *refs),
        [((1,) + first_local.shape, wide), ((1,) + second_local.shape, wide)],
        [],
        (16 * CAP * width * width, 24 * CAP * width, 0),
        me,
        halves[0][2],
        halves[1][2],
        halves[0][3],
        halves[1][3],
        *rows_rel,
        *upstream_rel,
        after=(grads[0],),
    )

    if quick:
        terms, _ = sum_e(grads)
        *grads, output_grad = call(
            join_kernel,
            [((piece, columns), low)] * SHARDS + [((piece, width), low)],
            [((SHARDS, piece, columns), wide)],
            (0, 8 * width * columns, 0),
            me,
            *terms,
        )
        (grads,) = call(
            lambda *refs: order_kernel(experts, *refs),
            [((piece, 4 * width + LANES), low)],
            [((SHARDS, piece, columns), wide)],
            (0, 8 * width * columns, 0),
            me,
            *exchange_w(grads),
            output_grad,
        )
        shape = (shard, width)
        outs = call(
            final_kernel,
            [(shape, wide)] * 4
            + [((1, shard), wide)] * 2
            + [((shard, experts), wide), ((table_rows, HEADS), wide)],
            [((shard, LANES), wide)],
            (0, 16 * shard * width, 0),
            me,
            *gather_e(grads),
        )
        query_grad, key_grad, value_grad, output_grad = outs[:4]
        gain_one_grad, gain_two_grad = outs[4].reshape(shard), outs[5].reshape(shard)
        router_grad, table_grad = outs[6], outs[7]
    else:
        grads = lax.psum(grads[0], E).astype(wide).reshape(SHARDS, shard, columns + shard)
        output_grad = grads[:, :, columns:].transpose(1, 0, 2).reshape(shard, width)
        grads = grads[:, :, :columns].astype(low)
        grads = place(
            exchange_w([lax.dynamic_index_in_dim(grads, me_w ^ s, 0, False) for s in range(SHARDS)]), me_w
        ).astype(wide)
        main = grads[:, :, : 3 * shard].reshape(SHARDS, shard, 3, shard).transpose(2, 1, 0, 3)
        query_grad, key_grad, value_grad = main.reshape(3, shard, width)
        extra = grads[:, :, 3 * shard :]
        summed = jnp.sum(extra[:, :, : 2 + experts], axis=0)
        gain_one_grad, gain_two_grad, router_grad = summed[:, 0], summed[:, 1], summed[:, 2:]
        table_grad = extra[:, :table_rows, 2 + experts : 2 + experts + own_heads]
        table_grad = table_grad.transpose(1, 0, 2).reshape(table_rows, HEADS)
    return (
        layer_out,
        tokens_grad,
        gain_one_grad,
        query_grad,
        key_grad,
        value_grad,
        output_grad,
        table_grad,
        gain_two_grad,
        router_grad,
        first_grad,
        second_grad,
    )


def solution(mesh):
    in_specs = (
        P(("expert", "wshard"), None),
        P("expert", None),
        P(("expert", "wshard"), None),
        P("expert"),
        P("wshard"),
        P("wshard", None),
        P("wshard", None),
        P("wshard", None),
        P("wshard", None),
        P("wshard", None),
        P("wshard"),
        P("wshard", None),
        P("expert", "wshard", None),
        P("expert", "wshard", None),
        P(("expert", "wshard"), None),
    )
    out_specs = (
        P(("expert", "wshard"), None),
        P(("expert", "wshard"), None),
        P("wshard"),
        P("wshard", None),
        P("wshard", None),
        P("wshard", None),
        P("wshard", None),
        P("wshard", None),
        P("wshard"),
        P("wshard", None),
        P("expert", "wshard", None),
        P("expert", "wshard", None),
    )
    return jax.shard_map(local, mesh=mesh, in_specs=in_specs, out_specs=out_specs, check_vma=False)
```

```python
import math

import jax
import jax.numpy as jnp
from jax import lax
from jax.experimental import pallas as pl
from jax.experimental.pallas import tpu as pltpu
from jax.sharding import PartitionSpec as P

HEADS = 12
HEAD_DIM = 64
BUCKETS = 32
BLOCK = 128
MOST_BLOCKS = 2
SHARDS = 4
LANES = 128
CAP = MOST_BLOCKS * BLOCK
W = "wshard"
E = "expert"

epsilon = 1e-06
thresholds = tuple((math.ceil(16 * 2 ** (3 * order / 16)) for order in range(1, 16)))
low = jnp.bfloat16
wide = jnp.float32
FULL = 60 << 20


def bucket_of(distance):
    passed = jnp.zeros_like(distance)
    for edge in thresholds:
        passed = passed + (distance >= edge).astype(jnp.int32)
    return jnp.where(distance < 16, distance, 16 + passed)


def along_last(left, right):
    return lax.dot_general(left, right, (((1,), (1,)), ((), ())), preferred_element_type=wide)


def along_first(left, right):
    return lax.dot_general(left, right, (((0,), (0,)), ((), ())), preferred_element_type=wide)


def matmul(left, right):
    return jnp.dot(left, right, preferred_element_type=wide)


def swap(value, axis, step):
    count = lax.axis_size(axis)
    return lax.ppermute(value, axis, [(i, i ^ step) for i in range(count)])


def gather_w(value):
    far = swap(value, W, 2)
    near = swap(value, W, 1)
    return [value, near, far, swap(far, W, 1)]


def sum_w(own, across, pair):
    got = swap(pair, W, 1)
    across = (across.astype(wide) + got[0].astype(wide)).astype(low)
    return [own, got, swap(across, W, 2)], across


def exchange_w(parts):
    return [parts[0]] + [swap(parts[s], W, s) for s in (1, 2, 3)]


def place(parts, me):
    out = jnp.zeros((len(parts),) + parts[0].shape, parts[0].dtype)
    for s, part in enumerate(parts):
        out = lax.dynamic_update_index_in_dim(out, part, me ^ s, 0)
    return out


def gather_e(value):
    count = lax.axis_size(E)
    if count > 8:
        whole = lax.all_gather(value, E, axis=0)
        me = lax.axis_index(E)
        order = me ^ jnp.arange(count, dtype=jnp.int32)
        whole = whole[order]
        return [whole[s] for s in range(count)]
    out = {0: value}
    for s in (4, 6, 2):
        out[s] = swap(value, E, s)
    for s in (0, 4, 6, 2):
        out[s ^ 1] = swap(out[s], E, 1)
    return [out[s] for s in range(8)]


def sum_e(parts):
    count = lax.axis_size(E)
    if count > 8:
        me = lax.axis_index(E)
        whole = jnp.stack(parts)[me ^ jnp.arange(count, dtype=jnp.int32)]
        return [lax.psum_scatter(whole, E, scatter_dimension=0)]
    got = {s: swap(parts[s ^ 1], E, 1) for s in (4, 6, 2, 0)}
    terms = [parts[0], got[0]]
    for s in (4, 6, 2):
        part = (parts[s].astype(wide) + got[s].astype(wide)).astype(low)
        terms.append(swap(part, E, s))
    return terms


def experts_of(small_rows):
    return {32: 8, 80: 64}[small_rows]


def total_of(refs):
    rank = len(refs[0].shape)
    out = refs[0][...].astype(wide)
    for ref in refs[1:]:
        out = out + (ref[...] if len(ref.shape) == rank else ref[1]).astype(wide)
    return out


def store_w(outs, held, me):
    outs[0][...] = held[me]
    outs[1][...] = held[me ^ 2]
    outs[2][0] = held[me ^ 3]
    outs[2][1] = held[me ^ 1]


def call(kernel, outs, scratch, scalars, *args, after=(), room=None, cover=0):
    outs, scratch, after = tuple(outs), tuple(scratch), tuple(after)
    smem = pl.BlockSpec(memory_space=pltpu.SMEM)
    block = pl.BlockSpec()
    apart = pl.BlockSpec(memory_space=pl.ANY)
    size = sum(a.size * a.dtype.itemsize for a in args)
    size = size + sum(math.prod(s) * jnp.dtype(d).itemsize for s, d in outs + scratch)
    skip = len(after)
    return pl.pallas_call(
        lambda *refs: kernel(*refs[skip:]),
        out_shape=tuple(jax.ShapeDtypeStruct(s, d) for s, d in outs),
        in_specs=[apart] * skip + [smem] + [block] * len(args),
        out_specs=tuple(block for _ in outs),
        scratch_shapes=[pltpu.VMEM(s, d) for s, d in scratch],
        compiler_params=pltpu.CompilerParams(vmem_limit_bytes=room or (10 << 20) + size),
        cost_estimate=pl.CostEstimate(flops=1 + cover * 10**9, bytes_accessed=1, transcendentals=0),
    )(*after, scalars, *args)


def tie(value, *after):
    apart = pl.BlockSpec(memory_space=pl.ANY)
    return pl.pallas_call(
        lambda *refs: None,
        out_shape=jax.ShapeDtypeStruct(value.shape, value.dtype),
        in_specs=[apart] * (1 + len(after)),
        out_specs=apart,
        input_output_aliases={0: 0},
        compiler_params=pltpu.CompilerParams(vmem_limit_bytes=1 << 20),
        cost_estimate=pl.CostEstimate(flops=1, bytes_accessed=1, transcendentals=0),
    )(value, *after)


def start_kernel(me_ref, q_ref, k_ref, v_ref, router_ref, one_ref, two_ref, table_ref, *rest):
    outs, held = rest[:SHARDS], rest[SHARDS]
    shard = q_ref.shape[0]
    for w in range(SHARDS):
        here = slice(w * shard, (w + 1) * shard)
        held[w] = jnp.concatenate([q_ref[:, here], k_ref[:, here], v_ref[:, here]], axis=1)
    i = lax.broadcasted_iota(jnp.int32, (table_ref.shape[0], shard), 0)
    j = lax.broadcasted_iota(jnp.int32, (table_ref.shape[0], shard), 1)
    small = [
        router_ref[...],
        one_ref[...].reshape(1, shard),
        two_ref[...].reshape(1, shard),
        along_first(table_ref[...], (i == j).astype(low)).astype(low),
    ]
    used = sum(piece.shape[0] for piece in small)
    small = jnp.concatenate(small + [jnp.zeros((outs[0].shape[0] - shard - used, shard), low)], axis=0)
    small = jnp.concatenate([small, jnp.zeros((small.shape[0], 2 * shard), low)], axis=1)
    for s in range(SHARDS):
        outs[s][:shard, :] = held[me_ref[0] ^ s]
        outs[s][shard:, :] = small


def sent_kernel(me_ref, up_ref, routes_ref, sent_ref):
    rows, width = up_ref.shape
    sent_ref[:rows, :] = up_ref[...]
    blocks = jnp.full((1, rows), me_ref[2].astype(wide) / BLOCK).astype(low)
    named = jnp.concatenate([routes_ref[...].astype(low), blocks, jnp.zeros((13, rows), low)], axis=0)
    sent_ref[rows:, :] = jnp.concatenate([named, jnp.zeros((16, width - rows), low)], axis=1)


def attend_kernel(me_ref, *refs):
    tokens, weights = refs[:SHARDS], refs[SHARDS : 2 * SHARDS]
    row_ref, *rest = refs[2 * SHARDS :]
    tokens_ref, first_ref, qkv_ref, probs_ref, att_ref, weight_ref, small_ref, router_ref, held_w = rest
    me = me_ref[0]
    shard = att_ref.shape[1]
    chunk, width = tokens[0].shape
    length = chunk * SHARDS
    heads = probs_ref.shape[0]
    span = heads * HEAD_DIM
    for s in range(SHARDS):
        tokens_ref[me ^ s] = tokens[s][...]
        held_w[me ^ s] = weights[s][...]
    for w in range(SHARDS):
        weight_ref[w * shard : (w + 1) * shard, :] = held_w[w, :shard, :]
    small = jnp.concatenate([held_w[w, shard:, :shard] for w in range(SHARDS)], axis=1)
    small_ref[...] = small
    experts = experts_of(small_ref.shape[0])
    router_ref[...] = jnp.zeros_like(router_ref)
    router_ref[:experts, :] = small[:experts]
    gain_one = small[experts : experts + 1].astype(wide)

    shift = lax.broadcasted_iota(jnp.int32, (length, width), 0)
    lane = lax.broadcasted_iota(jnp.int32, (length, width), 1)
    bucket = bucket_of(jnp.where(shift > 0, length - shift, 0))
    per = BUCKETS // SHARDS
    hits = (lane == (bucket // per) * shard + bucket % per).astype(low)
    vectors = along_last(small[experts + 2 : experts + 2 + HEADS], hits)
    i = lax.broadcasted_iota(jnp.int32, (length, length), 0)
    j = lax.broadcasted_iota(jnp.int32, (length, length), 1)
    marks = jnp.broadcast_to(row_ref[...], (length, length))
    column = jnp.sum(jnp.where(i == j, marks, 0), axis=1, keepdims=True)
    allowed = (j <= i) & (marks == column)
    which = lax.broadcasted_iota(jnp.int32, vectors.shape, 0)

    rows = tokens_ref[...].reshape(length, width).astype(wide)
    scale = lax.rsqrt(jnp.mean(rows * rows, axis=-1, keepdims=True) + epsilon)
    first = (rows * scale * gain_one).astype(low)
    first_ref[...] = first
    qkv = matmul(first, weight_ref[...]).astype(low)
    qkv_ref[...] = qkv
    columns = []
    for h in range(heads):
        vector = jnp.sum(jnp.where(which == me * heads + h, vectors, 0.0), axis=0, keepdims=True)
        bias = pltpu.roll(jnp.broadcast_to(vector, (length, length)), 0, 1, stride=1, stride_axis=0)
        bias = jnp.where(allowed, bias, -1e30)
        q = qkv[:, h * HEAD_DIM : (h + 1) * HEAD_DIM] * (HEAD_DIM**-0.5)
        k = qkv[:, span + h * HEAD_DIM : span + (h + 1) * HEAD_DIM]
        v = qkv[:, 2 * span + h * HEAD_DIM : 2 * span + (h + 1) * HEAD_DIM]
        pieces = []
        for b in range(SHARDS):
            end = (b + 1) * chunk
            here = slice(b * chunk, end)
            scores = along_last(q[here], k[:end]) + bias[here, :end]
            largest = jnp.max(scores, axis=-1, keepdims=True)
            grown = jnp.exp(scores - largest)
            total = jnp.sum(grown, axis=-1, keepdims=True)
            probs = (grown / total).astype(low)
            probs_ref[h, here, :end] = probs
            if end < length:
                probs_ref[h, here, end:] = jnp.zeros((chunk, length - end), low)
            pieces.append(matmul(probs, v[:end]))
        columns.append(jnp.concatenate(pieces, axis=0))
    att_ref[...] = jnp.concatenate(columns, axis=1).astype(low)


def branch_kernel(me_ref, att_ref, out_ref, *refs):
    sent, branches, held = refs[:-5], refs[-5:-2], refs[-1]
    chunk = held.shape[1]
    for k, ref in enumerate(sent):
        refs[-2][k] = ref[...]
    branch = matmul(att_ref[...], out_ref[...]).astype(low)
    for w in range(SHARDS):
        held[w] = branch[w * chunk : (w + 1) * chunk]
    store_w(branches, held, me_ref[0])


def second_kernel(me_ref, tokens_ref, small_ref, *refs):
    terms, (resid_ref, second_ref) = refs[:-2], refs[-2:]
    experts = experts_of(small_ref.shape[0])
    gain = small_ref[experts + 1 : experts + 2, :].astype(wide)
    resid = tokens_ref[...].astype(wide) + total_of(terms)
    resid_ref[...] = resid
    scale = lax.rsqrt(jnp.mean(resid * resid, axis=-1, keepdims=True) + epsilon)
    second_ref[...] = (resid * scale * gain).astype(low)


def route_kernel(me_ref, *refs):
    me, limit = me_ref[1], me_ref[2].astype(wide)
    mine = me.astype(wide)
    sent, (dispatch_ref, partner_ref, rows_ref, last_ref) = refs[:-4], refs[-4:]
    if len(sent[-1].shape) == 3:
        sent = [sent[s // 2] if s % 2 == 0 else sent[-1].at[s // 2] for s in range(8)]
    count = len(sent)
    tall = sent[0].shape[0] - 16
    i = lax.broadcasted_iota(jnp.int32, (tall, tall), 0)
    j = lax.broadcasted_iota(jnp.int32, (tall, tall), 1)
    before = (i < j).astype(low)
    slots = lax.broadcasted_iota(jnp.int32, (CAP, tall), 0).astype(wide)
    named = [sent[s][tall:, :tall].astype(wide) for s in range(count)]

    def one_hots(expert, limit, wanted):
        mine = expert.astype(wide)
        hits = jnp.concatenate([((r[0:1] == mine) | (r[1:2] == mine)).astype(wide) for r in named], axis=0)
        within = matmul(hits.astype(low), before)
        counts = jnp.sum(hits, axis=1, keepdims=True)
        index = me ^ lax.broadcasted_iota(jnp.int32, (count, 1), 0)
        for s in wanted:
            base = jnp.sum(jnp.where(index < (me ^ s), counts, 0.0), axis=0, keepdims=True)
            rank = within[s : s + 1] + base
            slot = jnp.where((hits[s : s + 1] > 0) & (rank < limit), rank, -1.0)
            yield s, (slots == slot).astype(low)

    packed = jnp.zeros((CAP, rows_ref.shape[1]), wide)
    other = jnp.zeros((16, CAP), wide)
    mine = me.astype(wide)
    for s, one_hot in one_hots(me, limit, range(count)):
        dispatch_ref[:, s * tall : (s + 1) * tall] = one_hot
        packed = packed + matmul(one_hot, sent[s][:tall, :])
        name = jnp.where(named[s][0:1] == mine, named[s][1:2], named[s][0:1])
        other = other + along_last(jnp.broadcast_to(name, (16, tall)).astype(low), one_hot)
    half = rows_ref.shape[0]
    rows_ref[...] = packed[:half].astype(low)
    last_ref[: CAP - half, :] = packed[half:].astype(low)
    tail = jnp.zeros((16, rows_ref.shape[1] - CAP), low)
    last_ref[CAP - half :, :] = jnp.concatenate([other.astype(low), tail], axis=1)
    for s, one_hot in one_hots(me ^ 1, named[1][2:3] * BLOCK, range(0, count, 2)):
        partner_ref[:, s // 2 * tall : (s // 2 + 1) * tall] = one_hot


def upstream_kernel(me_ref, weight_ref, *refs):
    rows, backs, choices = refs[: 2 * SHARDS], refs[2 * SHARDS : 3 * SHARDS], refs[3 * SHARDS :]
    half = rows[0].shape[0]
    mine = me_ref[1].astype(wide)
    i = lax.broadcasted_iota(jnp.int32, (CAP, CAP), 0)
    j = lax.broadcasted_iota(jnp.int32, (CAP, CAP), 1)
    lane = lax.broadcasted_iota(jnp.int32, (CAP, LANES), 1).astype(wide)
    for k in range(SHARDS):
        backs[k][:half, :] = along_last(rows[2 * k][...], weight_ref[...])
        backs[k][half:, :] = along_last(rows[2 * k + 1][: CAP - half, :], weight_ref[...])
        across = rows[2 * k + 1][CAP - half :, :CAP].astype(wide)[0:1]
        other = jnp.sum(jnp.where(i == j, across, 0.0), axis=1, keepdims=True)
        choices[k][...] = (lane == mine).astype(wide) - (lane == other).astype(wide)


def pack_kernel(me_ref, dispatch_ref, *refs):
    rows, out_ref = refs[:-1], refs[-1]
    tall = rows[0].shape[0]
    total = jnp.zeros(out_ref.shape, wide)
    for s, ref in enumerate(rows):
        total = total + matmul(dispatch_ref[:, s * tall : (s + 1) * tall], ref[...])
    out_ref[...] = total.astype(low)


def expert_kernel(me_ref, back_a, back_b, choice_a, choice_b, weight_ref, router_ref, *refs):
    rows, outs, (act_ref, back_pre_ref, logits_ref) = refs[:2], refs[2:4], refs[4:]
    for k in range(2):
        here = slice(k * CAP, (k + 1) * CAP)
        block = rows[k][...]
        choice = (choice_a, choice_b)[k][...]
        back = (back_a, back_b)[k][...]
        chosen = jnp.sum(along_last(block, router_ref[...]) * choice, axis=1, keepdims=True)
        gate = jax.nn.sigmoid(chosen)
        pre = along_last(block, weight_ref[...])
        square = pre * pre
        slope = math.sqrt(2 / math.pi)
        bent = jnp.tanh(slope * pre * (1.0 + 0.044715 * square))
        half = 0.5 * (1.0 + bent)
        act = pre * half
        steep = half + 0.5 * pre * (1.0 - bent * bent) * (slope * (1.0 + 3 * 0.044715 * square))
        act_ref[here, :] = (act * gate).astype(low)
        back_pre = (steep * (back * gate)).astype(low)
        back_pre_ref[here, :] = back_pre
        back_gate = jnp.sum(act * back, axis=1, keepdims=True)
        logits = (gate * jax.nn.sigmoid(-chosen) * back_gate * choice).astype(low)
        logits_ref[here, :] = logits
        outs[k][...] = (matmul(back_pre, weight_ref[...]) + matmul(logits, router_ref[...])).astype(low)


def result_kernel(order, me_ref, weight_ref, act_a, act_b, logits_a, logits_b, *refs):
    rows, (own_ref, across_ref, pair_ref, router_ref) = refs[:SHARDS], refs[SHARDS:]
    router = jnp.zeros(router_ref.shape, wide)
    for k, s in enumerate(order):
        here = slice((k % 2) * CAP, (k % 2 + 1) * CAP)
        result = matmul((act_a, act_b)[k // 2][here, :], weight_ref[...]).astype(low)
        if s % 2 == 0:
            (own_ref, across_ref)[s // 2][...] = result
        else:
            pair_ref[(3 - s) // 2] = result
        router = router + along_first(rows[s][...], (logits_a, logits_b)[k // 2][here, :])
    router_ref[...] = router


def layer_kernel(me_ref, resid_ref, *refs):
    refs[-1][...] = (resid_ref[...] + total_of(refs[:-1])).astype(low)


def grads_kernel(order, me_ref, *refs):
    acts, pres = refs[0:2], refs[2:4]
    rows, ups = refs[4 : 4 + SHARDS], refs[4 + SHARDS : 4 + 3 * SHARDS]
    first_ref, second_ref = refs[4 + 3 * SHARDS :]
    acts = jnp.concatenate([ref[...] for ref in acts], axis=0)
    pres = jnp.concatenate([ref[...] for ref in pres], axis=0)
    block = jnp.concatenate([rows[s][...] for s in order], axis=0)
    first_ref[0] = along_first(pres, block)
    half = CAP - ups[0].shape[0]
    ups = jnp.concatenate([ref[...] for s in order for ref in (ups[2 * s], ups[2 * s + 1].at[:half])], axis=0)
    second_ref[0] = along_first(acts, ups)


def unpack_kernel(me_ref, dispatch_ref, *refs):
    terms, outs = refs[:3], refs[3:]
    block = total_of(terms).astype(low)
    tall = outs[0].shape[0]
    for s, ref in enumerate(outs):
        ref[...] = along_first(dispatch_ref[:, s * tall : (s + 1) * tall], block).astype(low)


def total_kernel(me_ref, *refs):
    refs[-1][...] = total_of(refs[:-1]).astype(low)


def unpack_both_kernel(me_ref, dispatch_ref, partner_ref, block_ref, other_ref, *outs):
    tall = outs[0].shape[0]
    for k, ref in enumerate(outs):
        own = along_first(dispatch_ref[:, 2 * k * tall : (2 * k + 1) * tall], block_ref[...])
        other = along_first(partner_ref[:, k * tall : (k + 1) * tall], other_ref[...])
        ref[...] = (own + other).astype(low)


def resid_back_kernel(me_ref, resid_ref, small_ref, cotangent_ref, *refs):
    terms, (back_ref, branch_ref, gain_ref) = refs[:-3], refs[-3:]
    experts = experts_of(small_ref.shape[0])
    gain = small_ref[experts + 1 : experts + 2, :].astype(wide)
    resid = resid_ref[...]
    upstream = total_of(terms)
    r = lax.rsqrt(jnp.mean(resid * resid, axis=-1, keepdims=True) + epsilon)
    gain_ref[...] = jnp.sum(upstream * (resid * r), axis=0, keepdims=True)
    m = upstream * gain
    back = r * m - (r * r * r) * resid * jnp.mean(m * resid, axis=-1, keepdims=True)
    back = back + cotangent_ref[...].astype(wide)
    back_ref[...] = back
    branch_ref[...] = back.astype(low)


def attend_back_kernel(
    experts,
    table_rows,
    me_ref,
    out_ref,
    qkv_ref,
    probs_ref,
    weight_ref,
    tokens_ref,
    first_ref,
    att_ref,
    gain_two_ref,
    router_ref,
    *refs,
):
    ups, backs = refs[:SHARDS], refs[SHARDS : SHARDS + 3]
    parts, (held, table) = refs[SHARDS + 3 : -2], refs[-2:]
    me = me_ref[0]
    shard = out_ref.shape[0]
    chunk, width = ups[0].shape
    length = chunk * SHARDS
    heads = probs_ref.shape[0]
    span = heads * HEAD_DIM
    scale = HEAD_DIM**-0.5
    for s in range(SHARDS):
        held[me ^ s] = ups[s][...]
    up = held[...].reshape(length, width)
    back = along_last(up, out_ref[...]).astype(low)
    qkv = qkv_ref[...]
    dq, dk, dv = [], [], []
    i = lax.broadcasted_iota(jnp.int32, (chunk, chunk), 0)
    j = lax.broadcasted_iota(jnp.int32, (chunk, chunk), 1)
    reverse = (i + j == chunk - 1).astype(low)
    diagonals = []
    for h in range(heads):
        q = qkv[:, h * HEAD_DIM : (h + 1) * HEAD_DIM]
        k = qkv[:, span + h * HEAD_DIM : span + (h + 1) * HEAD_DIM]
        v = qkv[:, 2 * span + h * HEAD_DIM : 2 * span + (h + 1) * HEAD_DIM]
        d = back[:, h * HEAD_DIM : (h + 1) * HEAD_DIM]
        probs_low = probs_ref[h]
        probs = probs_low.astype(wide)
        back_probs = along_last(d, v)
        inner = jnp.sum(back_probs * probs, axis=-1, keepdims=True)
        scores = (probs * (back_probs - inner)).astype(low)
        diagonal = jnp.zeros((1, length), wide)
        for b in range(SHARDS):
            turned = matmul(reverse, scores[b * chunk : (b + 1) * chunk])
            start = (1 - (b + 1) * chunk) % length
            turned = pltpu.roll(turned, start, 1, stride=1, stride_axis=0)
            diagonal = diagonal + jnp.sum(turned, axis=0, keepdims=True)
        diagonals.append(diagonal)
        dq.append((matmul(scores, k) * scale).astype(low))
        dk.append((along_first(scores, q) * scale).astype(low))
        dv.append(along_first(probs_low, d).astype(low))
    dqkv = jnp.concatenate(dq + dk + dv, axis=1)
    back_first = along_last(dqkv, weight_ref[...])
    rows = tokens_ref[...].reshape(length, width).astype(wide)
    rows = rows * lax.rsqrt(jnp.mean(rows * rows, axis=-1, keepdims=True) + epsilon)
    for w in range(SHARDS):
        held[w] = back_first[w * chunk : (w + 1) * chunk].astype(low)
    store_w(backs, held, me)

    gains = [jnp.sum(back_first * rows, axis=0, keepdims=True), gain_two_ref[...]]
    gains = jnp.concatenate(gains + [jnp.zeros((14, width), wide)], axis=0).astype(low)
    i = lax.broadcasted_iota(jnp.int32, (LANES, LANES), 0)
    j = lax.broadcasted_iota(jnp.int32, (LANES, LANES), 1)
    extra = along_first(gains, (i[:16] == j[:16]).astype(low))
    extra = extra + matmul(router_ref[...].astype(low), (i + 2 == j).astype(low))
    above = jnp.zeros((2 + experts, length), wide)
    below = jnp.zeros((LANES - 2 - experts - heads, length), wide)
    spread = jnp.concatenate([above] + diagonals + [below], axis=0)
    shift = lax.broadcasted_iota(jnp.int32, (length, width), 0)
    lane = lax.broadcasted_iota(jnp.int32, (length, width), 1)
    bucket = bucket_of(jnp.where(shift > 0, length - shift, 0))
    hits = (lane == (bucket // table_rows) * shard + bucket % table_rows).astype(low)
    spread_low = spread.astype(low)
    rest = (spread - spread_low.astype(wide)).astype(low)
    turn = (((0,), (1,)), ((), ()))
    extra = extra + lax.dot_general(hits, spread_low, turn, preferred_element_type=wide)
    extra = extra + lax.dot_general(hits, rest, turn, preferred_element_type=wide)
    output = along_first(att_ref[...], up)
    output = jnp.concatenate([output[:, w * shard : (w + 1) * shard] for w in range(SHARDS)], axis=0)
    grads = jnp.concatenate([along_first(first_ref[...], dqkv), extra, output], axis=1)
    if len(parts) == 1:
        parts[0][...] = grads.astype(low)
    else:
        table[...] = grads
        piece = parts[0].shape[1]
        for s, ref in enumerate(parts):
            for w in range(SHARDS):
                start = pl.multiple_of(w * shard + (me_ref[1] ^ s) * piece, 8)
                ref[w] = table[pl.ds(start, piece), :].astype(low)


def join_kernel(me_ref, *refs):
    terms, outs, output_ref, held = refs[:5], refs[5 : 5 + SHARDS], refs[5 + SHARDS], refs[6 + SHARDS]
    total = total_of(terms)
    columns = outs[0].shape[1]
    held[...] = total[:, :, :columns]
    for s in range(SHARDS):
        outs[s][...] = held[me_ref[0] ^ s].astype(low)
    output_ref[...] = jnp.concatenate([total[w][:, columns:] for w in range(SHARDS)], axis=1).astype(low)


def order_kernel(experts, me_ref, *refs):
    parts, output_ref, out_ref, held = refs[:SHARDS], refs[SHARDS], refs[SHARDS + 1], refs[SHARDS + 2]
    for s in range(SHARDS):
        held[me_ref[0] ^ s] = parts[s][...].astype(wide)
    own = HEADS // SHARDS
    span = own * HEAD_DIM
    blocks = [held[w] for w in range(SHARDS)]
    pieces = [blocks[w][:, k * span : (k + 1) * span] for k in range(3) for w in range(SHARDS)]
    lane = lax.broadcasted_iota(jnp.int32, (parts[0].shape[0], LANES), 1)
    extra = jnp.zeros((parts[0].shape[0], LANES), wide)
    for w in range(SHARDS):
        small = blocks[w][:, 3 * span :]
        heads = jnp.where((lane >= 2 + experts) & (lane < 2 + experts + own), small, 0.0)
        extra = extra + jnp.where(lane < 2 + experts, small, 0.0) + pltpu.roll(heads, own * w, 1)
    pieces = pieces + [output_ref[...].astype(wide), extra]
    out_ref[...] = jnp.concatenate(pieces, axis=1).astype(low)


def final_kernel(me_ref, *refs):
    parts, outs = refs[:-9], refs[-9:-1]
    held = refs[-1]
    piece = parts[0].shape[0]
    width = outs[0].shape[1]
    experts = outs[6].shape[1]
    for s, ref in enumerate(parts):
        here = pl.ds(pl.multiple_of((me_ref[1] ^ s) * piece, 8), piece)
        block = ref[...].astype(wide)
        for k in range(4):
            outs[k][here, :] = block[:, k * width : (k + 1) * width]
        held[here, :] = block[:, 4 * width :]
    extra = held[...]
    shard = extra.shape[0]
    i = lax.broadcasted_iota(jnp.int32, (shard, shard), 0)
    j = lax.broadcasted_iota(jnp.int32, (shard, shard), 1)
    turned = along_first(extra.astype(low), (i == j).astype(low))
    outs[4][...] = turned[0:1]
    outs[5][...] = turned[1:2]
    outs[6][...] = extra[:, 2 : 2 + experts]
    outs[7][...] = extra[: outs[7].shape[0], 2 + experts : 2 + experts + HEADS]


def tokens_back_kernel(me_ref, tokens_ref, small_ref, resid_ref, *refs):
    terms, out_ref = refs[:-1], refs[-1]
    experts = experts_of(small_ref.shape[0])
    gain = small_ref[experts : experts + 1, :].astype(wide)
    rows = tokens_ref[...].astype(wide)
    r = lax.rsqrt(jnp.mean(rows * rows, axis=-1, keepdims=True) + epsilon)
    m = total_of(terms) * gain
    back = r * m - (r * r * r) * rows * jnp.mean(m * rows, axis=-1, keepdims=True)
    out_ref[...] = resid_ref[...] + back


def local(
    tokens,
    segments,
    routes,
    blocks,
    attention_gain,
    query_weight,
    key_weight,
    value_weight,
    output_weight,
    position_bias,
    feed_gain,
    router_weight,
    expert_in,
    expert_out,
    cotangent,
):
    rows, width = tokens.shape
    length = rows * SHARDS
    experts = lax.axis_size(E)
    me_w = lax.axis_index(W)
    me_e = lax.axis_index(E)
    me = jnp.stack([me_w, me_e, blocks[0] * BLOCK]).astype(jnp.int32)
    shard = query_weight.shape[0]
    own_heads = HEADS // SHARDS
    table_rows = position_bias.shape[0]
    first_local, second_local = expert_in[0], expert_out[0]
    row = (rows, width)
    packed_row = (CAP, width)
    three_rows = [(row, low), (row, low), ((2,) + row, low)]

    quick = experts == 8
    small_rows = -(-(experts + 2 + HEADS) // 16) * 16
    tokens_rel = gather_w(tokens)
    weight_rel = exchange_w(
        call(
            start_kernel,
            [((shard + small_rows, 3 * shard), low)] * SHARDS,
            [((SHARDS, shard, 3 * shard), low)],
            me,
            query_weight,
            key_weight,
            value_weight,
            router_weight.T,
            attention_gain,
            feed_gain,
            position_bias,
            room=FULL,
        )
    )
    (sent,) = call(
        sent_kernel,
        [((rows + 16, width), low)],
        [],
        me,
        cotangent,
        routes.T,
    )
    sent = [sent, swap(sent, E, 2), swap(sent, E, 4), swap(sent, E, 6)] if quick else gather_e(sent)

    square = (own_heads, length, length)
    outs = call(
        attend_kernel,
        [
            ((SHARDS, rows, width), low),
            ((length, width), low),
            ((length, 3 * shard), low),
            (square, low),
            ((length, shard), low),
            ((width, 3 * shard), low),
            ((small_rows, width), low),
            ((LANES, width), low),
        ],
        [((SHARDS, shard + small_rows, 3 * shard), low)],
        me,
        *tokens_rel,
        *weight_rel,
        segments,
        room=FULL,
        cover=20,
    )
    tokens_all, first, qkv, probs, attended, weight, small, router = outs
    near_sent = sent if quick else sent[:4]
    *branches, stacked = call(
        branch_kernel,
        three_rows + [((len(near_sent), rows + 16, width), low)],
        [((SHARDS, rows, width), low)],
        me,
        attended,
        output_weight,
        *near_sent,
    )
    branch_terms, _ = sum_w(*branches)
    resid, second = call(
        second_kernel,
        [(row, wide), (row, low)],
        [],
        me,
        tokens,
        small,
        *branch_terms,
    )

    second_rel = gather_e(second)

    if quick:
        sent.append(swap(stacked, E, 1))
    dispatch, partner, *upstream_rows = call(
        route_kernel,
        [
            ((CAP, experts * rows), low),
            ((CAP, experts * rows // 2), low),
            ((CAP // 2, width), low),
            ((CAP // 2 + 16, width), low),
        ],
        [],
        me,
        *sent,
        after=(second,),
    )
    upstream_rel = list(zip(gather_w(upstream_rows[0]), gather_w(upstream_rows[1])))
    order = (0, 1, 2, 3)
    outs = call(
        upstream_kernel,
        [(packed_row, wide)] * SHARDS + [((CAP, LANES), wide)] * SHARDS,
        [],
        me,
        second_local,
        *[piece for s in order for piece in upstream_rel[s]],
    )
    back_act, choice = outs[:SHARDS], outs[SHARDS:]

    (packed,) = call(
        pack_kernel,
        [(packed_row, low)],
        [],
        me,
        dispatch,
        *second_rel,
        after=upstream_rel[2],
    )
    half = (2 * CAP, width)

    def expert_half(k, after):
        return call(
            expert_kernel,
            [(packed_row, low)] * 2 + [(half, low), (half, low), ((2 * CAP, LANES), low)],
            [],
            me,
            back_act[2 * k],
            back_act[2 * k + 1],
            choice[2 * k],
            choice[2 * k + 1],
            first_local,
            router,
            rows_rel[order[2 * k]],
            rows_rel[order[2 * k + 1]],
            after=after,
        )

    far = swap(packed, W, 2)
    rows_rel = [packed, swap(packed, W, 1)]
    halves = [expert_half(0, ())]
    far = tie(far, halves[0][0])
    rows_rel = rows_rel + [far, swap(far, W, 1)]
    halves.append(expert_half(1, ()))
    near = swap(halves[1][1], W, 1)
    across = (halves[1][0].astype(wide) + near.astype(wide)).astype(low)
    back_parts = call(
        unpack_kernel,
        [(row, low)] * experts,
        [],
        me,
        dispatch,
        halves[0][0],
        swap(halves[0][1], W, 1),
        swap(across, W, 2),
    )
    back_terms = sum_e(back_parts)

    *results, router_grad = call(
        lambda *refs: result_kernel(order, *refs),
        [(packed_row, low), (packed_row, low), ((2,) + packed_row, low), ((width, LANES), wide)],
        [],
        me,
        second_local,
        halves[0][2],
        halves[1][2],
        halves[0][4],
        halves[1][4],
        *rows_rel,
        after=(across,),
    )
    result_terms, _ = sum_w(*results)
    if quick:
        (mixed,) = call(total_kernel, [(packed_row, low)], [], me, *result_terms)
        mixed_parts = call(
            unpack_both_kernel, [(row, low)] * 4, [], me, dispatch, partner, mixed, swap(mixed, E, 1)
        )
        mixed_terms = [mixed_parts[0]] + [swap(mixed_parts[s // 2], E, s) for s in (4, 6, 2)]
    else:
        mixed_parts = call(unpack_kernel, [(row, low)] * experts, [], me, dispatch, *result_terms)
        mixed_terms = sum_e(mixed_parts)

    back_resid, back_branch, gain_two_grad = call(
        resid_back_kernel,
        [(row, wide), (row, low), ((1, width), wide)],
        [],
        me,
        resid,
        small,
        cotangent,
        *back_terms,
        after=(mixed_parts[0],),
    )
    back_rel = gather_w(back_branch)
    columns = 3 * shard + LANES
    piece = shard // experts
    part = (SHARDS, piece, columns + shard)
    outs = call(
        lambda *refs: attend_back_kernel(experts, table_rows, *refs),
        three_rows
        + ([(part, low)] * experts if quick else [((width, columns + shard), low)]),
        [((SHARDS, rows, width), low), ((width, columns + shard), wide)],
        me,
        output_weight,
        qkv,
        probs,
        weight,
        tokens_all,
        first,
        attended,
        gain_two_grad,
        router_grad,
        *back_rel,
        cover=20,
    )
    grads = list(outs[3:])
    (layer_out,) = call(layer_kernel, [(row, low)], [], me, resid, *mixed_terms, after=(grads[0],))
    if quick:
        grads[5] = tie(grads[5], layer_out)
    back_terms, _ = sum_w(*outs[:3])
    (tokens_grad,) = call(
        tokens_back_kernel,
        [(row, wide)],
        [],
        me,
        tokens,
        small,
        back_resid,
        *back_terms,
    )

    first_grad, second_grad = call(
        lambda *refs: grads_kernel(order, *refs),
        [((1,) + first_local.shape, wide), ((1,) + second_local.shape, wide)],
        [],
        me,
        halves[0][2],
        halves[1][2],
        halves[0][3],
        halves[1][3],
        *rows_rel,
        *[piece for pieces in upstream_rel for piece in pieces],
        after=(grads[-1],),
    )

    if quick:
        terms = sum_e(grads)
        *grads, output_grad = call(
            join_kernel,
            [((piece, columns), low)] * SHARDS + [((piece, width), low)],
            [((SHARDS, piece, columns), wide)],
            me,
            *terms,
        )
        (grads,) = call(
            lambda *refs: order_kernel(experts, *refs),
            [((piece, 4 * width + LANES), low)],
            [((SHARDS, piece, columns), wide)],
            me,
            *exchange_w(grads),
            output_grad,
        )
        shape = (shard, width)
        outs = call(
            final_kernel,
            [(shape, wide)] * 4
            + [((1, shard), wide)] * 2
            + [((shard, experts), wide), ((table_rows, HEADS), wide)],
            [((shard, LANES), wide)],
            me,
            *gather_e(grads),
        )
        query_grad, key_grad, value_grad, output_grad = outs[:4]
        gain_one_grad, gain_two_grad = outs[4].reshape(shard), outs[5].reshape(shard)
        router_grad, table_grad = outs[6], outs[7]
    else:
        grads = lax.psum(grads[0], E).astype(wide).reshape(SHARDS, shard, columns + shard)
        output_grad = grads[:, :, columns:].transpose(1, 0, 2).reshape(shard, width)
        grads = grads[:, :, :columns].astype(low)
        grads = place(
            exchange_w([lax.dynamic_index_in_dim(grads, me_w ^ s, 0, False) for s in range(SHARDS)]), me_w
        ).astype(wide)
        main = grads[:, :, : 3 * shard].reshape(SHARDS, shard, 3, shard).transpose(2, 1, 0, 3)
        query_grad, key_grad, value_grad = main.reshape(3, shard, width)
        extra = grads[:, :, 3 * shard :]
        summed = jnp.sum(extra[:, :, : 2 + experts], axis=0)
        gain_one_grad, gain_two_grad, router_grad = summed[:, 0], summed[:, 1], summed[:, 2:]
        table_grad = extra[:, :table_rows, 2 + experts : 2 + experts + own_heads]
        table_grad = table_grad.transpose(1, 0, 2).reshape(table_rows, HEADS)
    return (
        layer_out,
        tokens_grad,
        gain_one_grad,
        query_grad,
        key_grad,
        value_grad,
        output_grad,
        table_grad,
        gain_two_grad,
        router_grad,
        first_grad,
        second_grad,
    )


def solution(mesh):
    in_specs = (
        P(("expert", "wshard"), None),
        P("expert", None),
        P(("expert", "wshard"), None),
        P("expert"),
        P("wshard"),
        P("wshard", None),
        P("wshard", None),
        P("wshard", None),
        P("wshard", None),
        P("wshard", None),
        P("wshard"),
        P("wshard", None),
        P("expert", "wshard", None),
        P("expert", "wshard", None),
        P(("expert", "wshard"), None),
    )
    out_specs = (
        P(("expert", "wshard"), None),
        P(("expert", "wshard"), None),
        P("wshard"),
        P("wshard", None),
        P("wshard", None),
        P("wshard", None),
        P("wshard", None),
        P("wshard", None),
        P("wshard"),
        P("wshard", None),
        P("expert", "wshard", None),
        P("expert", "wshard", None),
    )
    return jax.shard_map(local, mesh=mesh, in_specs=in_specs, out_specs=out_specs, check_vma=False)
```

```python
import math

import jax
import jax.numpy as jnp
from jax import lax
from jax.experimental import pallas as pl
from jax.experimental.pallas import tpu as pltpu
from jax.sharding import PartitionSpec as P

HEADS = 12
HEAD_DIM = 64
BUCKETS = 32
BLOCK = 128
MOST_BLOCKS = 2
SHARDS = 4
LANES = 128
CAP = MOST_BLOCKS * BLOCK
W = "wshard"
E = "expert"

epsilon = 1e-06
thresholds = tuple((math.ceil(16 * 2 ** (3 * order / 16)) for order in range(1, 16)))
low = jnp.bfloat16
wide = jnp.float32
FULL = 60 << 20


def bucket_of(distance):
    passed = jnp.zeros_like(distance)
    for edge in thresholds:
        passed = passed + (distance >= edge).astype(jnp.int32)
    return jnp.where(distance < 16, distance, 16 + passed)


def along_last(left, right):
    return lax.dot_general(left, right, (((1,), (1,)), ((), ())), preferred_element_type=wide)


def along_first(left, right):
    return lax.dot_general(left, right, (((0,), (0,)), ((), ())), preferred_element_type=wide)


def matmul(left, right):
    return jnp.dot(left, right, preferred_element_type=wide)


def swap(value, axis, step):
    count = lax.axis_size(axis)
    return lax.ppermute(value, axis, [(i, i ^ step) for i in range(count)])


def gather_w(value):
    far = swap(value, W, 2)
    near = swap(value, W, 1)
    return [value, near, far, swap(far, W, 1)]


def sum_w(own, across, pair):
    got = swap(pair, W, 1)
    across = (across.astype(wide) + got[0].astype(wide)).astype(low)
    return [own, got, swap(across, W, 2)], across


def exchange_w(parts):
    return [parts[0]] + [swap(parts[s], W, s) for s in (1, 2, 3)]


def place(parts, me):
    out = jnp.zeros((len(parts),) + parts[0].shape, parts[0].dtype)
    for s, part in enumerate(parts):
        out = lax.dynamic_update_index_in_dim(out, part, me ^ s, 0)
    return out


def gather_e(value):
    count = lax.axis_size(E)
    if count > 8:
        whole = lax.all_gather(value, E, axis=0)
        me = lax.axis_index(E)
        order = me ^ jnp.arange(count, dtype=jnp.int32)
        whole = whole[order]
        return [whole[s] for s in range(count)]
    out = {0: value}
    for s in (4, 6, 2):
        out[s] = swap(value, E, s)
    for s in (0, 4, 6, 2):
        out[s ^ 1] = swap(out[s], E, 1)
    return [out[s] for s in range(8)]


def sum_e(parts):
    count = lax.axis_size(E)
    if count > 8:
        me = lax.axis_index(E)
        whole = jnp.stack(parts)[me ^ jnp.arange(count, dtype=jnp.int32)]
        return [lax.psum_scatter(whole, E, scatter_dimension=0)]
    got = {s: swap(parts[s ^ 1], E, 1) for s in (4, 6, 2)}
    terms = [parts[0], swap(tie(parts[1], got[4]), E, 1)]
    for s in (4, 6, 2):
        part = (parts[s].astype(wide) + got[s].astype(wide)).astype(low)
        terms.append(swap(part, E, s))
    return terms


def experts_of(small_rows):
    return {32: 8, 80: 64}[small_rows]


def total_of(refs):
    rank = len(refs[0].shape)
    out = refs[0][...].astype(wide)
    for ref in refs[1:]:
        out = out + (ref[...] if len(ref.shape) == rank else ref[1]).astype(wide)
    return out


def store_w(outs, held, me):
    outs[0][...] = held[me]
    outs[1][...] = held[me ^ 2]
    outs[2][0] = held[me ^ 3]
    outs[2][1] = held[me ^ 1]


def call(kernel, outs, scratch, scalars, *args, after=(), room=None, cover=0):
    outs, scratch, after = tuple(outs), tuple(scratch), tuple(after)
    smem = pl.BlockSpec(memory_space=pltpu.SMEM)
    block = pl.BlockSpec()
    apart = pl.BlockSpec(memory_space=pl.ANY)
    size = sum(a.size * a.dtype.itemsize for a in args)
    size = size + sum(math.prod(s) * jnp.dtype(d).itemsize for s, d in outs + scratch)
    skip = len(after)
    return pl.pallas_call(
        lambda *refs: kernel(*refs[skip:]),
        out_shape=tuple(jax.ShapeDtypeStruct(s, d) for s, d in outs),
        in_specs=[apart] * skip + [smem] + [block] * len(args),
        out_specs=tuple(block for _ in outs),
        scratch_shapes=[pltpu.VMEM(s, d) for s, d in scratch],
        compiler_params=pltpu.CompilerParams(vmem_limit_bytes=room or (10 << 20) + size),
        cost_estimate=pl.CostEstimate(flops=1 + cover * 10**9, bytes_accessed=1, transcendentals=0),
    )(*after, scalars, *args)


def tie(value, *after):
    apart = pl.BlockSpec(memory_space=pl.ANY)
    return pl.pallas_call(
        lambda *refs: None,
        out_shape=jax.ShapeDtypeStruct(value.shape, value.dtype),
        in_specs=[apart] * (1 + len(after)),
        out_specs=apart,
        input_output_aliases={0: 0},
        compiler_params=pltpu.CompilerParams(vmem_limit_bytes=1 << 20),
        cost_estimate=pl.CostEstimate(flops=1, bytes_accessed=1, transcendentals=0),
    )(value, *after)


def start_kernel(me_ref, q_ref, k_ref, v_ref, router_ref, one_ref, two_ref, table_ref, *rest):
    outs, held = rest[:SHARDS], rest[SHARDS]
    shard = q_ref.shape[0]
    for w in range(SHARDS):
        here = slice(w * shard, (w + 1) * shard)
        held[w] = jnp.concatenate([q_ref[:, here], k_ref[:, here], v_ref[:, here]], axis=1)
    i = lax.broadcasted_iota(jnp.int32, (table_ref.shape[0], shard), 0)
    j = lax.broadcasted_iota(jnp.int32, (table_ref.shape[0], shard), 1)
    small = [
        router_ref[...],
        one_ref[...].reshape(1, shard),
        two_ref[...].reshape(1, shard),
        along_first(table_ref[...], (i == j).astype(low)).astype(low),
    ]
    used = sum(piece.shape[0] for piece in small)
    small = jnp.concatenate(small + [jnp.zeros((outs[0].shape[0] - shard - used, shard), low)], axis=0)
    small = jnp.concatenate([small, jnp.zeros((small.shape[0], 2 * shard), low)], axis=1)
    for s in range(SHARDS):
        outs[s][:shard, :] = held[me_ref[0] ^ s]
        outs[s][shard:, :] = small


def sent_kernel(me_ref, up_ref, routes_ref, sent_ref):
    rows, width = up_ref.shape
    sent_ref[:rows, :] = up_ref[...]
    blocks = jnp.full((1, rows), me_ref[2].astype(wide) / BLOCK).astype(low)
    named = jnp.concatenate([routes_ref[...].astype(low), blocks, jnp.zeros((13, rows), low)], axis=0)
    sent_ref[rows:, :] = jnp.concatenate([named, jnp.zeros((16, width - rows), low)], axis=1)


def attend_kernel(me_ref, *refs):
    tokens, weights = refs[:SHARDS], refs[SHARDS : 2 * SHARDS]
    row_ref, *rest = refs[2 * SHARDS :]
    tokens_ref, first_ref, qkv_ref, probs_ref, att_ref, weight_ref, small_ref, router_ref, held_w = rest
    me = me_ref[0]
    shard = att_ref.shape[1]
    chunk, width = tokens[0].shape
    length = chunk * SHARDS
    heads = probs_ref.shape[0]
    span = heads * HEAD_DIM
    for s in range(SHARDS):
        tokens_ref[me ^ s] = tokens[s][...]
        held_w[me ^ s] = weights[s][...]
    for w in range(SHARDS):
        weight_ref[w * shard : (w + 1) * shard, :] = held_w[w, :shard, :]
    small = jnp.concatenate([held_w[w, shard:, :shard] for w in range(SHARDS)], axis=1)
    small_ref[...] = small
    experts = experts_of(small_ref.shape[0])
    router_ref[...] = jnp.zeros_like(router_ref)
    router_ref[:experts, :] = small[:experts]
    gain_one = small[experts : experts + 1].astype(wide)

    shift = lax.broadcasted_iota(jnp.int32, (length, width), 0)
    lane = lax.broadcasted_iota(jnp.int32, (length, width), 1)
    bucket = bucket_of(jnp.where(shift > 0, length - shift, 0))
    per = BUCKETS // SHARDS
    hits = (lane == (bucket // per) * shard + bucket % per).astype(low)
    vectors = along_last(small[experts + 2 : experts + 2 + HEADS], hits)
    i = lax.broadcasted_iota(jnp.int32, (length, length), 0)
    j = lax.broadcasted_iota(jnp.int32, (length, length), 1)
    marks = jnp.broadcast_to(row_ref[...], (length, length))
    column = jnp.sum(jnp.where(i == j, marks, 0), axis=1, keepdims=True)
    allowed = (j <= i) & (marks == column)
    which = lax.broadcasted_iota(jnp.int32, vectors.shape, 0)

    rows = tokens_ref[...].reshape(length, width).astype(wide)
    scale = lax.rsqrt(jnp.mean(rows * rows, axis=-1, keepdims=True) + epsilon)
    first = (rows * scale * gain_one).astype(low)
    first_ref[...] = first
    qkv = matmul(first, weight_ref[...]).astype(low)
    qkv_ref[...] = qkv
    columns = []
    for h in range(heads):
        vector = jnp.sum(jnp.where(which == me * heads + h, vectors, 0.0), axis=0, keepdims=True)
        bias = pltpu.roll(jnp.broadcast_to(vector, (length, length)), 0, 1, stride=1, stride_axis=0)
        bias = jnp.where(allowed, bias, -1e30)
        q = qkv[:, h * HEAD_DIM : (h + 1) * HEAD_DIM] * (HEAD_DIM**-0.5)
        k = qkv[:, span + h * HEAD_DIM : span + (h + 1) * HEAD_DIM]
        v = qkv[:, 2 * span + h * HEAD_DIM : 2 * span + (h + 1) * HEAD_DIM]
        pieces = []
        for b in range(SHARDS):
            end = (b + 1) * chunk
            here = slice(b * chunk, end)
            scores = along_last(q[here], k[:end]) + bias[here, :end]
            largest = jnp.max(scores, axis=-1, keepdims=True)
            grown = jnp.exp(scores - largest)
            total = jnp.sum(grown, axis=-1, keepdims=True)
            probs = (grown / total).astype(low)
            probs_ref[h, here, :end] = probs
            if end < length:
                probs_ref[h, here, end:] = jnp.zeros((chunk, length - end), low)
            pieces.append(matmul(probs, v[:end]))
        columns.append(jnp.concatenate(pieces, axis=0))
    att_ref[...] = jnp.concatenate(columns, axis=1).astype(low)


def branch_kernel(me_ref, att_ref, out_ref, *refs):
    sent, branches, held = refs[:-5], refs[-5:-2], refs[-1]
    chunk = held.shape[1]
    for k, ref in enumerate(sent):
        refs[-2][k] = ref[...]
    branch = matmul(att_ref[...], out_ref[...]).astype(low)
    for w in range(SHARDS):
        held[w] = branch[w * chunk : (w + 1) * chunk]
    store_w(branches, held, me_ref[0])


def second_kernel(me_ref, tokens_ref, small_ref, *refs):
    terms, (resid_ref, second_ref) = refs[:-2], refs[-2:]
    experts = experts_of(small_ref.shape[0])
    gain = small_ref[experts + 1 : experts + 2, :].astype(wide)
    resid = tokens_ref[...].astype(wide) + total_of(terms)
    resid_ref[...] = resid
    scale = lax.rsqrt(jnp.mean(resid * resid, axis=-1, keepdims=True) + epsilon)
    second_ref[...] = (resid * scale * gain).astype(low)


def route_kernel(me_ref, *refs):
    me, limit = me_ref[1], me_ref[2].astype(wide)
    mine = me.astype(wide)
    sent, (dispatch_ref, partner_ref, rows_ref, last_ref) = refs[:-4], refs[-4:]
    if len(sent[-1].shape) == 3:
        sent = [sent[s // 2] if s % 2 == 0 else sent[-1].at[s // 2] for s in range(8)]
    count = len(sent)
    tall = sent[0].shape[0] - 16
    i = lax.broadcasted_iota(jnp.int32, (tall, tall), 0)
    j = lax.broadcasted_iota(jnp.int32, (tall, tall), 1)
    before = (i < j).astype(low)
    slots = lax.broadcasted_iota(jnp.int32, (CAP, tall), 0).astype(wide)
    named = [sent[s][tall:, :tall].astype(wide) for s in range(count)]

    def one_hots(expert, limit, wanted):
        mine = expert.astype(wide)
        hits = jnp.concatenate([((r[0:1] == mine) | (r[1:2] == mine)).astype(wide) for r in named], axis=0)
        within = matmul(hits.astype(low), before)
        counts = jnp.sum(hits, axis=1, keepdims=True)
        index = me ^ lax.broadcasted_iota(jnp.int32, (count, 1), 0)
        for s in wanted:
            base = jnp.sum(jnp.where(index < (me ^ s), counts, 0.0), axis=0, keepdims=True)
            rank = within[s : s + 1] + base
            slot = jnp.where((hits[s : s + 1] > 0) & (rank < limit), rank, -1.0)
            yield s, (slots == slot).astype(low)

    packed = jnp.zeros((CAP, rows_ref.shape[1]), wide)
    other = jnp.zeros((16, CAP), wide)
    mine = me.astype(wide)
    for s, one_hot in one_hots(me, limit, range(count)):
        dispatch_ref[:, s * tall : (s + 1) * tall] = one_hot
        packed = packed + matmul(one_hot, sent[s][:tall, :])
        name = jnp.where(named[s][0:1] == mine, named[s][1:2], named[s][0:1])
        other = other + along_last(jnp.broadcast_to(name, (16, tall)).astype(low), one_hot)
    half = rows_ref.shape[0]
    rows_ref[...] = packed[:half].astype(low)
    last_ref[: CAP - half, :] = packed[half:].astype(low)
    tail = jnp.zeros((16, rows_ref.shape[1] - CAP), low)
    last_ref[CAP - half :, :] = jnp.concatenate([other.astype(low), tail], axis=1)
    for s, one_hot in one_hots(me ^ 1, named[1][2:3] * BLOCK, range(0, count, 2)):
        partner_ref[:, s // 2 * tall : (s // 2 + 1) * tall] = one_hot


def upstream_kernel(me_ref, weight_ref, *refs):
    rows, backs, choices = refs[: 2 * SHARDS], refs[2 * SHARDS : 3 * SHARDS], refs[3 * SHARDS :]
    half = rows[0].shape[0]
    mine = me_ref[1].astype(wide)
    i = lax.broadcasted_iota(jnp.int32, (CAP, CAP), 0)
    j = lax.broadcasted_iota(jnp.int32, (CAP, CAP), 1)
    lane = lax.broadcasted_iota(jnp.int32, (CAP, LANES), 1).astype(wide)
    for k in range(SHARDS):
        backs[k][:half, :] = along_last(rows[2 * k][...], weight_ref[...])
        backs[k][half:, :] = along_last(rows[2 * k + 1][: CAP - half, :], weight_ref[...])
        across = rows[2 * k + 1][CAP - half :, :CAP].astype(wide)[0:1]
        other = jnp.sum(jnp.where(i == j, across, 0.0), axis=1, keepdims=True)
        choices[k][...] = (lane == mine).astype(wide) - (lane == other).astype(wide)


def pack_kernel(me_ref, dispatch_ref, *refs):
    rows, out_ref = refs[:-1], refs[-1]
    tall = rows[0].shape[0]
    total = jnp.zeros(out_ref.shape, wide)
    for s, ref in enumerate(rows):
        total = total + matmul(dispatch_ref[:, s * tall : (s + 1) * tall], ref[...])
    out_ref[...] = total.astype(low)


def expert_kernel(me_ref, back_a, back_b, choice_a, choice_b, weight_ref, router_ref, *refs):
    rows, outs, (act_ref, back_pre_ref, logits_ref) = refs[:2], refs[2:4], refs[4:]
    for k in range(2):
        here = slice(k * CAP, (k + 1) * CAP)
        block = rows[k][...]
        choice = (choice_a, choice_b)[k][...]
        back = (back_a, back_b)[k][...]
        chosen = jnp.sum(along_last(block, router_ref[...]) * choice, axis=1, keepdims=True)
        gate = jax.nn.sigmoid(chosen)
        pre = along_last(block, weight_ref[...])
        square = pre * pre
        slope = math.sqrt(2 / math.pi)
        bent = jnp.tanh(slope * pre * (1.0 + 0.044715 * square))
        half = 0.5 * (1.0 + bent)
        act = pre * half
        steep = half + 0.5 * pre * (1.0 - bent * bent) * (slope * (1.0 + 3 * 0.044715 * square))
        act_ref[here, :] = (act * gate).astype(low)
        back_pre = (steep * (back * gate)).astype(low)
        back_pre_ref[here, :] = back_pre
        back_gate = jnp.sum(act * back, axis=1, keepdims=True)
        logits = (gate * jax.nn.sigmoid(-chosen) * back_gate * choice).astype(low)
        logits_ref[here, :] = logits
        outs[k][...] = (matmul(back_pre, weight_ref[...]) + matmul(logits, router_ref[...])).astype(low)


def result_kernel(order, me_ref, weight_ref, act_a, act_b, logits_a, logits_b, *refs):
    rows, outs, router_ref = refs[:SHARDS], refs[SHARDS:-1], refs[-1]
    router = jnp.zeros(router_ref.shape, wide)
    for k, s in enumerate(order):
        here = slice((k % 2) * CAP, (k % 2 + 1) * CAP)
        outs[s][...] = matmul((act_a, act_b)[k // 2][here, :], weight_ref[...]).astype(low)
        router = router + along_first(rows[s][...], (logits_a, logits_b)[k // 2][here, :])
    router_ref[...] = router


def layer_kernel(me_ref, resid_ref, *refs):
    refs[-1][...] = (resid_ref[...] + total_of(refs[:-1])).astype(low)


def grads_kernel(order, me_ref, *refs):
    acts, pres = refs[0:2], refs[2:4]
    rows, ups = refs[4 : 4 + SHARDS], refs[4 + SHARDS : 4 + 3 * SHARDS]
    first_ref, second_ref = refs[4 + 3 * SHARDS :]
    acts = jnp.concatenate([ref[...] for ref in acts], axis=0)
    pres = jnp.concatenate([ref[...] for ref in pres], axis=0)
    block = jnp.concatenate([rows[s][...] for s in order], axis=0)
    first_ref[0] = along_first(pres, block)
    half = CAP - ups[0].shape[0]
    ups = jnp.concatenate([ref[...] for s in order for ref in (ups[2 * s], ups[2 * s + 1].at[:half])], axis=0)
    second_ref[0] = along_first(acts, ups)


def unpack_kernel(me_ref, dispatch_ref, *refs):
    terms, outs = refs[:3], refs[3:]
    block = total_of(terms).astype(low)
    tall = outs[0].shape[0]
    for s, ref in enumerate(outs):
        ref[...] = along_first(dispatch_ref[:, s * tall : (s + 1) * tall], block).astype(low)


def total_kernel(me_ref, *refs):
    refs[-1][...] = total_of(refs[:-1]).astype(low)


def unpack_both_kernel(me_ref, dispatch_ref, partner_ref, block_ref, other_ref, *outs):
    tall = outs[0].shape[0]
    for k, ref in enumerate(outs):
        own = along_first(dispatch_ref[:, 2 * k * tall : (2 * k + 1) * tall], block_ref[...])
        other = along_first(partner_ref[:, k * tall : (k + 1) * tall], other_ref[...])
        ref[...] = (own + other).astype(low)


def resid_back_kernel(me_ref, resid_ref, small_ref, cotangent_ref, *refs):
    terms, (back_ref, branch_ref, gain_ref) = refs[:-3], refs[-3:]
    experts = experts_of(small_ref.shape[0])
    gain = small_ref[experts + 1 : experts + 2, :].astype(wide)
    resid = resid_ref[...]
    upstream = total_of(terms)
    r = lax.rsqrt(jnp.mean(resid * resid, axis=-1, keepdims=True) + epsilon)
    gain_ref[...] = jnp.sum(upstream * (resid * r), axis=0, keepdims=True)
    m = upstream * gain
    back = r * m - (r * r * r) * resid * jnp.mean(m * resid, axis=-1, keepdims=True)
    back = back + cotangent_ref[...].astype(wide)
    back_ref[...] = back
    branch_ref[...] = back.astype(low)


def attend_back_kernel(
    experts,
    table_rows,
    me_ref,
    out_ref,
    qkv_ref,
    probs_ref,
    weight_ref,
    tokens_ref,
    first_ref,
    att_ref,
    gain_two_ref,
    router_ref,
    *refs,
):
    ups, backs = refs[:SHARDS], refs[SHARDS : SHARDS + 3]
    parts, (held, table) = refs[SHARDS + 3 : -2], refs[-2:]
    me = me_ref[0]
    shard = out_ref.shape[0]
    chunk, width = ups[0].shape
    length = chunk * SHARDS
    heads = probs_ref.shape[0]
    span = heads * HEAD_DIM
    scale = HEAD_DIM**-0.5
    for s in range(SHARDS):
        held[me ^ s] = ups[s][...]
    up = held[...].reshape(length, width)
    back = along_last(up, out_ref[...]).astype(low)
    qkv = qkv_ref[...]
    dq, dk, dv = [], [], []
    i = lax.broadcasted_iota(jnp.int32, (chunk, chunk), 0)
    j = lax.broadcasted_iota(jnp.int32, (chunk, chunk), 1)
    reverse = (i + j == chunk - 1).astype(low)
    diagonals = []
    for h in range(heads):
        q = qkv[:, h * HEAD_DIM : (h + 1) * HEAD_DIM]
        k = qkv[:, span + h * HEAD_DIM : span + (h + 1) * HEAD_DIM]
        v = qkv[:, 2 * span + h * HEAD_DIM : 2 * span + (h + 1) * HEAD_DIM]
        d = back[:, h * HEAD_DIM : (h + 1) * HEAD_DIM]
        probs_low = probs_ref[h]
        probs = probs_low.astype(wide)
        back_probs = along_last(d, v)
        inner = jnp.sum(back_probs * probs, axis=-1, keepdims=True)
        scores = (probs * (back_probs - inner)).astype(low)
        diagonal = jnp.zeros((1, length), wide)
        for b in range(SHARDS):
            turned = matmul(reverse, scores[b * chunk : (b + 1) * chunk])
            start = (1 - (b + 1) * chunk) % length
            turned = pltpu.roll(turned, start, 1, stride=1, stride_axis=0)
            diagonal = diagonal + jnp.sum(turned, axis=0, keepdims=True)
        diagonals.append(diagonal)
        dq.append((matmul(scores, k) * scale).astype(low))
        dk.append((along_first(scores, q) * scale).astype(low))
        dv.append(along_first(probs_low, d).astype(low))
    dqkv = jnp.concatenate(dq + dk + dv, axis=1)
    back_first = along_last(dqkv, weight_ref[...])
    rows = tokens_ref[...].reshape(length, width).astype(wide)
    rows = rows * lax.rsqrt(jnp.mean(rows * rows, axis=-1, keepdims=True) + epsilon)
    for w in range(SHARDS):
        held[w] = back_first[w * chunk : (w + 1) * chunk].astype(low)
    store_w(backs, held, me)

    gains = [jnp.sum(back_first * rows, axis=0, keepdims=True), gain_two_ref[...]]
    gains = jnp.concatenate(gains + [jnp.zeros((14, width), wide)], axis=0).astype(low)
    i = lax.broadcasted_iota(jnp.int32, (LANES, LANES), 0)
    j = lax.broadcasted_iota(jnp.int32, (LANES, LANES), 1)
    extra = along_first(gains, (i[:16] == j[:16]).astype(low))
    extra = extra + matmul(router_ref[...].astype(low), (i + 2 == j).astype(low))
    above = jnp.zeros((2 + experts, length), wide)
    below = jnp.zeros((LANES - 2 - experts - heads, length), wide)
    spread = jnp.concatenate([above] + diagonals + [below], axis=0)
    shift = lax.broadcasted_iota(jnp.int32, (length, width), 0)
    lane = lax.broadcasted_iota(jnp.int32, (length, width), 1)
    bucket = bucket_of(jnp.where(shift > 0, length - shift, 0))
    hits = (lane == (bucket // table_rows) * shard + bucket % table_rows).astype(low)
    spread_low = spread.astype(low)
    rest = (spread - spread_low.astype(wide)).astype(low)
    turn = (((0,), (1,)), ((), ()))
    extra = extra + lax.dot_general(hits, spread_low, turn, preferred_element_type=wide)
    extra = extra + lax.dot_general(hits, rest, turn, preferred_element_type=wide)
    output = along_first(att_ref[...], up)
    output = jnp.concatenate([output[:, w * shard : (w + 1) * shard] for w in range(SHARDS)], axis=0)
    grads = jnp.concatenate([along_first(first_ref[...], dqkv), extra, output], axis=1)
    if len(parts) == 1:
        parts[0][...] = grads.astype(low)
    else:
        table[...] = grads
        piece = parts[0].shape[1]
        for s, ref in enumerate(parts):
            for w in range(SHARDS):
                start = pl.multiple_of(w * shard + (me_ref[1] ^ s) * piece, 8)
                ref[w] = table[pl.ds(start, piece), :].astype(low)


def join_kernel(me_ref, *refs):
    terms, outs, output_ref, held = refs[:5], refs[5 : 5 + SHARDS], refs[5 + SHARDS], refs[6 + SHARDS]
    total = total_of(terms)
    columns = outs[0].shape[1]
    held[...] = total[:, :, :columns]
    for s in range(SHARDS):
        outs[s][...] = held[me_ref[0] ^ s].astype(low)
    output_ref[...] = jnp.concatenate([total[w][:, columns:] for w in range(SHARDS)], axis=1).astype(low)


def order_kernel(experts, me_ref, *refs):
    parts, output_ref, out_ref, held = refs[:SHARDS], refs[SHARDS], refs[SHARDS + 1], refs[SHARDS + 2]
    for s in range(SHARDS):
        held[me_ref[0] ^ s] = parts[s][...].astype(wide)
    own = HEADS // SHARDS
    span = own * HEAD_DIM
    blocks = [held[w] for w in range(SHARDS)]
    pieces = [blocks[w][:, k * span : (k + 1) * span] for k in range(3) for w in range(SHARDS)]
    lane = lax.broadcasted_iota(jnp.int32, (parts[0].shape[0], LANES), 1)
    extra = jnp.zeros((parts[0].shape[0], LANES), wide)
    for w in range(SHARDS):
        small = blocks[w][:, 3 * span :]
        heads = jnp.where((lane >= 2 + experts) & (lane < 2 + experts + own), small, 0.0)
        extra = extra + jnp.where(lane < 2 + experts, small, 0.0) + pltpu.roll(heads, own * w, 1)
    pieces = pieces + [output_ref[...].astype(wide), extra]
    out_ref[...] = jnp.concatenate(pieces, axis=1).astype(low)


def final_kernel(me_ref, *refs):
    parts, outs = refs[:-9], refs[-9:-1]
    held = refs[-1]
    piece = parts[0].shape[0]
    width = outs[0].shape[1]
    experts = outs[6].shape[1]
    for s, ref in enumerate(parts):
        here = pl.ds(pl.multiple_of((me_ref[1] ^ s) * piece, 8), piece)
        block = ref[...].astype(wide)
        for k in range(4):
            outs[k][here, :] = block[:, k * width : (k + 1) * width]
        held[here, :] = block[:, 4 * width :]
    extra = held[...]
    shard = extra.shape[0]
    i = lax.broadcasted_iota(jnp.int32, (shard, shard), 0)
    j = lax.broadcasted_iota(jnp.int32, (shard, shard), 1)
    turned = along_first(extra.astype(low), (i == j).astype(low))
    outs[4][...] = turned[0:1]
    outs[5][...] = turned[1:2]
    outs[6][...] = extra[:, 2 : 2 + experts]
    outs[7][...] = extra[: outs[7].shape[0], 2 + experts : 2 + experts + HEADS]


def tokens_back_kernel(me_ref, tokens_ref, small_ref, resid_ref, *refs):
    terms, out_ref = refs[:-1], refs[-1]
    experts = experts_of(small_ref.shape[0])
    gain = small_ref[experts : experts + 1, :].astype(wide)
    rows = tokens_ref[...].astype(wide)
    r = lax.rsqrt(jnp.mean(rows * rows, axis=-1, keepdims=True) + epsilon)
    m = total_of(terms) * gain
    back = r * m - (r * r * r) * rows * jnp.mean(m * rows, axis=-1, keepdims=True)
    out_ref[...] = resid_ref[...] + back


def local(
    tokens,
    segments,
    routes,
    blocks,
    attention_gain,
    query_weight,
    key_weight,
    value_weight,
    output_weight,
    position_bias,
    feed_gain,
    router_weight,
    expert_in,
    expert_out,
    cotangent,
):
    rows, width = tokens.shape
    length = rows * SHARDS
    experts = lax.axis_size(E)
    me_w = lax.axis_index(W)
    me_e = lax.axis_index(E)
    me = jnp.stack([me_w, me_e, blocks[0] * BLOCK]).astype(jnp.int32)
    shard = query_weight.shape[0]
    own_heads = HEADS // SHARDS
    table_rows = position_bias.shape[0]
    first_local, second_local = expert_in[0], expert_out[0]
    row = (rows, width)
    packed_row = (CAP, width)
    three_rows = [(row, low), (row, low), ((2,) + row, low)]

    quick = experts == 8
    small_rows = -(-(experts + 2 + HEADS) // 16) * 16
    tokens_rel = gather_w(tokens)
    weight_rel = exchange_w(
        call(
            start_kernel,
            [((shard + small_rows, 3 * shard), low)] * SHARDS,
            [((SHARDS, shard, 3 * shard), low)],
            me,
            query_weight,
            key_weight,
            value_weight,
            router_weight.T,
            attention_gain,
            feed_gain,
            position_bias,
            room=FULL,
        )
    )
    (sent,) = call(
        sent_kernel,
        [((rows + 16, width), low)],
        [],
        me,
        cotangent,
        routes.T,
        room=FULL,
    )
    sent = [sent, swap(sent, E, 2), swap(sent, E, 4), swap(sent, E, 6)] if quick else gather_e(sent)

    square = (own_heads, length, length)
    outs = call(
        attend_kernel,
        [
            ((SHARDS, rows, width), low),
            ((length, width), low),
            ((length, 3 * shard), low),
            (square, low),
            ((length, shard), low),
            ((width, 3 * shard), low),
            ((small_rows, width), low),
            ((LANES, width), low),
        ],
        [((SHARDS, shard + small_rows, 3 * shard), low)],
        me,
        *tokens_rel,
        *weight_rel,
        segments,
        cover=20,
    )
    tokens_all, first, qkv, probs, attended, weight, small, router = outs
    *branches, stacked = call(
        branch_kernel,
        three_rows + [((4, rows + 16, width), low)],
        [((SHARDS, rows, width), low)],
        me,
        attended,
        output_weight,
        *sent[:4],
    )
    branch_terms, _ = sum_w(*branches)
    resid, second = call(
        second_kernel,
        [(row, wide), (row, low)],
        [],
        me,
        tokens,
        small,
        *branch_terms,
    )

    second_rel = gather_e(second)

    if quick:
        sent.append(swap(stacked, E, 1))
    dispatch, partner, *upstream_rows = call(
        route_kernel,
        [
            ((CAP, experts * rows), low),
            ((CAP, experts * rows // 2), low),
            ((CAP // 2, width), low),
            ((CAP // 2 + 16, width), low),
        ],
        [],
        me,
        *sent,
        after=(second,),
    )
    upstream_rel = list(zip(gather_w(upstream_rows[0]), gather_w(upstream_rows[1])))
    order = (0, 1, 2, 3)
    outs = call(
        upstream_kernel,
        [(packed_row, wide)] * SHARDS + [((CAP, LANES), wide)] * SHARDS,
        [],
        me,
        second_local,
        *[piece for s in order for piece in upstream_rel[s]],
    )
    back_act, choice = outs[:SHARDS], outs[SHARDS:]

    (packed,) = call(
        pack_kernel,
        [(packed_row, low)],
        [],
        me,
        dispatch,
        *second_rel,
        after=upstream_rel[2],
    )
    half = (2 * CAP, width)

    def expert_half(k, after):
        return call(
            expert_kernel,
            [(packed_row, low)] * 2 + [(half, low), (half, low), ((2 * CAP, LANES), low)],
            [],
            me,
            back_act[2 * k],
            back_act[2 * k + 1],
            choice[2 * k],
            choice[2 * k + 1],
            first_local,
            router,
            rows_rel[order[2 * k]],
            rows_rel[order[2 * k + 1]],
            after=after,
        )

    far = swap(packed, W, 2)
    rows_rel = [packed, swap(packed, W, 1)]
    halves = [expert_half(0, ())]
    far = tie(far, halves[0][0])
    rows_rel = rows_rel + [far, swap(far, W, 1)]
    halves.append(expert_half(1, ()))
    near = swap(halves[1][1], W, 1)
    across = (halves[1][0].astype(wide) + near.astype(wide)).astype(low)
    *results, router_grad = call(
        lambda *refs: result_kernel(order, *refs),
        [(packed_row, low)] * SHARDS + [((width, LANES), wide)],
        [],
        me,
        second_local,
        halves[0][2],
        halves[1][2],
        halves[0][4],
        halves[1][4],
        *rows_rel,
        after=(across,),
    )
    back_parts = call(
        unpack_kernel,
        [(row, low)] * experts,
        [],
        me,
        dispatch,
        halves[0][0],
        swap(halves[0][1], W, 1),
        swap(across, W, 2),
        after=(results[0],),
    )
    back_terms = sum_e(back_parts)

    near = swap(results[3], W, 1)
    across = (results[2].astype(wide) + near.astype(wide)).astype(low)
    result_terms = [results[0], swap(results[1], W, 1), swap(across, W, 2)]
    if quick:
        (mixed,) = call(total_kernel, [(packed_row, low)], [], me, *result_terms)
        mixed_parts = call(
            unpack_both_kernel, [(row, low)] * 4, [], me, dispatch, partner, mixed, swap(mixed, E, 1)
        )
        mixed_terms = [mixed_parts[0]] + [swap(mixed_parts[s // 2], E, s) for s in (4, 6, 2)]
    else:
        mixed_parts = call(unpack_kernel, [(row, low)] * experts, [], me, dispatch, *result_terms)
        mixed_terms = sum_e(mixed_parts)

    back_resid, back_branch, gain_two_grad = call(
        resid_back_kernel,
        [(row, wide), (row, low), ((1, width), wide)],
        [],
        me,
        resid,
        small,
        cotangent,
        *back_terms,
        after=(mixed_parts[0],),
    )
    back_rel = exchange_w([back_branch] * SHARDS)
    columns = 3 * shard + LANES
    piece = shard // experts
    part = (SHARDS, piece, columns + shard)
    outs = call(
        lambda *refs: attend_back_kernel(experts, table_rows, *refs),
        three_rows
        + ([(part, low)] * experts if quick else [((width, columns + shard), low)]),
        [((SHARDS, rows, width), low), ((width, columns + shard), wide)],
        me,
        output_weight,
        qkv,
        probs,
        weight,
        tokens_all,
        first,
        attended,
        gain_two_grad,
        router_grad,
        *back_rel,
        cover=20,
    )
    grads = list(outs[3:])
    (layer_out,) = call(layer_kernel, [(row, low)], [], me, resid, *mixed_terms, after=(grads[-1],))
    if quick:
        grads[5] = tie(grads[5], *mixed_terms[1:])
    back_terms, _ = sum_w(*outs[:3])
    (tokens_grad,) = call(
        tokens_back_kernel,
        [(row, wide)],
        [],
        me,
        tokens,
        small,
        back_resid,
        *back_terms,
    )

    first_grad, second_grad = call(
        lambda *refs: grads_kernel(order, *refs),
        [((1,) + first_local.shape, wide), ((1,) + second_local.shape, wide)],
        [],
        me,
        halves[0][2],
        halves[1][2],
        halves[0][3],
        halves[1][3],
        *rows_rel,
        *[piece for pieces in upstream_rel for piece in pieces],
        after=(grads[-1],),
    )

    if quick:
        terms = sum_e(grads)
        *grads, output_grad = call(
            join_kernel,
            [((piece, columns), low)] * SHARDS + [((piece, width), low)],
            [((SHARDS, piece, columns), wide)],
            me,
            *terms,
        )
        (grads,) = call(
            lambda *refs: order_kernel(experts, *refs),
            [((piece, 4 * width + LANES), low)],
            [((SHARDS, piece, columns), wide)],
            me,
            *exchange_w(grads),
            output_grad,
        )
        shape = (shard, width)
        outs = call(
            final_kernel,
            [(shape, wide)] * 4
            + [((1, shard), wide)] * 2
            + [((shard, experts), wide), ((table_rows, HEADS), wide)],
            [((shard, LANES), wide)],
            me,
            *gather_e(grads),
        )
        query_grad, key_grad, value_grad, output_grad = outs[:4]
        gain_one_grad, gain_two_grad = outs[4].reshape(shard), outs[5].reshape(shard)
        router_grad, table_grad = outs[6], outs[7]
    else:
        grads = lax.psum(grads[0], E).astype(wide).reshape(SHARDS, shard, columns + shard)
        output_grad = grads[:, :, columns:].transpose(1, 0, 2).reshape(shard, width)
        grads = grads[:, :, :columns].astype(low)
        grads = place(
            exchange_w([lax.dynamic_index_in_dim(grads, me_w ^ s, 0, False) for s in range(SHARDS)]), me_w
        ).astype(wide)
        main = grads[:, :, : 3 * shard].reshape(SHARDS, shard, 3, shard).transpose(2, 1, 0, 3)
        query_grad, key_grad, value_grad = main.reshape(3, shard, width)
        extra = grads[:, :, 3 * shard :]
        summed = jnp.sum(extra[:, :, : 2 + experts], axis=0)
        gain_one_grad, gain_two_grad, router_grad = summed[:, 0], summed[:, 1], summed[:, 2:]
        table_grad = extra[:, :table_rows, 2 + experts : 2 + experts + own_heads]
        table_grad = table_grad.transpose(1, 0, 2).reshape(table_rows, HEADS)
    return (
        layer_out,
        tokens_grad,
        gain_one_grad,
        query_grad,
        key_grad,
        value_grad,
        output_grad,
        table_grad,
        gain_two_grad,
        router_grad,
        first_grad,
        second_grad,
    )


def solution(mesh):
    in_specs = (
        P(("expert", "wshard"), None),
        P("expert", None),
        P(("expert", "wshard"), None),
        P("expert"),
        P("wshard"),
        P("wshard", None),
        P("wshard", None),
        P("wshard", None),
        P("wshard", None),
        P("wshard", None),
        P("wshard"),
        P("wshard", None),
        P("expert", "wshard", None),
        P("expert", "wshard", None),
        P(("expert", "wshard"), None),
    )
    out_specs = (
        P(("expert", "wshard"), None),
        P(("expert", "wshard"), None),
        P("wshard"),
        P("wshard", None),
        P("wshard", None),
        P("wshard", None),
        P("wshard", None),
        P("wshard", None),
        P("wshard"),
        P("wshard", None),
        P("expert", "wshard", None),
        P("expert", "wshard", None),
    )
    return jax.shard_map(local, mesh=mesh, in_specs=in_specs, out_specs=out_specs, check_vma=False)
```

```python
import math

import jax
import jax.numpy as jnp
from jax import lax
from jax.experimental import pallas as pl
from jax.experimental.pallas import tpu as pltpu
from jax.sharding import PartitionSpec as P

HEADS = 12
HEAD_DIM = 64
BUCKETS = 32
BLOCK = 128
MOST_BLOCKS = 2
SHARDS = 4
LANES = 128
CAP = MOST_BLOCKS * BLOCK
W = "wshard"
E = "expert"

epsilon = 1e-06
thresholds = tuple((math.ceil(16 * 2 ** (3 * order / 16)) for order in range(1, 16)))
low = jnp.bfloat16
wide = jnp.float32
FULL = 60 << 20


def bucket_of(distance):
    passed = jnp.zeros_like(distance)
    for edge in thresholds:
        passed = passed + (distance >= edge).astype(jnp.int32)
    return jnp.where(distance < 16, distance, 16 + passed)


def along_last(left, right):
    return lax.dot_general(left, right, (((1,), (1,)), ((), ())), preferred_element_type=wide)


def along_first(left, right):
    return lax.dot_general(left, right, (((0,), (0,)), ((), ())), preferred_element_type=wide)


def matmul(left, right):
    return jnp.dot(left, right, preferred_element_type=wide)


def swap(value, axis, step):
    count = lax.axis_size(axis)
    return lax.ppermute(value, axis, [(i, i ^ step) for i in range(count)])


def gather_w(value):
    far = swap(value, W, 2)
    near = swap(value, W, 1)
    return [value, near, far, swap(far, W, 1)]


def sum_w(own, across, pair):
    got = swap(pair, W, 1)
    across = (across.astype(wide) + got[0].astype(wide)).astype(low)
    return [own, got, swap(across, W, 2)], across


def exchange_w(parts):
    return [parts[0]] + [swap(parts[s], W, s) for s in (1, 2, 3)]


def place(parts, me):
    out = jnp.zeros((len(parts),) + parts[0].shape, parts[0].dtype)
    for s, part in enumerate(parts):
        out = lax.dynamic_update_index_in_dim(out, part, me ^ s, 0)
    return out


def gather_e(value):
    count = lax.axis_size(E)
    if count > 8:
        whole = lax.all_gather(value, E, axis=0)
        me = lax.axis_index(E)
        order = me ^ jnp.arange(count, dtype=jnp.int32)
        whole = whole[order]
        return [whole[s] for s in range(count)]
    out = {0: value}
    for s in (4, 6, 2):
        out[s] = swap(value, E, s)
    for s in (0, 4, 6, 2):
        out[s ^ 1] = swap(out[s], E, 1)
    return [out[s] for s in range(8)]


def sum_e(parts):
    count = lax.axis_size(E)
    if count > 8:
        me = lax.axis_index(E)
        whole = jnp.stack(parts)[me ^ jnp.arange(count, dtype=jnp.int32)]
        return [lax.psum_scatter(whole, E, scatter_dimension=0)]
    got = {s: swap(parts[s ^ 1], E, 1) for s in (4, 6, 2)}
    terms = [parts[0], swap(tie(parts[1], got[4]), E, 1)]
    for s in (4, 6, 2):
        part = (parts[s].astype(wide) + got[s].astype(wide)).astype(low)
        terms.append(swap(part, E, s))
    return terms


def experts_of(small_rows):
    return {32: 8, 80: 64}[small_rows]


def total_of(refs):
    rank = len(refs[0].shape)
    out = refs[0][...].astype(wide)
    for ref in refs[1:]:
        out = out + (ref[...] if len(ref.shape) == rank else ref[1]).astype(wide)
    return out


def store_w(outs, held, me):
    outs[0][...] = held[me]
    outs[1][...] = held[me ^ 2]
    outs[2][0] = held[me ^ 3]
    outs[2][1] = held[me ^ 1]


def call(kernel, outs, scratch, scalars, *args, after=(), room=None, cover=0):
    outs, scratch, after = tuple(outs), tuple(scratch), tuple(after)
    smem = pl.BlockSpec(memory_space=pltpu.SMEM)
    block = pl.BlockSpec()
    apart = pl.BlockSpec(memory_space=pl.ANY)
    size = sum(a.size * a.dtype.itemsize for a in args)
    size = size + sum(math.prod(s) * jnp.dtype(d).itemsize for s, d in outs + scratch)
    skip = len(after)
    return pl.pallas_call(
        lambda *refs: kernel(*refs[skip:]),
        out_shape=tuple(jax.ShapeDtypeStruct(s, d) for s, d in outs),
        in_specs=[apart] * skip + [smem] + [block] * len(args),
        out_specs=tuple(block for _ in outs),
        scratch_shapes=[pltpu.VMEM(s, d) for s, d in scratch],
        compiler_params=pltpu.CompilerParams(vmem_limit_bytes=room or (10 << 20) + size),
        cost_estimate=pl.CostEstimate(flops=1 + cover * 10**9, bytes_accessed=1, transcendentals=0),
    )(*after, scalars, *args)


def tie(value, *after):
    apart = pl.BlockSpec(memory_space=pl.ANY)
    return pl.pallas_call(
        lambda *refs: None,
        out_shape=jax.ShapeDtypeStruct(value.shape, value.dtype),
        in_specs=[apart] * (1 + len(after)),
        out_specs=apart,
        input_output_aliases={0: 0},
        compiler_params=pltpu.CompilerParams(vmem_limit_bytes=1 << 20),
        cost_estimate=pl.CostEstimate(flops=1, bytes_accessed=1, transcendentals=0),
    )(value, *after)


def start_kernel(me_ref, q_ref, k_ref, v_ref, router_ref, one_ref, two_ref, table_ref, *rest):
    outs, held = rest[:SHARDS], rest[SHARDS]
    shard = q_ref.shape[0]
    for w in range(SHARDS):
        here = slice(w * shard, (w + 1) * shard)
        held[w] = jnp.concatenate([q_ref[:, here], k_ref[:, here], v_ref[:, here]], axis=1)
    i = lax.broadcasted_iota(jnp.int32, (table_ref.shape[0], shard), 0)
    j = lax.broadcasted_iota(jnp.int32, (table_ref.shape[0], shard), 1)
    small = [
        router_ref[...],
        one_ref[...].reshape(1, shard),
        two_ref[...].reshape(1, shard),
        along_first(table_ref[...], (i == j).astype(low)).astype(low),
    ]
    used = sum(piece.shape[0] for piece in small)
    small = jnp.concatenate(small + [jnp.zeros((outs[0].shape[0] - shard - used, shard), low)], axis=0)
    small = jnp.concatenate([small, jnp.zeros((small.shape[0], 2 * shard), low)], axis=1)
    for s in range(SHARDS):
        outs[s][:shard, :] = held[me_ref[0] ^ s]
        outs[s][shard:, :] = small


def sent_kernel(me_ref, up_ref, routes_ref, sent_ref):
    rows, width = up_ref.shape
    sent_ref[:rows, :] = up_ref[...]
    blocks = jnp.full((1, rows), me_ref[2].astype(wide) / BLOCK).astype(low)
    named = jnp.concatenate([routes_ref[...].astype(low), blocks, jnp.zeros((13, rows), low)], axis=0)
    sent_ref[rows:, :] = jnp.concatenate([named, jnp.zeros((16, width - rows), low)], axis=1)


def attend_kernel(me_ref, *refs):
    tokens, weights = refs[:SHARDS], refs[SHARDS : 2 * SHARDS]
    row_ref, *rest = refs[2 * SHARDS :]
    tokens_ref, first_ref, qkv_ref, probs_ref, att_ref, weight_ref, small_ref, router_ref, held_w = rest
    me = me_ref[0]
    shard = att_ref.shape[1]
    chunk, width = tokens[0].shape
    length = chunk * SHARDS
    heads = probs_ref.shape[0]
    span = heads * HEAD_DIM
    for s in range(SHARDS):
        tokens_ref[me ^ s] = tokens[s][...]
        held_w[me ^ s] = weights[s][...]
    for w in range(SHARDS):
        weight_ref[w * shard : (w + 1) * shard, :] = held_w[w, :shard, :]
    small = jnp.concatenate([held_w[w, shard:, :shard] for w in range(SHARDS)], axis=1)
    small_ref[...] = small
    experts = experts_of(small_ref.shape[0])
    router_ref[...] = jnp.zeros_like(router_ref)
    router_ref[:experts, :] = small[:experts]
    gain_one = small[experts : experts + 1].astype(wide)

    shift = lax.broadcasted_iota(jnp.int32, (length, width), 0)
    lane = lax.broadcasted_iota(jnp.int32, (length, width), 1)
    bucket = bucket_of(jnp.where(shift > 0, length - shift, 0))
    per = BUCKETS // SHARDS
    hits = (lane == (bucket // per) * shard + bucket % per).astype(low)
    vectors = along_last(small[experts + 2 : experts + 2 + HEADS], hits)
    i = lax.broadcasted_iota(jnp.int32, (length, length), 0)
    j = lax.broadcasted_iota(jnp.int32, (length, length), 1)
    marks = jnp.broadcast_to(row_ref[...], (length, length))
    column = jnp.sum(jnp.where(i == j, marks, 0), axis=1, keepdims=True)
    allowed = (j <= i) & (marks == column)
    which = lax.broadcasted_iota(jnp.int32, vectors.shape, 0)

    rows = tokens_ref[...].reshape(length, width).astype(wide)
    scale = lax.rsqrt(jnp.mean(rows * rows, axis=-1, keepdims=True) + epsilon)
    first = (rows * scale * gain_one).astype(low)
    first_ref[...] = first
    qkv = matmul(first, weight_ref[...]).astype(low)
    qkv_ref[...] = qkv
    columns = []
    for h in range(heads):
        vector = jnp.sum(jnp.where(which == me * heads + h, vectors, 0.0), axis=0, keepdims=True)
        bias = pltpu.roll(jnp.broadcast_to(vector, (length, length)), 0, 1, stride=1, stride_axis=0)
        bias = jnp.where(allowed, bias, -1e30)
        q = qkv[:, h * HEAD_DIM : (h + 1) * HEAD_DIM] * (HEAD_DIM**-0.5)
        k = qkv[:, span + h * HEAD_DIM : span + (h + 1) * HEAD_DIM]
        v = qkv[:, 2 * span + h * HEAD_DIM : 2 * span + (h + 1) * HEAD_DIM]
        pieces = []
        for b in range(SHARDS):
            end = (b + 1) * chunk
            here = slice(b * chunk, end)
            scores = along_last(q[here], k[:end]) + bias[here, :end]
            largest = jnp.max(scores, axis=-1, keepdims=True)
            grown = jnp.exp(scores - largest)
            total = jnp.sum(grown, axis=-1, keepdims=True)
            probs = (grown / total).astype(low)
            probs_ref[h, here, :end] = probs
            if end < length:
                probs_ref[h, here, end:] = jnp.zeros((chunk, length - end), low)
            pieces.append(matmul(probs, v[:end]))
        columns.append(jnp.concatenate(pieces, axis=0))
    att_ref[...] = jnp.concatenate(columns, axis=1).astype(low)


def branch_kernel(me_ref, att_ref, out_ref, *refs):
    sent, branches, held = refs[:-5], refs[-5:-2], refs[-1]
    chunk = held.shape[1]
    for k, ref in enumerate(sent):
        refs[-2][k] = ref[...]
    branch = matmul(att_ref[...], out_ref[...]).astype(low)
    for w in range(SHARDS):
        held[w] = branch[w * chunk : (w + 1) * chunk]
    store_w(branches, held, me_ref[0])


def second_kernel(me_ref, tokens_ref, small_ref, *refs):
    terms, (resid_ref, second_ref) = refs[:-2], refs[-2:]
    experts = experts_of(small_ref.shape[0])
    gain = small_ref[experts + 1 : experts + 2, :].astype(wide)
    resid = tokens_ref[...].astype(wide) + total_of(terms)
    resid_ref[...] = resid
    scale = lax.rsqrt(jnp.mean(resid * resid, axis=-1, keepdims=True) + epsilon)
    second_ref[...] = (resid * scale * gain).astype(low)


def route_kernel(me_ref, *refs):
    me, limit = me_ref[1], me_ref[2].astype(wide)
    mine = me.astype(wide)
    sent, (dispatch_ref, partner_ref, rows_ref, last_ref) = refs[:-4], refs[-4:]
    if len(sent[-1].shape) == 3:
        sent = [sent[s // 2] if s % 2 == 0 else sent[-1].at[s // 2] for s in range(8)]
    count = len(sent)
    tall = sent[0].shape[0] - 16
    i = lax.broadcasted_iota(jnp.int32, (tall, tall), 0)
    j = lax.broadcasted_iota(jnp.int32, (tall, tall), 1)
    before = (i < j).astype(low)
    slots = lax.broadcasted_iota(jnp.int32, (CAP, tall), 0).astype(wide)
    named = [sent[s][tall:, :tall].astype(wide) for s in range(count)]

    def one_hots(expert, limit, wanted):
        mine = expert.astype(wide)
        hits = jnp.concatenate([((r[0:1] == mine) | (r[1:2] == mine)).astype(wide) for r in named], axis=0)
        within = matmul(hits.astype(low), before)
        counts = jnp.sum(hits, axis=1, keepdims=True)
        index = me ^ lax.broadcasted_iota(jnp.int32, (count, 1), 0)
        for s in wanted:
            base = jnp.sum(jnp.where(index < (me ^ s), counts, 0.0), axis=0, keepdims=True)
            rank = within[s : s + 1] + base
            slot = jnp.where((hits[s : s + 1] > 0) & (rank < limit), rank, -1.0)
            yield s, (slots == slot).astype(low)

    packed = jnp.zeros((CAP, rows_ref.shape[1]), wide)
    other = jnp.zeros((16, CAP), wide)
    mine = me.astype(wide)
    for s, one_hot in one_hots(me, limit, range(count)):
        dispatch_ref[:, s * tall : (s + 1) * tall] = one_hot
        packed = packed + matmul(one_hot, sent[s][:tall, :])
        name = jnp.where(named[s][0:1] == mine, named[s][1:2], named[s][0:1])
        other = other + along_last(jnp.broadcast_to(name, (16, tall)).astype(low), one_hot)
    half = rows_ref.shape[0]
    rows_ref[...] = packed[:half].astype(low)
    last_ref[: CAP - half, :] = packed[half:].astype(low)
    tail = jnp.zeros((16, rows_ref.shape[1] - CAP), low)
    last_ref[CAP - half :, :] = jnp.concatenate([other.astype(low), tail], axis=1)
    for s, one_hot in one_hots(me ^ 1, named[1][2:3] * BLOCK, range(0, count, 2)):
        partner_ref[:, s // 2 * tall : (s // 2 + 1) * tall] = one_hot


def upstream_kernel(me_ref, weight_ref, *refs):
    rows, backs, choices = refs[: 2 * SHARDS], refs[2 * SHARDS : 3 * SHARDS], refs[3 * SHARDS :]
    half = rows[0].shape[0]
    mine = me_ref[1].astype(wide)
    i = lax.broadcasted_iota(jnp.int32, (CAP, CAP), 0)
    j = lax.broadcasted_iota(jnp.int32, (CAP, CAP), 1)
    lane = lax.broadcasted_iota(jnp.int32, (CAP, LANES), 1).astype(wide)
    for k in range(SHARDS):
        backs[k][:half, :] = along_last(rows[2 * k][...], weight_ref[...])
        backs[k][half:, :] = along_last(rows[2 * k + 1][: CAP - half, :], weight_ref[...])
        across = rows[2 * k + 1][CAP - half :, :CAP].astype(wide)[0:1]
        other = jnp.sum(jnp.where(i == j, across, 0.0), axis=1, keepdims=True)
        choices[k][...] = (lane == mine).astype(wide) - (lane == other).astype(wide)


def pack_kernel(me_ref, dispatch_ref, *refs):
    rows, out_ref = refs[:-1], refs[-1]
    tall = rows[0].shape[0]
    total = jnp.zeros(out_ref.shape, wide)
    for s, ref in enumerate(rows):
        total = total + matmul(dispatch_ref[:, s * tall : (s + 1) * tall], ref[...])
    out_ref[...] = total.astype(low)


def expert_kernel(count, me_ref, weight_ref, router_ref, *refs):
    backs, choices, rows, outs = (refs[k * count : (k + 1) * count] for k in range(4))
    act_ref, back_pre_ref, logits_ref = refs[4 * count :]
    for k in range(count):
        here = slice(k * CAP, (k + 1) * CAP)
        block = rows[k][...]
        choice = choices[k][...]
        back = backs[k][...]
        chosen = jnp.sum(along_last(block, router_ref[...]) * choice, axis=1, keepdims=True)
        gate = jax.nn.sigmoid(chosen)
        pre = along_last(block, weight_ref[...])
        square = pre * pre
        slope = math.sqrt(2 / math.pi)
        bent = jnp.tanh(slope * pre * (1.0 + 0.044715 * square))
        half = 0.5 * (1.0 + bent)
        act = pre * half
        steep = half + 0.5 * pre * (1.0 - bent * bent) * (slope * (1.0 + 3 * 0.044715 * square))
        act_ref[here, :] = (act * gate).astype(low)
        back_pre = (steep * (back * gate)).astype(low)
        back_pre_ref[here, :] = back_pre
        back_gate = jnp.sum(act * back, axis=1, keepdims=True)
        logits = (gate * jax.nn.sigmoid(-chosen) * back_gate * choice).astype(low)
        logits_ref[here, :] = logits
        outs[k][...] = (matmul(back_pre, weight_ref[...]) + matmul(logits, router_ref[...])).astype(low)


def result_kernel(me_ref, weight_ref, *refs):
    acts, logits, rows, outs = refs[:3], refs[3:6], refs[6 : 6 + SHARDS], refs[6 + SHARDS : -1]
    router = jnp.zeros(refs[-1].shape, wide)
    for s in range(SHARDS):
        k, here = (0, slice(s * CAP, (s + 1) * CAP)) if s < 2 else (s - 1, slice(0, CAP))
        outs[s][...] = matmul(acts[k][here, :], weight_ref[...]).astype(low)
        router = router + along_first(rows[s][...], logits[k][here, :])
    refs[-1][...] = router


def layer_kernel(me_ref, resid_ref, *refs):
    refs[-1][...] = (resid_ref[...] + total_of(refs[:-1])).astype(low)


def grads_kernel(me_ref, *refs):
    acts, pres, rows, ups = refs[:3], refs[3:6], refs[6 : 6 + SHARDS], refs[6 + SHARDS : 6 + 3 * SHARDS]
    first_ref, second_ref, flag_ref = refs[6 + 3 * SHARDS :]
    flag_ref[...] = jnp.zeros_like(flag_ref)
    acts = jnp.concatenate([ref[...] for ref in acts], axis=0)
    pres = jnp.concatenate([ref[...] for ref in pres], axis=0)
    first_ref[0] = along_first(pres, jnp.concatenate([ref[...] for ref in rows], axis=0))
    half = CAP - ups[0].shape[0]
    ups = jnp.concatenate([ref[...] for s in range(SHARDS) for ref in (ups[2 * s], ups[2 * s + 1].at[:half])], axis=0)
    second_ref[0] = along_first(acts, ups)


def unpack_kernel(me_ref, dispatch_ref, *refs):
    terms, outs = refs[:3], refs[3:]
    block = total_of(terms).astype(low)
    tall = outs[0].shape[0]
    for s, ref in enumerate(outs):
        ref[...] = along_first(dispatch_ref[:, s * tall : (s + 1) * tall], block).astype(low)


def total_kernel(me_ref, *refs):
    refs[-1][...] = total_of(refs[:-1]).astype(low)


def unpack_both_kernel(me_ref, dispatch_ref, partner_ref, block_ref, other_ref, *outs):
    tall = outs[0].shape[0]
    for k, ref in enumerate(outs):
        own = along_first(dispatch_ref[:, 2 * k * tall : (2 * k + 1) * tall], block_ref[...])
        other = along_first(partner_ref[:, k * tall : (k + 1) * tall], other_ref[...])
        ref[...] = (own + other).astype(low)


def resid_back_kernel(me_ref, resid_ref, small_ref, cotangent_ref, *refs):
    terms, (back_ref, branch_ref, gain_ref) = refs[:-3], refs[-3:]
    experts = experts_of(small_ref.shape[0])
    gain = small_ref[experts + 1 : experts + 2, :].astype(wide)
    resid = resid_ref[...]
    upstream = total_of(terms)
    r = lax.rsqrt(jnp.mean(resid * resid, axis=-1, keepdims=True) + epsilon)
    gain_ref[...] = jnp.sum(upstream * (resid * r), axis=0, keepdims=True)
    m = upstream * gain
    back = r * m - (r * r * r) * resid * jnp.mean(m * resid, axis=-1, keepdims=True)
    back = back + cotangent_ref[...].astype(wide)
    back_ref[...] = back
    branch_ref[...] = back.astype(low)


def attend_back_kernel(
    experts,
    table_rows,
    me_ref,
    out_ref,
    qkv_ref,
    probs_ref,
    weight_ref,
    tokens_ref,
    first_ref,
    att_ref,
    gain_two_ref,
    router_ref,
    *refs,
):
    ups, backs = refs[:SHARDS], refs[SHARDS : SHARDS + 3]
    parts, (held, table) = refs[SHARDS + 3 : -2], refs[-2:]
    me = me_ref[0]
    shard = out_ref.shape[0]
    chunk, width = ups[0].shape
    length = chunk * SHARDS
    heads = probs_ref.shape[0]
    span = heads * HEAD_DIM
    scale = HEAD_DIM**-0.5
    for s in range(SHARDS):
        held[me ^ s] = ups[s][...]
    up = held[...].reshape(length, width)
    back = along_last(up, out_ref[...]).astype(low)
    qkv = qkv_ref[...]
    dq, dk, dv = [], [], []
    i = lax.broadcasted_iota(jnp.int32, (chunk, chunk), 0)
    j = lax.broadcasted_iota(jnp.int32, (chunk, chunk), 1)
    reverse = (i + j == chunk - 1).astype(low)
    diagonals = []
    for h in range(heads):
        q = qkv[:, h * HEAD_DIM : (h + 1) * HEAD_DIM]
        k = qkv[:, span + h * HEAD_DIM : span + (h + 1) * HEAD_DIM]
        v = qkv[:, 2 * span + h * HEAD_DIM : 2 * span + (h + 1) * HEAD_DIM]
        d = back[:, h * HEAD_DIM : (h + 1) * HEAD_DIM]
        probs_low = probs_ref[h]
        probs = probs_low.astype(wide)
        back_probs = along_last(d, v)
        inner = jnp.sum(back_probs * probs, axis=-1, keepdims=True)
        scores = (probs * (back_probs - inner)).astype(low)
        diagonal = jnp.zeros((1, length), wide)
        for b in range(SHARDS):
            turned = matmul(reverse, scores[b * chunk : (b + 1) * chunk])
            start = (1 - (b + 1) * chunk) % length
            turned = pltpu.roll(turned, start, 1, stride=1, stride_axis=0)
            diagonal = diagonal + jnp.sum(turned, axis=0, keepdims=True)
        diagonals.append(diagonal)
        dq.append((matmul(scores, k) * scale).astype(low))
        dk.append((along_first(scores, q) * scale).astype(low))
        dv.append(along_first(probs_low, d).astype(low))
    dqkv = jnp.concatenate(dq + dk + dv, axis=1)
    back_first = along_last(dqkv, weight_ref[...])
    rows = tokens_ref[...].reshape(length, width).astype(wide)
    rows = rows * lax.rsqrt(jnp.mean(rows * rows, axis=-1, keepdims=True) + epsilon)
    for w in range(SHARDS):
        held[w] = back_first[w * chunk : (w + 1) * chunk].astype(low)
    store_w(backs, held, me)

    gains = [jnp.sum(back_first * rows, axis=0, keepdims=True), gain_two_ref[...]]
    gains = jnp.concatenate(gains + [jnp.zeros((14, width), wide)], axis=0).astype(low)
    i = lax.broadcasted_iota(jnp.int32, (LANES, LANES), 0)
    j = lax.broadcasted_iota(jnp.int32, (LANES, LANES), 1)
    extra = along_first(gains, (i[:16] == j[:16]).astype(low))
    extra = extra + matmul(router_ref[...].astype(low), (i + 2 == j).astype(low))
    above = jnp.zeros((2 + experts, length), wide)
    below = jnp.zeros((LANES - 2 - experts - heads, length), wide)
    spread = jnp.concatenate([above] + diagonals + [below], axis=0)
    shift = lax.broadcasted_iota(jnp.int32, (length, width), 0)
    lane = lax.broadcasted_iota(jnp.int32, (length, width), 1)
    bucket = bucket_of(jnp.where(shift > 0, length - shift, 0))
    hits = (lane == (bucket // table_rows) * shard + bucket % table_rows).astype(low)
    spread_low = spread.astype(low)
    rest = (spread - spread_low.astype(wide)).astype(low)
    turn = (((0,), (1,)), ((), ()))
    extra = extra + lax.dot_general(hits, spread_low, turn, preferred_element_type=wide)
    extra = extra + lax.dot_general(hits, rest, turn, preferred_element_type=wide)
    output = along_first(att_ref[...], up)
    output = jnp.concatenate([output[:, w * shard : (w + 1) * shard] for w in range(SHARDS)], axis=0)
    grads = jnp.concatenate([along_first(first_ref[...], dqkv), extra, output], axis=1)
    if len(parts) == 1:
        parts[0][...] = grads.astype(low)
    else:
        table[...] = grads
        piece = parts[0].shape[1]
        for s, ref in enumerate(parts):
            for w in range(SHARDS):
                start = pl.multiple_of(w * shard + (me_ref[1] ^ s) * piece, 8)
                ref[w] = table[pl.ds(start, piece), :].astype(low)


def join_kernel(me_ref, *refs):
    terms, outs, output_ref, held = refs[:5], refs[5 : 5 + SHARDS], refs[5 + SHARDS], refs[6 + SHARDS]
    total = total_of(terms)
    columns = outs[0].shape[1]
    held[...] = total[:, :, :columns]
    for s in range(SHARDS):
        outs[s][...] = held[me_ref[0] ^ s].astype(low)
    output_ref[...] = jnp.concatenate([total[w][:, columns:] for w in range(SHARDS)], axis=1).astype(low)


def order_kernel(experts, me_ref, *refs):
    parts, output_ref, out_ref, held = refs[:SHARDS], refs[SHARDS], refs[SHARDS + 1], refs[SHARDS + 2]
    for s in range(SHARDS):
        held[me_ref[0] ^ s] = parts[s][...].astype(wide)
    own = HEADS // SHARDS
    span = own * HEAD_DIM
    blocks = [held[w] for w in range(SHARDS)]
    pieces = [blocks[w][:, k * span : (k + 1) * span] for k in range(3) for w in range(SHARDS)]
    lane = lax.broadcasted_iota(jnp.int32, (parts[0].shape[0], LANES), 1)
    extra = jnp.zeros((parts[0].shape[0], LANES), wide)
    for w in range(SHARDS):
        small = blocks[w][:, 3 * span :]
        heads = jnp.where((lane >= 2 + experts) & (lane < 2 + experts + own), small, 0.0)
        extra = extra + jnp.where(lane < 2 + experts, small, 0.0) + pltpu.roll(heads, own * w, 1)
    pieces = pieces + [output_ref[...].astype(wide), extra]
    out_ref[...] = jnp.concatenate(pieces, axis=1).astype(low)


def final_kernel(me_ref, *refs):
    parts, outs = refs[:-9], refs[-9:-1]
    held = refs[-1]
    piece = parts[0].shape[0]
    width = outs[0].shape[1]
    experts = outs[6].shape[0]
    for s, ref in enumerate(parts):
        here = pl.ds(pl.multiple_of((me_ref[1] ^ s) * piece, 8), piece)
        block = ref[...].astype(wide)
        for k in range(4):
            outs[k][here, :] = block[:, k * width : (k + 1) * width]
        held[here, :] = block[:, 4 * width :]
    extra = held[...]
    shard = extra.shape[0]
    i = lax.broadcasted_iota(jnp.int32, (shard, shard), 0)
    j = lax.broadcasted_iota(jnp.int32, (shard, shard), 1)
    turned = along_first(extra.astype(low), (i == j).astype(low))
    outs[4][...] = turned[0]
    outs[5][...] = turned[1]
    outs[6][...] = turned[2 : 2 + experts]
    outs[7][...] = extra[: outs[7].shape[0], 2 + experts : 2 + experts + HEADS]


def tokens_back_kernel(me_ref, tokens_ref, small_ref, resid_ref, *refs):
    terms, out_ref = refs[:-1], refs[-1]
    experts = experts_of(small_ref.shape[0])
    gain = small_ref[experts : experts + 1, :].astype(wide)
    rows = tokens_ref[...].astype(wide)
    r = lax.rsqrt(jnp.mean(rows * rows, axis=-1, keepdims=True) + epsilon)
    m = total_of(terms) * gain
    back = r * m - (r * r * r) * rows * jnp.mean(m * rows, axis=-1, keepdims=True)
    out_ref[...] = resid_ref[...] + back


def local(
    tokens,
    segments,
    routes,
    blocks,
    attention_gain,
    query_weight,
    key_weight,
    value_weight,
    output_weight,
    position_bias,
    feed_gain,
    router_weight,
    expert_in,
    expert_out,
    cotangent,
):
    rows, width = tokens.shape
    length = rows * SHARDS
    experts = lax.axis_size(E)
    me_w = lax.axis_index(W)
    me_e = lax.axis_index(E)
    me = jnp.stack([me_w, me_e, blocks[0] * BLOCK]).astype(jnp.int32)
    shard = query_weight.shape[0]
    own_heads = HEADS // SHARDS
    table_rows = position_bias.shape[0]
    first_local, second_local = expert_in[0], expert_out[0]
    row = (rows, width)
    packed_row = (CAP, width)
    three_rows = [(row, low), (row, low), ((2,) + row, low)]

    quick = experts == 8
    small_rows = -(-(experts + 2 + HEADS) // 16) * 16
    tokens_rel = gather_w(tokens)
    weight_rel = exchange_w(
        call(
            start_kernel,
            [((shard + small_rows, 3 * shard), low)] * SHARDS,
            [((SHARDS, shard, 3 * shard), low)],
            me,
            query_weight,
            key_weight,
            value_weight,
            router_weight.T,
            attention_gain,
            feed_gain,
            position_bias,
            room=FULL,
        )
    )
    (sent,) = call(
        sent_kernel,
        [((rows + 16, width), low)],
        [],
        me,
        cotangent,
        routes.T,
        room=FULL,
    )
    sent = [sent, swap(sent, E, 2), swap(sent, E, 4), swap(sent, E, 6)] if quick else gather_e(sent)

    square = (own_heads, length, length)
    outs = call(
        attend_kernel,
        [
            ((SHARDS, rows, width), low),
            ((length, width), low),
            ((length, 3 * shard), low),
            (square, low),
            ((length, shard), low),
            ((width, 3 * shard), low),
            ((small_rows, width), low),
            ((LANES, width), low),
        ],
        [((SHARDS, shard + small_rows, 3 * shard), low)],
        me,
        *tokens_rel,
        *weight_rel,
        segments,
        cover=20,
    )
    tokens_all, first, qkv, probs, attended, weight, small, router = outs
    *branches, stacked = call(
        branch_kernel,
        three_rows + [((4, rows + 16, width), low)],
        [((SHARDS, rows, width), low)],
        me,
        attended,
        output_weight,
        *sent[:4],
    )
    branch_terms, _ = sum_w(*branches)
    resid, second = call(
        second_kernel,
        [(row, wide), (row, low)],
        [],
        me,
        tokens,
        small,
        *branch_terms,
    )

    second_rel = gather_e(second)

    if quick:
        sent.append(swap(stacked, E, 1))
    dispatch, partner, *upstream_rows = call(
        route_kernel,
        [
            ((CAP, experts * rows), low),
            ((CAP, experts * rows // 2), low),
            ((CAP // 2, width), low),
            ((CAP // 2 + 16, width), low),
        ],
        [],
        me,
        *sent,
        after=(second,),
    )
    upstream_rel = list(zip(gather_w(upstream_rows[0]), gather_w(upstream_rows[1])))
    order = (0, 1, 2, 3)
    outs = call(
        upstream_kernel,
        [(packed_row, wide)] * SHARDS + [((CAP, LANES), wide)] * SHARDS,
        [],
        me,
        second_local,
        *[piece for s in order for piece in upstream_rel[s]],
    )
    back_act, choice = outs[:SHARDS], outs[SHARDS:]

    (packed,) = call(
        pack_kernel,
        [(packed_row, low)],
        [],
        me,
        dispatch,
        *second_rel,
        after=upstream_rel[2],
    )

    def expert_rows(parts, after=()):
        tall = len(parts) * CAP
        *outs, act, pre, logits = call(
            lambda *refs: expert_kernel(len(parts), *refs),
            [(packed_row, low)] * len(parts) + [((tall, width), low), ((tall, width), low), ((tall, LANES), low)],
            [],
            me,
            first_local,
            router,
            *[back_act[s] for s in parts],
            *[choice[s] for s in parts],
            *[rows_rel[s] for s in parts],
            after=after,
        )
        return outs, act, pre, logits

    far = swap(packed, W, 2)
    rows_rel = [packed, swap(packed, W, 1)]
    (own_rows, near_rows), *kept_a = expert_rows((0, 1))
    far = tie(far, own_rows)
    rows_rel = rows_rel + [far, swap(far, W, 1)]
    (across_rows,), *kept_b = expert_rows((2,))
    (last_rows,), *kept_c = expert_rows((3,), after=(kept_b[2],))
    acts, pres, logits = zip(kept_a, kept_b, kept_c)
    near = swap(last_rows, W, 1)
    across = (across_rows.astype(wide) + near.astype(wide)).astype(low)
    *results, router_grad = call(
        result_kernel,
        [(packed_row, low)] * SHARDS + [((width, LANES), wide)],
        [],
        me,
        second_local,
        *acts,
        *logits,
        *rows_rel,
        after=(across,),
    )
    first_grad, second_grad, flag = call(
        grads_kernel,
        [((1,) + first_local.shape, wide), ((1,) + second_local.shape, wide), ((8, LANES), wide)],
        [],
        me,
        *acts,
        *pres,
        *rows_rel,
        *[piece for pieces in upstream_rel for piece in pieces],
        after=(results[0],),
    )
    back_parts = call(
        unpack_kernel,
        [(row, low)] * experts,
        [],
        me,
        dispatch,
        own_rows,
        swap(near_rows, W, 1),
        swap(across, W, 2),
        after=(results[0], flag),
    )
    back_terms = sum_e(back_parts)

    near = swap(results[3], W, 1)
    across = (results[2].astype(wide) + near.astype(wide)).astype(low)
    result_terms = [results[0], swap(results[1], W, 1), swap(across, W, 2)]
    if quick:
        (mixed,) = call(total_kernel, [(packed_row, low)], [], me, *result_terms)
        mixed_parts = call(
            unpack_both_kernel, [(row, low)] * 4, [], me, dispatch, partner, mixed, swap(mixed, E, 1)
        )
        mixed_terms = [mixed_parts[0]] + [swap(mixed_parts[s // 2], E, s) for s in (4, 6, 2)]
    else:
        mixed_parts = call(unpack_kernel, [(row, low)] * experts, [], me, dispatch, *result_terms)
        mixed_terms = sum_e(mixed_parts)

    back_resid, back_branch, gain_two_grad = call(
        resid_back_kernel,
        [(row, wide), (row, low), ((1, width), wide)],
        [],
        me,
        resid,
        small,
        cotangent,
        *back_terms,
        after=(mixed_parts[0],),
    )
    back_rel = exchange_w([back_branch] * SHARDS)
    columns = 3 * shard + LANES
    piece = shard // experts
    part = (SHARDS, piece, columns + shard)
    outs = call(
        lambda *refs: attend_back_kernel(experts, table_rows, *refs),
        three_rows
        + ([(part, low)] * experts if quick else [((width, columns + shard), low)]),
        [((SHARDS, rows, width), low), ((width, columns + shard), wide)],
        me,
        output_weight,
        qkv,
        probs,
        weight,
        tokens_all,
        first,
        attended,
        gain_two_grad,
        router_grad,
        *back_rel,
        cover=20,
    )
    grads = list(outs[3:])
    (layer_out,) = call(layer_kernel, [(row, low)], [], me, resid, *mixed_terms, after=(grads[-1],))
    if quick:
        grads[5] = tie(grads[5], *mixed_terms[1:])
    back_terms, _ = sum_w(*outs[:3])
    (tokens_grad,) = call(
        tokens_back_kernel,
        [(row, wide)],
        [],
        me,
        tokens,
        small,
        back_resid,
        *back_terms,
    )

    if quick:
        terms = sum_e(grads)
        *grads, output_grad = call(
            join_kernel,
            [((piece, columns), low)] * SHARDS + [((piece, width), low)],
            [((SHARDS, piece, columns), wide)],
            me,
            *terms,
        )
        (grads,) = call(
            lambda *refs: order_kernel(experts, *refs),
            [((piece, 4 * width + LANES), low)],
            [((SHARDS, piece, columns), wide)],
            me,
            *exchange_w(grads),
            output_grad,
        )
        shape = (shard, width)
        outs = call(
            final_kernel,
            [(shape, wide)] * 4
            + [((shard,), wide)] * 2
            + [((experts, shard), wide), ((table_rows, HEADS), wide)],
            [((shard, LANES), wide)],
            me,
            *gather_e(grads),
        )
        query_grad, key_grad, value_grad, output_grad = outs[:4]
        gain_one_grad, gain_two_grad = outs[4], outs[5]
        router_grad, table_grad = outs[6].T, outs[7]
    else:
        grads = lax.psum(grads[0], E).astype(wide).reshape(SHARDS, shard, columns + shard)
        output_grad = grads[:, :, columns:].transpose(1, 0, 2).reshape(shard, width)
        grads = grads[:, :, :columns].astype(low)
        grads = place(
            exchange_w([lax.dynamic_index_in_dim(grads, me_w ^ s, 0, False) for s in range(SHARDS)]), me_w
        ).astype(wide)
        main = grads[:, :, : 3 * shard].reshape(SHARDS, shard, 3, shard).transpose(2, 1, 0, 3)
        query_grad, key_grad, value_grad = main.reshape(3, shard, width)
        extra = grads[:, :, 3 * shard :]
        summed = jnp.sum(extra[:, :, : 2 + experts], axis=0)
        gain_one_grad, gain_two_grad, router_grad = summed[:, 0], summed[:, 1], summed[:, 2:]
        table_grad = extra[:, :table_rows, 2 + experts : 2 + experts + own_heads]
        table_grad = table_grad.transpose(1, 0, 2).reshape(table_rows, HEADS)
    return (
        layer_out,
        tokens_grad,
        gain_one_grad,
        query_grad,
        key_grad,
        value_grad,
        output_grad,
        table_grad,
        gain_two_grad,
        router_grad,
        first_grad,
        second_grad,
    )


def solution(mesh):
    in_specs = (
        P(("expert", "wshard"), None),
        P("expert", None),
        P(("expert", "wshard"), None),
        P("expert"),
        P("wshard"),
        P("wshard", None),
        P("wshard", None),
        P("wshard", None),
        P("wshard", None),
        P("wshard", None),
        P("wshard"),
        P("wshard", None),
        P("expert", "wshard", None),
        P("expert", "wshard", None),
        P(("expert", "wshard"), None),
    )
    out_specs = (
        P(("expert", "wshard"), None),
        P(("expert", "wshard"), None),
        P("wshard"),
        P("wshard", None),
        P("wshard", None),
        P("wshard", None),
        P("wshard", None),
        P("wshard", None),
        P("wshard"),
        P("wshard", None),
        P("expert", "wshard", None),
        P("expert", "wshard", None),
    )
    return jax.shard_map(local, mesh=mesh, in_specs=in_specs, out_specs=out_specs, check_vma=False)
```

```python
import math

import jax
import jax.numpy as jnp
from jax import lax
from jax.experimental import pallas as pl
from jax.experimental.pallas import tpu as pltpu
from jax.sharding import PartitionSpec as P

HEADS = 12
HEAD_DIM = 64
BUCKETS = 32
BLOCK = 128
MOST_BLOCKS = 2
SHARDS = 4
LANES = 128
CAP = MOST_BLOCKS * BLOCK
W = "wshard"
E = "expert"

epsilon = 1e-06
thresholds = tuple((math.ceil(16 * 2 ** (3 * order / 16)) for order in range(1, 16)))
low = jnp.bfloat16
wide = jnp.float32
FULL = 60 << 20


def bucket_of(distance):
    passed = jnp.zeros_like(distance)
    for edge in thresholds:
        passed = passed + (distance >= edge).astype(jnp.int32)
    return jnp.where(distance < 16, distance, 16 + passed)


def along_last(left, right):
    return lax.dot_general(left, right, (((1,), (1,)), ((), ())), preferred_element_type=wide)


def along_first(left, right):
    return lax.dot_general(left, right, (((0,), (0,)), ((), ())), preferred_element_type=wide)


def matmul(left, right):
    return jnp.dot(left, right, preferred_element_type=wide)


def swap(value, axis, step):
    count = lax.axis_size(axis)
    return lax.ppermute(value, axis, [(i, i ^ step) for i in range(count)])


def gather_w(value):
    far = swap(value, W, 2)
    near = swap(value, W, 1)
    return [value, near, far, swap(far, W, 1)]


def sum_w(own, across, pair):
    got = swap(pair, W, 1)
    across = (across.astype(wide) + got[0].astype(wide)).astype(low)
    return [own, got, swap(across, W, 2)], across


def exchange_w(parts):
    return [parts[0]] + [swap(parts[s], W, s) for s in (1, 2, 3)]


def place(parts, me):
    out = jnp.zeros((len(parts),) + parts[0].shape, parts[0].dtype)
    for s, part in enumerate(parts):
        out = lax.dynamic_update_index_in_dim(out, part, me ^ s, 0)
    return out


def gather_e(value):
    count = lax.axis_size(E)
    if count > 8:
        whole = lax.all_gather(value, E, axis=0)
        me = lax.axis_index(E)
        order = me ^ jnp.arange(count, dtype=jnp.int32)
        whole = whole[order]
        return [whole[s] for s in range(count)]
    out = {0: value}
    for s in (4, 6, 2):
        out[s] = swap(value, E, s)
    for s in (0, 4, 6, 2):
        out[s ^ 1] = swap(out[s], E, 1)
    return [out[s] for s in range(8)]


def sum_e(parts, early=False):
    count = lax.axis_size(E)
    if count > 8:
        me = lax.axis_index(E)
        whole = jnp.stack(parts)[me ^ jnp.arange(count, dtype=jnp.int32)]
        return [lax.psum_scatter(whole, E, scatter_dimension=0)]
    got = {s: swap(parts[s ^ 1], E, 1) for s in (4, 6, 2)}
    terms = [parts[0], swap(tie(parts[1], got[4]), E, 1)]
    for s in (4, 6, 2):
        part = (parts[s].astype(wide) + got[s].astype(wide)).astype(low)
        terms.append(swap(part, E, s))
    if early:
        (first,) = call(
            partial_kernel, [(parts[0].shape, wide)], [], jnp.zeros((1,), jnp.int32), parts[0], terms[2], cover=20
        )
        terms = [first, terms[1], *terms[3:]]
    return terms


def experts_of(small_rows):
    return {32: 8, 80: 64}[small_rows]


def total_of(refs):
    rank = len(refs[0].shape)
    out = refs[0][...].astype(wide)
    for ref in refs[1:]:
        out = out + (ref[...] if len(ref.shape) == rank else ref[1]).astype(wide)
    return out


def partial_kernel(me_ref, *refs):
    refs[-1][...] = total_of(refs[:-1])


def store_w(outs, held, me):
    outs[0][...] = held[me]
    outs[1][...] = held[me ^ 2]
    outs[2][0] = held[me ^ 3]
    outs[2][1] = held[me ^ 1]


def call(kernel, outs, scratch, scalars, *args, after=(), room=None, cover=0):
    outs, scratch, after = tuple(outs), tuple(scratch), tuple(after)
    smem = pl.BlockSpec(memory_space=pltpu.SMEM)
    block = pl.BlockSpec()
    apart = pl.BlockSpec(memory_space=pl.ANY)
    size = sum(a.size * a.dtype.itemsize for a in args)
    size = size + sum(math.prod(s) * jnp.dtype(d).itemsize for s, d in outs + scratch)
    skip = len(after)
    return pl.pallas_call(
        lambda *refs: kernel(*refs[skip:]),
        out_shape=tuple(jax.ShapeDtypeStruct(s, d) for s, d in outs),
        in_specs=[apart] * skip + [smem] + [block] * len(args),
        out_specs=tuple(block for _ in outs),
        scratch_shapes=[pltpu.VMEM(s, d) for s, d in scratch],
        compiler_params=pltpu.CompilerParams(vmem_limit_bytes=room or (10 << 20) + size),
        cost_estimate=pl.CostEstimate(flops=1 + cover * 10**9, bytes_accessed=1, transcendentals=0),
    )(*after, scalars, *args)


def tie(value, *after):
    apart = pl.BlockSpec(memory_space=pl.ANY)
    return pl.pallas_call(
        lambda *refs: None,
        out_shape=jax.ShapeDtypeStruct(value.shape, value.dtype),
        in_specs=[apart] * (1 + len(after)),
        out_specs=apart,
        input_output_aliases={0: 0},
        compiler_params=pltpu.CompilerParams(vmem_limit_bytes=1 << 20),
        cost_estimate=pl.CostEstimate(flops=1, bytes_accessed=1, transcendentals=0),
    )(value, *after)


def start_kernel(me_ref, q_ref, k_ref, v_ref, router_ref, one_ref, two_ref, table_ref, *rest):
    outs, held = rest[:SHARDS], rest[SHARDS]
    shard = q_ref.shape[0]
    for w in range(SHARDS):
        here = slice(w * shard, (w + 1) * shard)
        held[w] = jnp.concatenate([q_ref[:, here], k_ref[:, here], v_ref[:, here]], axis=1)
    i = lax.broadcasted_iota(jnp.int32, (table_ref.shape[0], shard), 0)
    j = lax.broadcasted_iota(jnp.int32, (table_ref.shape[0], shard), 1)
    small = [
        router_ref[...],
        one_ref[...].reshape(1, shard),
        two_ref[...].reshape(1, shard),
        along_first(table_ref[...], (i == j).astype(low)).astype(low),
    ]
    used = sum(piece.shape[0] for piece in small)
    small = jnp.concatenate(small + [jnp.zeros((outs[0].shape[0] - shard - used, shard), low)], axis=0)
    small = jnp.concatenate([small, jnp.zeros((small.shape[0], 2 * shard), low)], axis=1)
    for s in range(SHARDS):
        outs[s][:shard, :] = held[me_ref[0] ^ s]
        outs[s][shard:, :] = small


def sent_kernel(me_ref, up_ref, routes_ref, sent_ref):
    rows, width = up_ref.shape
    sent_ref[:rows, :] = up_ref[...]
    blocks = jnp.full((1, rows), me_ref[2].astype(wide) / BLOCK).astype(low)
    named = jnp.concatenate([routes_ref[...].astype(low), blocks, jnp.zeros((13, rows), low)], axis=0)
    sent_ref[rows:, :] = jnp.concatenate([named, jnp.zeros((16, width - rows), low)], axis=1)


def attend_kernel(me_ref, *refs):
    tokens, weights = refs[:SHARDS], refs[SHARDS : 2 * SHARDS]
    row_ref, *rest = refs[2 * SHARDS :]
    tokens_ref, first_ref, qkv_ref, probs_ref, att_ref, weight_ref, small_ref, router_ref, held_w = rest
    me = me_ref[0]
    shard = att_ref.shape[1]
    chunk, width = tokens[0].shape
    length = chunk * SHARDS
    heads = probs_ref.shape[0]
    span = heads * HEAD_DIM
    for s in range(SHARDS):
        tokens_ref[me ^ s] = tokens[s][...]
        held_w[me ^ s] = weights[s][...]
    for w in range(SHARDS):
        weight_ref[w * shard : (w + 1) * shard, :] = held_w[w, :shard, :]
    small = jnp.concatenate([held_w[w, shard:, :shard] for w in range(SHARDS)], axis=1)
    small_ref[...] = small
    experts = experts_of(small_ref.shape[0])
    router_ref[...] = jnp.zeros_like(router_ref)
    router_ref[:experts, :] = small[:experts]
    gain_one = small[experts : experts + 1].astype(wide)

    shift = lax.broadcasted_iota(jnp.int32, (length, width), 0)
    lane = lax.broadcasted_iota(jnp.int32, (length, width), 1)
    bucket = bucket_of(jnp.where(shift > 0, length - shift, 0))
    per = BUCKETS // SHARDS
    hits = (lane == (bucket // per) * shard + bucket % per).astype(low)
    vectors = along_last(small[experts + 2 : experts + 2 + HEADS], hits)
    i = lax.broadcasted_iota(jnp.int32, (length, length), 0)
    j = lax.broadcasted_iota(jnp.int32, (length, length), 1)
    marks = jnp.broadcast_to(row_ref[...], (length, length))
    column = jnp.sum(jnp.where(i == j, marks, 0), axis=1, keepdims=True)
    allowed = (j <= i) & (marks == column)
    which = lax.broadcasted_iota(jnp.int32, vectors.shape, 0)

    rows = tokens_ref[...].reshape(length, width).astype(wide)
    scale = lax.rsqrt(jnp.mean(rows * rows, axis=-1, keepdims=True) + epsilon)
    first = (rows * scale * gain_one).astype(low)
    first_ref[...] = first
    qkv = matmul(first, weight_ref[...]).astype(low)
    qkv_ref[...] = qkv
    columns = []
    for h in range(heads):
        vector = jnp.sum(jnp.where(which == me * heads + h, vectors, 0.0), axis=0, keepdims=True)
        bias = pltpu.roll(jnp.broadcast_to(vector, (length, length)), 0, 1, stride=1, stride_axis=0)
        bias = jnp.where(allowed, bias, -1e30)
        q = qkv[:, h * HEAD_DIM : (h + 1) * HEAD_DIM] * (HEAD_DIM**-0.5)
        k = qkv[:, span + h * HEAD_DIM : span + (h + 1) * HEAD_DIM]
        v = qkv[:, 2 * span + h * HEAD_DIM : 2 * span + (h + 1) * HEAD_DIM]
        pieces = []
        for b in range(SHARDS):
            end = (b + 1) * chunk
            here = slice(b * chunk, end)
            scores = along_last(q[here], k[:end]) + bias[here, :end]
            largest = jnp.max(scores, axis=-1, keepdims=True)
            grown = jnp.exp(scores - largest)
            total = jnp.sum(grown, axis=-1, keepdims=True)
            probs = (grown / total).astype(low)
            probs_ref[h, here, :end] = probs
            if end < length:
                probs_ref[h, here, end:] = jnp.zeros((chunk, length - end), low)
            pieces.append(matmul(probs, v[:end]))
        columns.append(jnp.concatenate(pieces, axis=0))
    att_ref[...] = jnp.concatenate(columns, axis=1).astype(low)


def branch_kernel(me_ref, att_ref, out_ref, *refs):
    sent, branches, held = refs[:-5], refs[-5:-2], refs[-1]
    chunk = held.shape[1]
    for k, ref in enumerate(sent):
        refs[-2][k] = ref[...]
    branch = matmul(att_ref[...], out_ref[...]).astype(low)
    for w in range(SHARDS):
        held[w] = branch[w * chunk : (w + 1) * chunk]
    store_w(branches, held, me_ref[0])


def second_kernel(me_ref, tokens_ref, small_ref, *refs):
    terms, (resid_ref, second_ref) = refs[:-2], refs[-2:]
    experts = experts_of(small_ref.shape[0])
    gain = small_ref[experts + 1 : experts + 2, :].astype(wide)
    resid = tokens_ref[...].astype(wide) + total_of(terms)
    resid_ref[...] = resid
    scale = lax.rsqrt(jnp.mean(resid * resid, axis=-1, keepdims=True) + epsilon)
    second_ref[...] = (resid * scale * gain).astype(low)


def route_kernel(me_ref, *refs):
    me, limit = me_ref[1], me_ref[2].astype(wide)
    mine = me.astype(wide)
    sent, (dispatch_ref, partner_ref, rows_ref, last_ref) = refs[:-4], refs[-4:]
    if len(sent[-1].shape) == 3:
        sent = [sent[s // 2] if s % 2 == 0 else sent[-1].at[s // 2] for s in range(8)]
    count = len(sent)
    tall = sent[0].shape[0] - 16
    i = lax.broadcasted_iota(jnp.int32, (tall, tall), 0)
    j = lax.broadcasted_iota(jnp.int32, (tall, tall), 1)
    before = (i < j).astype(low)
    slots = lax.broadcasted_iota(jnp.int32, (CAP, tall), 0).astype(wide)
    named = [sent[s][tall:, :tall].astype(wide) for s in range(count)]

    def one_hots(expert, limit, wanted):
        mine = expert.astype(wide)
        hits = jnp.concatenate([((r[0:1] == mine) | (r[1:2] == mine)).astype(wide) for r in named], axis=0)
        within = matmul(hits.astype(low), before)
        counts = jnp.sum(hits, axis=1, keepdims=True)
        index = me ^ lax.broadcasted_iota(jnp.int32, (count, 1), 0)
        for s in wanted:
            base = jnp.sum(jnp.where(index < (me ^ s), counts, 0.0), axis=0, keepdims=True)
            rank = within[s : s + 1] + base
            slot = jnp.where((hits[s : s + 1] > 0) & (rank < limit), rank, -1.0)
            yield s, (slots == slot).astype(low)

    packed = jnp.zeros((CAP, rows_ref.shape[1]), wide)
    other = jnp.zeros((16, CAP), wide)
    mine = me.astype(wide)
    for s, one_hot in one_hots(me, limit, range(count)):
        dispatch_ref[:, s * tall : (s + 1) * tall] = one_hot
        packed = packed + matmul(one_hot, sent[s][:tall, :])
        name = jnp.where(named[s][0:1] == mine, named[s][1:2], named[s][0:1])
        other = other + along_last(jnp.broadcast_to(name, (16, tall)).astype(low), one_hot)
    half = rows_ref.shape[0]
    rows_ref[...] = packed[:half].astype(low)
    last_ref[: CAP - half, :] = packed[half:].astype(low)
    tail = jnp.zeros((16, rows_ref.shape[1] - CAP), low)
    last_ref[CAP - half :, :] = jnp.concatenate([other.astype(low), tail], axis=1)
    for s, one_hot in one_hots(me ^ 1, named[1][2:3] * BLOCK, range(0, count, 2)):
        partner_ref[:, s // 2 * tall : (s // 2 + 1) * tall] = one_hot


def upstream_kernel(me_ref, weight_ref, *refs):
    rows, backs, choices = refs[: 2 * SHARDS], refs[2 * SHARDS : 3 * SHARDS], refs[3 * SHARDS :]
    half = rows[0].shape[0]
    mine = me_ref[1].astype(wide)
    i = lax.broadcasted_iota(jnp.int32, (CAP, CAP), 0)
    j = lax.broadcasted_iota(jnp.int32, (CAP, CAP), 1)
    lane = lax.broadcasted_iota(jnp.int32, (CAP, LANES), 1).astype(wide)
    for k in range(SHARDS):
        backs[k][:half, :] = along_last(rows[2 * k][...], weight_ref[...])
        backs[k][half:, :] = along_last(rows[2 * k + 1][: CAP - half, :], weight_ref[...])
        across = rows[2 * k + 1][CAP - half :, :CAP].astype(wide)[0:1]
        other = jnp.sum(jnp.where(i == j, across, 0.0), axis=1, keepdims=True)
        choices[k][...] = (lane == mine).astype(wide) - (lane == other).astype(wide)


def pack_kernel(me_ref, dispatch_ref, *refs):
    rows, out_ref = refs[:-1], refs[-1]
    tall = rows[0].shape[0]
    total = jnp.zeros(out_ref.shape, wide)
    for s, ref in enumerate(rows):
        total = total + matmul(dispatch_ref[:, s * tall : (s + 1) * tall], ref[...])
    out_ref[...] = total.astype(low)


def expert_kernel(count, me_ref, weight_ref, router_ref, *refs):
    backs, choices, rows, outs = (refs[k * count : (k + 1) * count] for k in range(4))
    act_ref, back_pre_ref, logits_ref = refs[4 * count :]
    for k in range(count):
        here = slice(k * CAP, (k + 1) * CAP)
        block = rows[k][...]
        choice = choices[k][...]
        back = backs[k][...]
        chosen = jnp.sum(along_last(block, router_ref[...]) * choice, axis=1, keepdims=True)
        gate = jax.nn.sigmoid(chosen)
        pre = along_last(block, weight_ref[...])
        square = pre * pre
        slope = math.sqrt(2 / math.pi)
        bent = jnp.tanh(slope * pre * (1.0 + 0.044715 * square))
        half = 0.5 * (1.0 + bent)
        act = pre * half
        steep = half + 0.5 * pre * (1.0 - bent * bent) * (slope * (1.0 + 3 * 0.044715 * square))
        act_ref[here, :] = (act * gate).astype(low)
        back_pre = (steep * (back * gate)).astype(low)
        back_pre_ref[here, :] = back_pre
        back_gate = jnp.sum(act * back, axis=1, keepdims=True)
        logits = (gate * jax.nn.sigmoid(-chosen) * back_gate * choice).astype(low)
        logits_ref[here, :] = logits
        outs[k][...] = (matmul(back_pre, weight_ref[...]) + matmul(logits, router_ref[...])).astype(low)


def result_kernel(me_ref, weight_ref, *refs):
    acts, logits, rows, outs = refs[:3], refs[3:6], refs[6 : 6 + SHARDS], refs[6 + SHARDS : -1]
    router = jnp.zeros(refs[-1].shape, wide)
    for s in range(SHARDS):
        k, here = (0, slice(s * CAP, (s + 1) * CAP)) if s < 2 else (s - 1, slice(0, CAP))
        outs[s][...] = matmul(acts[k][here, :], weight_ref[...]).astype(low)
        router = router + along_first(rows[s][...], logits[k][here, :])
    refs[-1][...] = router


def layer_kernel(me_ref, resid_ref, *refs):
    refs[-1][...] = (resid_ref[...] + total_of(refs[:-1])).astype(low)


def grads_kernel(me_ref, *refs):
    acts, pres, rows, ups = refs[:3], refs[3:6], refs[6 : 6 + SHARDS], refs[6 + SHARDS : 6 + 3 * SHARDS]
    first_ref, second_ref, flag_ref = refs[6 + 3 * SHARDS :]
    flag_ref[...] = jnp.zeros_like(flag_ref)
    acts = jnp.concatenate([ref[...] for ref in acts], axis=0)
    pres = jnp.concatenate([ref[...] for ref in pres], axis=0)
    first_ref[0] = along_first(pres, jnp.concatenate([ref[...] for ref in rows], axis=0))
    half = CAP - ups[0].shape[0]
    ups = jnp.concatenate([ref[...] for s in range(SHARDS) for ref in (ups[2 * s], ups[2 * s + 1].at[:half])], axis=0)
    second_ref[0] = along_first(acts, ups)


def unpack_kernel(me_ref, dispatch_ref, *refs):
    terms, outs = refs[:3], refs[3:]
    block = total_of(terms).astype(low)
    tall = outs[0].shape[0]
    for s, ref in enumerate(outs):
        ref[...] = along_first(dispatch_ref[:, s * tall : (s + 1) * tall], block).astype(low)


def total_kernel(me_ref, *refs):
    refs[-1][...] = total_of(refs[:-1]).astype(low)


def unpack_both_kernel(me_ref, dispatch_ref, partner_ref, block_ref, other_ref, *outs):
    tall = outs[0].shape[0]
    for k, ref in enumerate(outs):
        own = along_first(dispatch_ref[:, 2 * k * tall : (2 * k + 1) * tall], block_ref[...])
        other = along_first(partner_ref[:, k * tall : (k + 1) * tall], other_ref[...])
        ref[...] = (own + other).astype(low)


def resid_back_kernel(me_ref, resid_ref, small_ref, cotangent_ref, *refs):
    terms, (back_ref, branch_ref, gain_ref) = refs[:-3], refs[-3:]
    experts = experts_of(small_ref.shape[0])
    gain = small_ref[experts + 1 : experts + 2, :].astype(wide)
    resid = resid_ref[...]
    upstream = total_of(terms)
    r = lax.rsqrt(jnp.mean(resid * resid, axis=-1, keepdims=True) + epsilon)
    gain_ref[...] = jnp.sum(upstream * (resid * r), axis=0, keepdims=True)
    m = upstream * gain
    back = r * m - (r * r * r) * resid * jnp.mean(m * resid, axis=-1, keepdims=True)
    back = back + cotangent_ref[...].astype(wide)
    back_ref[...] = back
    branch_ref[...] = back.astype(low)


def attend_back_kernel(
    experts,
    table_rows,
    me_ref,
    out_ref,
    qkv_ref,
    probs_ref,
    weight_ref,
    tokens_ref,
    first_ref,
    att_ref,
    gain_two_ref,
    router_ref,
    *refs,
):
    ups, backs = refs[:SHARDS], refs[SHARDS : SHARDS + 3]
    parts, (held, table) = refs[SHARDS + 3 : -2], refs[-2:]
    me = me_ref[0]
    shard = out_ref.shape[0]
    chunk, width = ups[0].shape
    length = chunk * SHARDS
    heads = probs_ref.shape[0]
    span = heads * HEAD_DIM
    scale = HEAD_DIM**-0.5
    for s in range(SHARDS):
        held[me ^ s] = ups[s][...]
    up = held[...].reshape(length, width)
    back = along_last(up, out_ref[...]).astype(low)
    qkv = qkv_ref[...]
    dq, dk, dv = [], [], []
    i = lax.broadcasted_iota(jnp.int32, (chunk, chunk), 0)
    j = lax.broadcasted_iota(jnp.int32, (chunk, chunk), 1)
    reverse = (i + j == chunk - 1).astype(low)
    diagonals = []
    for h in range(heads):
        q = qkv[:, h * HEAD_DIM : (h + 1) * HEAD_DIM]
        k = qkv[:, span + h * HEAD_DIM : span + (h + 1) * HEAD_DIM]
        v = qkv[:, 2 * span + h * HEAD_DIM : 2 * span + (h + 1) * HEAD_DIM]
        d = back[:, h * HEAD_DIM : (h + 1) * HEAD_DIM]
        probs_low = probs_ref[h]
        probs = probs_low.astype(wide)
        back_probs = along_last(d, v)
        inner = jnp.sum(back_probs * probs, axis=-1, keepdims=True)
        scores = (probs * (back_probs - inner)).astype(low)
        diagonal = jnp.zeros((1, length), wide)
        for b in range(SHARDS):
            turned = matmul(reverse, scores[b * chunk : (b + 1) * chunk])
            start = (1 - (b + 1) * chunk) % length
            turned = pltpu.roll(turned, start, 1, stride=1, stride_axis=0)
            diagonal = diagonal + jnp.sum(turned, axis=0, keepdims=True)
        diagonals.append(diagonal)
        dq.append((matmul(scores, k) * scale).astype(low))
        dk.append((along_first(scores, q) * scale).astype(low))
        dv.append(along_first(probs_low, d).astype(low))
    dqkv = jnp.concatenate(dq + dk + dv, axis=1)
    back_first = along_last(dqkv, weight_ref[...])
    rows = tokens_ref[...].reshape(length, width).astype(wide)
    rows = rows * lax.rsqrt(jnp.mean(rows * rows, axis=-1, keepdims=True) + epsilon)
    for w in range(SHARDS):
        held[w] = back_first[w * chunk : (w + 1) * chunk].astype(low)
    store_w(backs, held, me)

    gains = [jnp.sum(back_first * rows, axis=0, keepdims=True), gain_two_ref[...]]
    gains = jnp.concatenate(gains + [jnp.zeros((14, width), wide)], axis=0).astype(low)
    i = lax.broadcasted_iota(jnp.int32, (LANES, LANES), 0)
    j = lax.broadcasted_iota(jnp.int32, (LANES, LANES), 1)
    extra = along_first(gains, (i[:16] == j[:16]).astype(low))
    extra = extra + matmul(router_ref[...].astype(low), (i + 2 == j).astype(low))
    above = jnp.zeros((2 + experts, length), wide)
    below = jnp.zeros((LANES - 2 - experts - heads, length), wide)
    spread = jnp.concatenate([above] + diagonals + [below], axis=0)
    shift = lax.broadcasted_iota(jnp.int32, (length, width), 0)
    lane = lax.broadcasted_iota(jnp.int32, (length, width), 1)
    bucket = bucket_of(jnp.where(shift > 0, length - shift, 0))
    hits = (lane == (bucket // table_rows) * shard + bucket % table_rows).astype(low)
    spread_low = spread.astype(low)
    rest = (spread - spread_low.astype(wide)).astype(low)
    turn = (((0,), (1,)), ((), ()))
    extra = extra + lax.dot_general(hits, spread_low, turn, preferred_element_type=wide)
    extra = extra + lax.dot_general(hits, rest, turn, preferred_element_type=wide)
    output = along_first(att_ref[...], up)
    output = jnp.concatenate([output[:, w * shard : (w + 1) * shard] for w in range(SHARDS)], axis=0)
    grads = jnp.concatenate([along_first(first_ref[...], dqkv), extra, output], axis=1)
    if len(parts) == 1:
        parts[0][...] = grads.astype(low)
    else:
        table[...] = grads
        piece = parts[0].shape[1]
        for s, ref in enumerate(parts):
            for w in range(SHARDS):
                start = pl.multiple_of(w * shard + (me_ref[1] ^ s) * piece, 8)
                ref[w] = table[pl.ds(start, piece), :].astype(low)


def join_kernel(me_ref, *refs):
    terms, outs, (output_ref, held) = refs[: -SHARDS - 2], refs[-SHARDS - 2 : -2], refs[-2:]
    total = total_of(terms)
    columns = outs[0].shape[1]
    held[...] = total[:, :, :columns]
    for s in range(SHARDS):
        outs[s][...] = held[me_ref[0] ^ s].astype(low)
    output_ref[...] = jnp.concatenate([total[w][:, columns:] for w in range(SHARDS)], axis=1).astype(low)


def order_kernel(experts, me_ref, *refs):
    parts, output_ref, out_ref, held = refs[:SHARDS], refs[SHARDS], refs[SHARDS + 1], refs[SHARDS + 2]
    for s in range(SHARDS):
        held[me_ref[0] ^ s] = parts[s][...].astype(wide)
    own = HEADS // SHARDS
    span = own * HEAD_DIM
    blocks = [held[w] for w in range(SHARDS)]
    pieces = [blocks[w][:, k * span : (k + 1) * span] for k in range(3) for w in range(SHARDS)]
    lane = lax.broadcasted_iota(jnp.int32, (parts[0].shape[0], LANES), 1)
    extra = jnp.zeros((parts[0].shape[0], LANES), wide)
    for w in range(SHARDS):
        small = blocks[w][:, 3 * span :]
        heads = jnp.where((lane >= 2 + experts) & (lane < 2 + experts + own), small, 0.0)
        extra = extra + jnp.where(lane < 2 + experts, small, 0.0) + pltpu.roll(heads, own * w, 1)
    pieces = pieces + [output_ref[...].astype(wide), extra]
    out_ref[...] = jnp.concatenate(pieces, axis=1).astype(low)


def final_kernel(me_ref, *refs):
    parts, outs = refs[:-9], refs[-9:-1]
    held = refs[-1]
    piece = parts[0].shape[0]
    width = outs[0].shape[1]
    experts = outs[6].shape[0]
    for s, ref in enumerate(parts):
        here = pl.ds(pl.multiple_of((me_ref[1] ^ s) * piece, 8), piece)
        block = ref[...].astype(wide)
        for k in range(4):
            outs[k][here, :] = block[:, k * width : (k + 1) * width]
        held[here, :] = block[:, 4 * width :]
    extra = held[...]
    shard = extra.shape[0]
    i = lax.broadcasted_iota(jnp.int32, (shard, shard), 0)
    j = lax.broadcasted_iota(jnp.int32, (shard, shard), 1)
    turned = along_first(extra.astype(low), (i == j).astype(low))
    outs[4][...] = turned[0]
    outs[5][...] = turned[1]
    outs[6][...] = turned[2 : 2 + experts]
    outs[7][...] = extra[: outs[7].shape[0], 2 + experts : 2 + experts + HEADS]


def tokens_back_kernel(me_ref, tokens_ref, small_ref, resid_ref, *refs):
    terms, out_ref = refs[:-1], refs[-1]
    experts = experts_of(small_ref.shape[0])
    gain = small_ref[experts : experts + 1, :].astype(wide)
    rows = tokens_ref[...].astype(wide)
    r = lax.rsqrt(jnp.mean(rows * rows, axis=-1, keepdims=True) + epsilon)
    m = total_of(terms) * gain
    back = r * m - (r * r * r) * rows * jnp.mean(m * rows, axis=-1, keepdims=True)
    out_ref[...] = resid_ref[...] + back


def local(
    tokens,
    segments,
    routes,
    blocks,
    attention_gain,
    query_weight,
    key_weight,
    value_weight,
    output_weight,
    position_bias,
    feed_gain,
    router_weight,
    expert_in,
    expert_out,
    cotangent,
):
    rows, width = tokens.shape
    length = rows * SHARDS
    experts = lax.axis_size(E)
    me_w = lax.axis_index(W)
    me_e = lax.axis_index(E)
    me = jnp.stack([me_w, me_e, blocks[0] * BLOCK]).astype(jnp.int32)
    shard = query_weight.shape[0]
    own_heads = HEADS // SHARDS
    table_rows = position_bias.shape[0]
    first_local, second_local = expert_in[0], expert_out[0]
    row = (rows, width)
    packed_row = (CAP, width)
    three_rows = [(row, low), (row, low), ((2,) + row, low)]

    quick = experts == 8
    small_rows = -(-(experts + 2 + HEADS) // 16) * 16
    tokens_rel = gather_w(tokens)
    weight_rel = exchange_w(
        call(
            start_kernel,
            [((shard + small_rows, 3 * shard), low)] * SHARDS,
            [((SHARDS, shard, 3 * shard), low)],
            me,
            query_weight,
            key_weight,
            value_weight,
            router_weight.T,
            attention_gain,
            feed_gain,
            position_bias,
            room=FULL,
        )
    )
    (sent,) = call(
        sent_kernel,
        [((rows + 16, width), low)],
        [],
        me,
        cotangent,
        routes.T,
        room=FULL,
    )
    sent = [sent, swap(sent, E, 2), swap(sent, E, 4), swap(sent, E, 6)] if quick else gather_e(sent)

    square = (own_heads, length, length)
    outs = call(
        attend_kernel,
        [
            ((SHARDS, rows, width), low),
            ((length, width), low),
            ((length, 3 * shard), low),
            (square, low),
            ((length, shard), low),
            ((width, 3 * shard), low),
            ((small_rows, width), low),
            ((LANES, width), low),
        ],
        [((SHARDS, shard + small_rows, 3 * shard), low)],
        me,
        *tokens_rel,
        *weight_rel,
        segments,
        cover=20,
    )
    tokens_all, first, qkv, probs, attended, weight, small, router = outs
    *branches, stacked = call(
        branch_kernel,
        three_rows + [((4, rows + 16, width), low)],
        [((SHARDS, rows, width), low)],
        me,
        attended,
        output_weight,
        *sent[:4],
    )
    branch_terms, _ = sum_w(*branches)
    resid, second = call(
        second_kernel,
        [(row, wide), (row, low)],
        [],
        me,
        tokens,
        small,
        *branch_terms,
    )

    second_rel = gather_e(second)

    if quick:
        sent.append(swap(stacked, E, 1))
    dispatch, partner, *upstream_rows = call(
        route_kernel,
        [
            ((CAP, experts * rows), low),
            ((CAP, experts * rows // 2), low),
            ((CAP // 2, width), low),
            ((CAP // 2 + 16, width), low),
        ],
        [],
        me,
        *sent,
        after=(second,),
    )
    upstream_rel = list(zip(gather_w(upstream_rows[0]), gather_w(upstream_rows[1])))
    order = (0, 1, 2, 3)
    outs = call(
        upstream_kernel,
        [(packed_row, wide)] * SHARDS + [((CAP, LANES), wide)] * SHARDS,
        [],
        me,
        second_local,
        *[piece for s in order for piece in upstream_rel[s]],
    )
    back_act, choice = outs[:SHARDS], outs[SHARDS:]

    (packed,) = call(
        pack_kernel,
        [(packed_row, low)],
        [],
        me,
        dispatch,
        *second_rel,
        after=upstream_rel[2],
    )

    def expert_rows(parts, after=()):
        tall = len(parts) * CAP
        *outs, act, pre, logits = call(
            lambda *refs: expert_kernel(len(parts), *refs),
            [(packed_row, low)] * len(parts) + [((tall, width), low), ((tall, width), low), ((tall, LANES), low)],
            [],
            me,
            first_local,
            router,
            *[back_act[s] for s in parts],
            *[choice[s] for s in parts],
            *[rows_rel[s] for s in parts],
            after=after,
        )
        return outs, act, pre, logits

    far = swap(packed, W, 2)
    rows_rel = [packed, swap(packed, W, 1)]
    (own_rows, near_rows), *kept_a = expert_rows((0, 1))
    far = tie(far, own_rows)
    rows_rel = rows_rel + [far, swap(far, W, 1)]
    (across_rows,), *kept_b = expert_rows((2,))
    (last_rows,), *kept_c = expert_rows((3,), after=(kept_b[2],))
    acts, pres, logits = zip(kept_a, kept_b, kept_c)
    near = swap(last_rows, W, 1)
    across = (across_rows.astype(wide) + near.astype(wide)).astype(low)
    *results, router_grad = call(
        result_kernel,
        [(packed_row, low)] * SHARDS + [((width, LANES), wide)],
        [],
        me,
        second_local,
        *acts,
        *logits,
        *rows_rel,
        after=(across,),
    )
    first_grad, second_grad, flag = call(
        grads_kernel,
        [((1,) + first_local.shape, wide), ((1,) + second_local.shape, wide), ((8, LANES), wide)],
        [],
        me,
        *acts,
        *pres,
        *rows_rel,
        *[piece for pieces in upstream_rel for piece in pieces],
        after=(results[0],),
    )
    back_parts = call(
        unpack_kernel,
        [(row, low)] * experts,
        [],
        me,
        dispatch,
        own_rows,
        swap(near_rows, W, 1),
        swap(across, W, 2),
        after=(results[0], flag),
    )
    back_terms = sum_e(back_parts)

    near = swap(results[3], W, 1)
    across = (results[2].astype(wide) + near.astype(wide)).astype(low)
    result_terms = [results[0], swap(results[1], W, 1), swap(across, W, 2)]
    if quick:
        (mixed,) = call(total_kernel, [(packed_row, low)], [], me, *result_terms)
        mixed_parts = call(
            unpack_both_kernel, [(row, low)] * 4, [], me, dispatch, partner, mixed, swap(mixed, E, 1)
        )
        mixed_terms = [mixed_parts[0]] + [swap(mixed_parts[s // 2], E, s) for s in (4, 6, 2)]
    else:
        mixed_parts = call(unpack_kernel, [(row, low)] * experts, [], me, dispatch, *result_terms)
        mixed_terms = sum_e(mixed_parts)

    back_resid, back_branch, gain_two_grad = call(
        resid_back_kernel,
        [(row, wide), (row, low), ((1, width), wide)],
        [],
        me,
        resid,
        small,
        cotangent,
        *back_terms,
        after=(mixed_parts[0],),
    )
    back_rel = exchange_w([back_branch] * SHARDS)
    columns = 3 * shard + LANES
    piece = shard // experts
    part = (SHARDS, piece, columns + shard)
    outs = call(
        lambda *refs: attend_back_kernel(experts, table_rows, *refs),
        three_rows
        + ([(part, low)] * experts if quick else [((width, columns + shard), low)]),
        [((SHARDS, rows, width), low), ((width, columns + shard), wide)],
        me,
        output_weight,
        qkv,
        probs,
        weight,
        tokens_all,
        first,
        attended,
        gain_two_grad,
        router_grad,
        *back_rel,
        cover=20,
    )
    grads = list(outs[3:])
    (layer_out,) = call(layer_kernel, [(row, low)], [], me, resid, *mixed_terms, after=(grads[-1],))
    if quick:
        grads[3] = tie(grads[3], *mixed_terms[1:])
    back_terms, _ = sum_w(*outs[:3])
    (tokens_grad,) = call(
        tokens_back_kernel,
        [(row, wide)],
        [],
        me,
        tokens,
        small,
        back_resid,
        *back_terms,
    )

    if quick:
        terms = sum_e(grads, early=True)
        *grads, output_grad = call(
            join_kernel,
            [((piece, columns), low)] * SHARDS + [((piece, width), low)],
            [((SHARDS, piece, columns), wide)],
            me,
            *terms,
        )
        (grads,) = call(
            lambda *refs: order_kernel(experts, *refs),
            [((piece, 4 * width + LANES), low)],
            [((SHARDS, piece, columns), wide)],
            me,
            *exchange_w(grads),
            output_grad,
        )
        shape = (shard, width)
        outs = call(
            final_kernel,
            [(shape, wide)] * 4
            + [((shard,), wide)] * 2
            + [((experts, shard), wide), ((table_rows, HEADS), wide)],
            [((shard, LANES), wide)],
            me,
            *gather_e(grads),
        )
        query_grad, key_grad, value_grad, output_grad = outs[:4]
        gain_one_grad, gain_two_grad = outs[4], outs[5]
        router_grad, table_grad = outs[6].T, outs[7]
    else:
        grads = lax.psum(grads[0], E).astype(wide).reshape(SHARDS, shard, columns + shard)
        output_grad = grads[:, :, columns:].transpose(1, 0, 2).reshape(shard, width)
        grads = grads[:, :, :columns].astype(low)
        grads = place(
            exchange_w([lax.dynamic_index_in_dim(grads, me_w ^ s, 0, False) for s in range(SHARDS)]), me_w
        ).astype(wide)
        main = grads[:, :, : 3 * shard].reshape(SHARDS, shard, 3, shard).transpose(2, 1, 0, 3)
        query_grad, key_grad, value_grad = main.reshape(3, shard, width)
        extra = grads[:, :, 3 * shard :]
        summed = jnp.sum(extra[:, :, : 2 + experts], axis=0)
        gain_one_grad, gain_two_grad, router_grad = summed[:, 0], summed[:, 1], summed[:, 2:]
        table_grad = extra[:, :table_rows, 2 + experts : 2 + experts + own_heads]
        table_grad = table_grad.transpose(1, 0, 2).reshape(table_rows, HEADS)
    return (
        layer_out,
        tokens_grad,
        gain_one_grad,
        query_grad,
        key_grad,
        value_grad,
        output_grad,
        table_grad,
        gain_two_grad,
        router_grad,
        first_grad,
        second_grad,
    )


def solution(mesh):
    in_specs = (
        P(("expert", "wshard"), None),
        P("expert", None),
        P(("expert", "wshard"), None),
        P("expert"),
        P("wshard"),
        P("wshard", None),
        P("wshard", None),
        P("wshard", None),
        P("wshard", None),
        P("wshard", None),
        P("wshard"),
        P("wshard", None),
        P("expert", "wshard", None),
        P("expert", "wshard", None),
        P(("expert", "wshard"), None),
    )
    out_specs = (
        P(("expert", "wshard"), None),
        P(("expert", "wshard"), None),
        P("wshard"),
        P("wshard", None),
        P("wshard", None),
        P("wshard", None),
        P("wshard", None),
        P("wshard", None),
        P("wshard"),
        P("wshard", None),
        P("expert", "wshard", None),
        P("expert", "wshard", None),
    )
    return jax.shard_map(local, mesh=mesh, in_specs=in_specs, out_specs=out_specs, check_vma=False)
```
